32 devices in a mesh: dp: 8 (over y, x, core), mp: 4 (over z).
Axes of the slice: x: 2, y: 2, z: 4, core: 2. Of those that a mesh axis runs over, the one named last changes fastest.
Arguments:
- tokens: bfloat16 [256, 40, 768], P(('dp', 'mp')), may hold values from -6 to 6
- images: bfloat16 [256, 145, 1024], P(('dp', 'mp')), may hold values from -6 to 6
- segment_of_token: int32 [256, 40], P('dp'), may hold values from 0 to 3, never falling along the last dimension, each value on 1 to 20 neighbouring positions
- image_of_row: int32 [256], P('dp'), may hold values from 0 to 255, as said below
- attention_in: bfloat16 [3, 3, 768, 768], P(None, None, None, 'mp'), may hold values from -0.21875 to 0.21875
- query_value_bias: bfloat16 [3, 2, 768], P(None, None, 'mp'), may hold values from -3 to 3
- attention_out: bfloat16 [3, 768, 768], P(None, 'mp'), may hold values from -0.625 to 0.625
- output_bias: bfloat16 [5, 768], replicated, may hold values from -2 to 2
- feed_in: bfloat16 [2, 768, 3072], P(None, None, 'mp'), may hold values from -0.21875 to 0.21875
- feed_bias: bfloat16 [2, 3072], P(None, 'mp'), may hold values from -3 to 3
- feed_out: bfloat16 [2, 3072, 768], P(None, 'mp'), may hold values from -0.109375 to 0.109375
- image_weight: bfloat16 [1024, 768], P(None, 'mp'), may hold values from -0.1875 to 0.1875
- image_bias: bfloat16 [768], P('mp'), may hold values from -2 to 2
- norm_gain: bfloat16 [5, 768], replicated, may hold values from 0.5 to 1.5
- norm_bias: bfloat16 [5, 768], replicated, may hold values from -2 to 2
- cotangent: bfloat16 [256, 40, 768], P(('dp', 'mp')), may hold values from -6 to 6
Outputs:
- mixed_out: float32 [256, 40, 768], P(('dp', 'mp'))
- grad_tokens: float32 [256, 40, 768], P(('dp', 'mp'))
- grad_images: float32 [256, 145, 1024], P(('dp', 'mp'))
- grad_attention_in: float32 [3, 3, 768, 768], P(None, None, None, 'mp')
- grad_query_value_bias: float32 [3, 2, 768], P(None, None, 'mp')
- grad_attention_out: float32 [3, 768, 768], P(None, 'mp')
- grad_output_bias: float32 [5, 768], replicated
- grad_feed_in: float32 [2, 768, 3072], P(None, None, 'mp')
- grad_feed_bias: float32 [2, 3072], P(None, 'mp')
- grad_feed_out: float32 [2, 3072, 768], P(None, 'mp')
- grad_image_weight: float32 [1024, 768], P(None, 'mp')
- grad_image_bias: float32 [768], P('mp')
- grad_norm_gain: float32 [5, 768], replicated
- grad_norm_bias: float32 [5, 768], replicated
The draws below stay inside these ranges and needn't reach their ends.
Inputs may be any that keep to these rules, and one draw needn't show every extreme that they name: `image_of_row`: within each aligned block of 32 rows the entries are a permutation of that block's row numbers: each row uses one image of its own block. `segment_of_token`: along a row the numbers never fall; a token attends to the tokens of its row with the same number.
All inputs are finite; a program needn't handle non-finite values.
Results may differ from the reference program's by a relative error of at most 0.03.
Values may be sent and summed in bfloat16 or wider, within the bound.
No kernel may reach another device: no remote copies, remote signals or barrier semaphores. Data moves between devices by JAX's collectives and lax.ppermute only.
A program may use at most 256 MiB of HBM per device.

```python
import math
import jax
import jax.numpy as jnp
import numpy as np
from jax import lax

D = 768
FF = 3072
IMAGE_WIDTH = 1024
PATCHES = 145
SEQ = 40
HEAD_DIM = 64
GROUP_ROWS = 32
ROWS = 256


def draw_image_of_row(key, part):
    key = jax.random.fold_in(key, 7)
    blocks = ROWS // GROUP_ROWS
    block_keys = jax.random.split(key, blocks)
    orders = jax.vmap(lambda single: jax.random.permutation(single, GROUP_ROWS))(block_keys)
    starts = jnp.arange(blocks, dtype=jnp.int32)[:, None] * GROUP_ROWS
    return (orders.astype(jnp.int32) + starts).reshape(ROWS)


def block_scale(stream_key, shape, shards, low, largest):
    gain = 1.0
    for dim, blocks in shards:
        heights = jax.random.uniform(jax.random.fold_in(jax.random.fold_in(stream_key, 6), dim), (blocks,), jnp.float32, low / len(shards), largest / len(shards))
        gain = gain * jnp.repeat(jnp.exp(heights), shape[dim] // blocks).reshape((-1,) + (1,) * (len(shape) - 1 - dim))
    return gain


def profile(number_of, total, most, lean):
    loads = [(1 << 20) // math.isqrt(rank ** lean) + 1 for rank in range(2, number_of + 1)]
    rest, given = total - most - (number_of - 1), [1] * (number_of - 1)
    while rest > 0:
        candidates = [i for i in range(number_of - 1) if given[i] < most]
        whole, budget = sum([loads[i] for i in candidates]), rest
        for i in candidates:
            extra = min(most - given[i], max(1, budget * loads[i] // whole), rest)
            given[i] = given[i] + extra
            rest = rest - extra
    return np.array([most] + given)


def uneven(own_key, amount, total, limit, skew):
    if amount == 2:
        one = jax.random.randint(own_key, (), max(1, total - limit), min(limit, total - 1) + 1)
        return jnp.stack([one, total - one])
    tallies = jnp.asarray(profile(amount, total, limit, skew), jnp.int32)
    twos = (amount - 1) // 2
    donor, sink = tallies[1:1 + 2 * twos:2], tallies[2:2 + 2 * twos:2]
    slack = jnp.minimum(donor - 1, limit - sink)
    moved = jax.random.randint(jax.random.fold_in(own_key, 1), (twos,), 0, 1 << 20) % (slack + 1)
    tallies = tallies.at[1:1 + 2 * twos:2].set(donor - moved).at[2:2 + 2 * twos:2].set(sink + moved)
    return tallies[jax.random.permutation(jax.random.fold_in(own_key, 2), amount)]


def scatter_about(rng, dims, scale, most, cuts=(), kind=jnp.bfloat16):
    values = jax.random.normal(rng, dims, jnp.float32) * scale
    if len(cuts) > 0:
        values = block_scale(rng, dims, cuts, -0.22, 0.18) * values
    return jnp.clip(values, min=-most, max=most).astype(kind)


def setup_inputs(seed: int = 0) -> dict:
    seeds = jax.random.split(jax.random.key(seed), 17)
    return {
        "tokens": scatter_about(seeds[0], (ROWS, SEQ, D), 1.0, 6.0, ((0, 32),)),
        "images": scatter_about(seeds[1], (ROWS, PATCHES, IMAGE_WIDTH), 1.0, 6.0, ((0, 32),)),
        "segment_of_token": jax.vmap(lambda own: jnp.searchsorted(jnp.cumsum(uneven(own, 4, SEQ, SEQ // 2, 0)), jnp.arange(SEQ), side="right"))(jax.random.split(seeds[2], ROWS)).reshape((ROWS, SEQ)).astype(jnp.int32),
        "image_of_row": draw_image_of_row(jax.random.fold_in(seeds[16], 71), 0),
        "attention_in": scatter_about(seeds[4], (3, 3, D, D), D ** -0.5, 0.21875, ((3, 4),)),
        "query_value_bias": scatter_about(seeds[5], (3, 2, D), 0.5, 3.0, ((2, 4),)),
        "attention_out": scatter_about(seeds[6], (3, D, D), (D // 8) ** -0.5, 0.625, ((1, 4),)),
        "output_bias": scatter_about(seeds[7], (5, D), 0.3, 2.0),
        "feed_in": scatter_about(seeds[8], (2, D, FF), D ** -0.5, 0.21875, ((2, 4),)),
        "feed_bias": scatter_about(seeds[9], (2, FF), 0.5, 3.0, ((1, 4),)),
        "feed_out": scatter_about(seeds[10], (2, FF, D), FF ** -0.5, 0.109375, ((1, 4),)),
        "image_weight": scatter_about(seeds[11], (IMAGE_WIDTH, D), IMAGE_WIDTH ** -0.5, 0.1875, ((1, 4),)),
        "image_bias": scatter_about(seeds[12], (D,), 0.3, 2.0, ((0, 4),)),
        "norm_gain": jnp.clip(1.0 + 0.1 * jax.random.normal(seeds[13], (5, D), jnp.float32), 0.5, 1.5).astype(jnp.bfloat16),
        "norm_bias": scatter_about(seeds[14], (5, D), 0.3, 2.0),
        "cotangent": scatter_about(seeds[15], (ROWS, SEQ, D), 1.0, 6.0, ((0, 32),)),
    }


@jax.custom_vjp
def low(v):
    return lax.optimization_barrier(v.astype(jnp.bfloat16)).astype(jnp.float32)

@jax.custom_vjp
def low_back(v):
    return v

def low_keep(v):
    return (low(v), None)

def low_pass(kept, grad):
    return (grad,)

def back_keep(v):
    return (v, None)

def back_low(kept, grad):
    return (low(grad),)
low.defvjp(low_keep, low_pass)
low_back.defvjp(back_keep, back_low)
highest = lax.Precision.HIGHEST
epsilon = 1e-06
blocked = -1000000000.0

def rounded(values):
    return low_back(low(values))

def matmul(values, weight):
    return jnp.einsum('...k,kn->...n', values, weight, precision=highest)

def norm_rows(values, gain_row, shift_row):
    center = values - lax.optimization_barrier(jnp.mean(values, axis=-1, keepdims=True))
    moment = lax.optimization_barrier(jnp.mean(center * center, axis=-1, keepdims=True))
    return center * lax.rsqrt(moment + epsilon) * gain_row + shift_row

def split_heads(values):
    return values.reshape(values.shape[:-1] + (values.shape[-1] // HEAD_DIM, HEAD_DIM))

def attend(query_rows, key_rows, value_rows, allowed):
    scores = jnp.einsum('rqhe,rkhe->rhqk', split_heads(query_rows), split_heads(key_rows), precision=highest) * HEAD_DIM ** (-0.5)
    if allowed is not None:
        scores = jnp.where(allowed[:, None], scores, blocked)
    weights = low(jax.nn.softmax(low_back(scores), axis=-1))
    context = jnp.einsum('rhqk,rkhe->rqhe', weights, split_heads(value_rows), precision=highest)
    return rounded(context.reshape(query_rows.shape))

def attention_block(stream, source, weight_in, bias_pair, weight_out, bias_out, gain_row, shift_row, allowed):
    stream_low = low(stream)
    source_rows = stream_low if source is None else source
    query_rows = rounded(matmul(stream_low, weight_in[0]) + bias_pair[0])
    key_rows = rounded(matmul(source_rows, weight_in[1]))
    value_rows = rounded(matmul(source_rows, weight_in[2]) + bias_pair[1])
    context = attend(query_rows, key_rows, value_rows, allowed)
    branch = low_back(matmul(context, weight_out))
    return norm_rows(branch + bias_out + stream, gain_row, shift_row)

def feed_block(stream, weight_in, bias_in, weight_out, bias_out, gain_row, shift_row):
    stream_low = low(stream)
    inner_rows = low_back(matmul(stream_low, weight_in) + bias_in)
    active = low(jax.nn.gelu(inner_rows, approximate=False))
    branch = low_back(matmul(active, weight_out))
    return norm_rows(branch + bias_out + stream, gain_row, shift_row)

def forward(params, token_rows, image_rows, segment_rows, local_order):
    attention_in, query_value_bias, attention_out, output_bias, feed_in, feed_bias, feed_out, image_weight, image_bias, norm_gain, norm_bias = params
    allowed = segment_rows[:, :, None] == segment_rows[:, None, :]
    stream = attention_block(token_rows, None, attention_in[0], query_value_bias[0], attention_out[0], output_bias[0], norm_gain[0], norm_bias[0], allowed)
    stream = feed_block(stream, feed_in[0], feed_bias[0], feed_out[0], output_bias[1], norm_gain[1], norm_bias[1])
    stream = attention_block(stream, None, attention_in[1], query_value_bias[1], attention_out[1], output_bias[2], norm_gain[2], norm_bias[2], allowed)
    projected = rounded(matmul(image_rows, image_weight) + image_bias)
    picked = jnp.take(projected, local_order, axis=0)
    stream = attention_block(stream, picked, attention_in[2], query_value_bias[2], attention_out[2], output_bias[3], norm_gain[3], norm_bias[3], None)
    return feed_block(stream, feed_in[1], feed_bias[1], feed_out[1], output_bias[4], norm_gain[4], norm_bias[4])

def reference(tokens, images, segment_of_token, image_of_row, attention_in, query_value_bias, attention_out, output_bias, feed_in, feed_bias, feed_out, image_weight, image_bias, norm_gain, norm_bias, cotangent):
    params = tuple((weight.astype(jnp.float32) for weight in (attention_in, query_value_bias, attention_out, output_bias, feed_in, feed_bias, feed_out, image_weight, image_bias, norm_gain, norm_bias)))
    groups = ROWS // GROUP_ROWS

    def blocks_of(values):
        return values.reshape((groups, GROUP_ROWS) + values.shape[1:])
    pieces = (blocks_of(tokens.astype(jnp.float32)), blocks_of(images.astype(jnp.float32)), blocks_of(segment_of_token), blocks_of(image_of_row), blocks_of(cotangent.astype(jnp.float32)))

    def scan_step(totals, block_piece):
        token_rows, image_rows, segment_rows, order_rows, grad_rows = block_piece
        local_order = (order_rows % GROUP_ROWS).astype(jnp.int32)

        def run_block(weights, token_in, image_in):
            return forward(weights, token_in, image_in, segment_rows, local_order)
        result, pullback = jax.vjp(run_block, params, token_rows, image_rows)
        grad_weights, grad_token, grad_image = pullback(grad_rows)
        totals = jax.tree.map(jnp.add, totals, grad_weights)
        return (totals, (result, grad_token, grad_image))
    zero_totals = tuple((jnp.zeros_like(weight) for weight in params))
    totals, outputs = lax.scan(scan_step, zero_totals, pieces)
    mixed_out = outputs[0].reshape((ROWS, SEQ, D))
    grad_tokens = outputs[1].reshape((ROWS, SEQ, D))
    grad_images = outputs[2].reshape((ROWS, PATCHES, IMAGE_WIDTH))
    return (mixed_out, grad_tokens, grad_images, totals[0], totals[1], totals[2], totals[3], totals[4], totals[5], totals[6], totals[7], totals[8], totals[9], totals[10])
```

```python
from functools import partial

import jax
import jax.numpy as jnp
from jax import lax
from jax.experimental import pallas as pl
from jax.experimental.pallas import tpu as pltpu
from jax.sharding import PartitionSpec as P

HEAD_DIM = 64
PAIR = 2 * HEAD_DIM
SLICES = 8
EPSILON = 1e-06
BLOCKED = -1000000000.0
SCALE = HEAD_DIM ** (-0.5)
DISTANCES = ((0, 2, 4, 6), (0, 4, 2, 6))
F32 = jnp.float32
BF16 = jnp.bfloat16

ANY = pl.BlockSpec(memory_space=pl.ANY)
VMEM = pl.BlockSpec(memory_space=pltpu.VMEM)
SMEM = pl.BlockSpec(memory_space=pltpu.SMEM)


def swap(values, bit):
    count = lax.axis_size("dp")
    return lax.ppermute(values, "dp", [(i, i ^ bit) for i in range(count)])


def pass_on(values):
    count = lax.axis_size("mp")
    return lax.ppermute(values, "mp", [(i, (i + 1) % count) for i in range(count)])


def add(left, right):
    return (left.astype(F32) + right.astype(F32)).astype(BF16)


def ring(values):
    parts = [values]
    for _ in range(lax.axis_size("mp") - 1):
        parts.append(pass_on(parts[-1]))
    return parts


def widen(first, second):
    first = jnp.stack([first, swap(first, 2)])
    second = jnp.stack([second, swap(second, 4)])
    both = jnp.stack(
        [
            jnp.concatenate([first, swap(first, 4)]),
            jnp.concatenate([second, swap(second, 2)]),
        ]
    )
    return both, swap(both, 1)


def gather_weights(own):
    others = jnp.stack(ring(own)[1:], axis=1)
    return widen(others[0], others[1])


def reduce_grads(both):
    mp = lax.axis_size("mp")
    first = add(both[0, :2], swap(both[0, 2:], 4))
    second = add(both[1, :2], swap(both[1, 2:], 2))
    total = jnp.stack([add(first[0], swap(first[1], 2)), add(second[0], swap(second[1], 4))], axis=1)
    own = total[1]
    for step in range(1, mp):
        own = add(pass_on(own), total[(step + 1) % mp])
    bit = SLICES
    while bit < lax.axis_size("dp"):
        own = add(own, swap(own, bit))
        bit *= 2
    return widen(own[0], own[1])


def total_everywhere(values):
    bit = 1
    while bit < lax.axis_size("dp"):
        values = values + swap(values, bit)
        bit *= 2
    count = lax.axis_size("mp")
    bit = 1
    while bit < count:
        values = values + lax.ppermute(values, "mp", [(i, i ^ bit) for i in range(count)])
        bit *= 2
    return values


def dot_nn(left, right):
    return lax.dot_general(left, right, (((1,), (0,)), ((), ())), preferred_element_type=F32)


def dot_nt(left, right):
    return lax.dot_general(left, right, (((1,), (1,)), ((), ())), preferred_element_type=F32)


def dot_tn(left, right):
    return lax.dot_general(left, right, (((0,), (0,)), ((), ())), preferred_element_type=F32)


def start(source, target, sem):
    pltpu.make_async_copy(source, target, sem).start()


def finish(whole, sem):
    pltpu.make_async_copy(whole, whole, sem).wait()


def aligned(first, count, step=16):
    return pl.ds(pl.multiple_of(first, step), count)


def each_slice(place, first_step, mp):
    for core in range(2):
        for half in range(2):
            for entry in range(4):
                slot = place[0] ^ (core ^ DISTANCES[half][entry])
                for step in range(first_step, mp):
                    yield core, half, entry, step, slot, (place[1] + mp - step) % mp


def attention_spot(whole, quarter, half, slot, owner):
    span = 4 * quarter // SLICES
    count = quarter // span
    row = owner * quarter + (slot % count) * span + half * (span // 2)
    return whole.at[slot // count, aligned(row, span // 2)]


def load_attention(place, own, pieces, offset, whole, sem):
    mp = pieces[0].shape[2] + 1
    quarter = whole.shape[1] // mp
    rows = quarter // 4
    for mat in range(4):
        start(
            own.at[pl.ds(mat * quarter, quarter)],
            whole.at[mat, aligned(place[1] * quarter, quarter)],
            sem,
        )
    for core, half, entry, step, slot, owner in each_slice(place, 1, mp):
        start(
            pieces[core].at[half, entry, step - 1, pl.ds(offset, rows)],
            attention_spot(whole, quarter, half, slot, owner),
            sem,
        )


def store_attention(place, whole, outs, sem):
    mp = outs[0].shape[2]
    quarter = whole.shape[1] // mp
    for core, half, entry, step, slot, owner in each_slice(place, 0, mp):
        start(
            attention_spot(whole, quarter, half, slot, owner),
            outs[core].at[half, entry, step],
            sem,
        )


def feed_spot(whole, quarter, half, slot, owner):
    span = quarter // SLICES
    return whole.at[half, aligned(owner * quarter + slot * span, span)]


def load_feed(place, own, pieces, offset, whole, sem):
    mp = pieces[0].shape[2] + 1
    quarter = whole.shape[1] // mp
    rows = quarter // SLICES
    for half in range(2):
        start(
            own.at[pl.ds(half * quarter, quarter)],
            whole.at[half, aligned(place[1] * quarter, quarter)],
            sem,
        )
    for core, half, entry, step, slot, owner in each_slice(place, 1, mp):
        start(
            pieces[core].at[half, entry, step - 1, pl.ds(offset, rows)],
            feed_spot(whole, quarter, half, slot, owner),
            sem,
        )


def store_feed(place, whole, outs, sem):
    mp = outs[0].shape[2]
    quarter = whole.shape[1] // mp
    for core, half, entry, step, slot, owner in each_slice(place, 0, mp):
        start(
            feed_spot(whole, quarter, half, slot, owner),
            outs[core].at[half, entry, step],
            sem,
        )


def image_copies(whole, piece, quarter, half, slot, owner, sem, inward):
    rows, width = piece.shape
    span = 2 * rows
    beyond = whole.shape[1] - width
    blocks = width // beyond
    plain = quarter // span
    base = owner * quarter + half * rows

    def move(inner, outer):
        start(inner, outer, sem) if inward else start(outer, inner, sem)

    @pl.when(slot < plain)
    def _():
        move(piece, whole.at[aligned(base + slot * span, rows), pl.ds(0, width)])

    @pl.when(slot >= plain)
    def _():
        for block in range(blocks):
            row = base + block * (quarter // blocks) + (slot - plain) * span
            move(
                piece.at[:, pl.ds(block * beyond, beyond)],
                whole.at[aligned(row, rows), pl.ds(width, beyond)],
            )


def load_image(place, own, pieces, offset, rows, whole, sem):
    mp = pieces[0].shape[2] + 1
    quarter = whole.shape[0] // mp
    start(own, whole.at[aligned(place[1] * quarter, quarter)], sem)
    for core, half, entry, step, slot, owner in each_slice(place, 1, mp):
        piece = pieces[core].at[half, entry, step - 1, pl.ds(offset, rows)]
        image_copies(whole, piece, quarter, half, slot, owner, sem, True)


def store_image(place, whole, outs, sem):
    mp = outs[0].shape[2]
    quarter = whole.shape[0] // mp
    for core, half, entry, step, slot, owner in each_slice(place, 0, mp):
        piece = outs[core].at[half, entry, step]
        image_copies(whole, piece, quarter, half, slot, owner, sem, False)


def norm_rows(values, gain_row, shift_row):
    center = values - jnp.mean(values, axis=-1, keepdims=True)
    moment = jnp.mean(center * center, axis=-1, keepdims=True)
    return center * lax.rsqrt(moment + EPSILON) * gain_row + shift_row


def norm_back(pre_norm, gain_row, grad_out, small):
    center = pre_norm - jnp.mean(pre_norm, axis=-1, keepdims=True)
    scale = lax.rsqrt(jnp.mean(center * center, axis=-1, keepdims=True) + EPSILON)
    normal = center * scale
    lifted = grad_out * gain_row
    grad_pre = scale * (
        lifted
        - jnp.mean(lifted, axis=-1, keepdims=True)
        - normal * jnp.mean(lifted * normal, axis=-1, keepdims=True)
    )
    small[...] = jnp.zeros_like(small)
    small[0:1] = jnp.sum(grad_out * normal, axis=0, keepdims=True)
    small[1:2] = jnp.sum(grad_out, axis=0, keepdims=True)
    small[2:3] = jnp.sum(grad_pre, axis=0, keepdims=True)
    return grad_pre


def column_total(values):
    return jnp.sum(values.astype(F32), axis=0, keepdims=True)


def head_masks(kind):
    lane = lax.broadcasted_iota(jnp.int32, (1, PAIR), 1)
    return (lane < HEAD_DIM).astype(F32).astype(kind), (lane >= HEAD_DIM).astype(F32).astype(kind)


def both_heads(values):
    left, right = head_masks(values.dtype)
    return jnp.concatenate([values * left, values * right], axis=0)


def one_of_heads(values):
    lane = lax.broadcasted_iota(jnp.int32, (1, PAIR), 1)
    rows = values.shape[0] // 2
    return jnp.where(lane < HEAD_DIM, values[:rows], values[rows:])


def softmax(scores):
    raised = jnp.exp(scores - jnp.max(scores, axis=-1, keepdims=True))
    return raised * (1.0 / jnp.sum(raised, axis=-1, keepdims=True))


def self_weights(query, keys, code_col, code_row):
    allowed = jnp.concatenate([code_col, code_col], axis=0) == code_row
    return softmax(jnp.where(allowed, dot_nt(query, keys) * SCALE, BLOCKED))


def cross_weights(query, keys, patches):
    column = lax.broadcasted_iota(jnp.int32, (1, keys.shape[0]), 1)
    return softmax(jnp.where(column < patches, dot_nt(query, keys) * SCALE, BLOCKED))


def score_back(weights, grad_weights):
    along = weights * grad_weights
    return (along - weights * jnp.sum(along, axis=-1, keepdims=True)).astype(BF16)


def gather_rows(picks, rows_ref, target):
    seq = rows_ref.shape[1]
    for row in range(target.shape[0] // seq):
        target[row * seq : (row + 1) * seq] = rows_ref[picks[row]].astype(target.dtype)


def leave_rows(values, target):
    seq = target.shape[1]
    for row in range(target.shape[0]):
        target[row] = values[row * seq : (row + 1) * seq].astype(target.dtype)


def self_forward_kernel(
    pick, offset, place, picks, rows_ref, own, piece0, piece1, bias, params, code_col, code_row,
    out, low, pre, query, keys, value, context, whole, sem, *held,
):
    load_attention(place, own, (piece0, piece1), offset, whole, sem)
    if pick:
        gather_rows(picks, rows_ref, held[0])
        stream = held[0][...]
    else:
        stream = rows_ref[...]
    hb = stream.astype(BF16)
    low[...] = hb
    finish(whole, sem)
    query[...] = (dot_nt(hb, whole[0]) + bias[0:1]).astype(BF16)
    keys[...] = dot_nt(hb, whole[1]).astype(BF16)
    value[...] = (dot_nt(hb, whole[2]) + bias[1:2]).astype(BF16)
    groups, size = code_row.shape
    for group in range(groups):
        rows = slice(group * size, (group + 1) * size)
        for first in range(0, hb.shape[1], PAIR):
            lanes = slice(first, first + PAIR)
            weights = self_weights(
                both_heads(query[rows, lanes]), keys[rows, lanes], code_col[rows], code_row[group : group + 1]
            )
            mixed = one_of_heads(dot_nn(weights.astype(BF16), value[rows, lanes]))
            context[rows, lanes] = mixed.astype(BF16)
    total = dot_nn(context[...], whole[3]) + params[0:1] + stream
    pre[...] = total
    out[...] = norm_rows(total, params[1:2], params[2:3])


def self_backward_kernel(
    leave, offset, place, grad, low, pre, query, keys, value, context, own, piece0, piece1, params, code_col, code_row,
    out, small, keep, send, whole, grads, grad_context, grad_query, grad_keys, grad_value, sem, out_sem,
):
    load_attention(place, own, (piece0, piece1), offset, whole, sem)
    grad_pre = norm_back(pre[...], params[1:2], grad[...], small)
    branch = grad_pre.astype(BF16)
    finish(whole, sem)
    grad_context[...] = dot_nt(branch, whole[3]).astype(BF16)
    grads[3] = dot_tn(context[...], branch).astype(BF16)
    groups, size = code_row.shape
    for group in range(groups):
        rows = slice(group * size, (group + 1) * size)
        for first in range(0, branch.shape[1], PAIR):
            lanes = slice(first, first + PAIR)
            query_pair, context_pair = both_heads(query[rows, lanes]), both_heads(grad_context[rows, lanes])
            weights = self_weights(query_pair, keys[rows, lanes], code_col[rows], code_row[group : group + 1])
            grad_scores = score_back(weights, dot_nt(context_pair, value[rows, lanes]))
            mixed = one_of_heads(dot_nn(grad_scores, keys[rows, lanes])) * SCALE
            grad_query[rows, lanes] = mixed.astype(BF16)
            grad_keys[rows, lanes] = (dot_tn(grad_scores, query_pair) * SCALE).astype(BF16)
            grad_value[rows, lanes] = dot_tn(weights.astype(BF16), context_pair).astype(BF16)
    hb = low[...]
    grads[0] = dot_tn(grad_query[...], hb).astype(BF16)
    grads[1] = dot_tn(grad_keys[...], hb).astype(BF16)
    grads[2] = dot_tn(grad_value[...], hb).astype(BF16)
    store_attention(place, grads, (keep, send), out_sem)
    small[3:4] = column_total(grad_query[...])
    small[4:5] = column_total(grad_value[...])
    total = grad_pre + dot_nn(grad_query[...], whole[0])
    total = total + dot_nn(grad_keys[...], whole[1])
    total = total + dot_nn(grad_value[...], whole[2])
    if leave:
        leave_rows(total, out)
    else:
        out[...] = total
    finish(grads, out_sem)


def gelu_parts(inner):
    spread = 0.5 * (1.0 + lax.erf(inner * (2.0 ** -0.5)))
    return spread


def feed_forward_kernel(
    leave, offset, place, rows_ref, own, piece0, piece1, bias, params,
    out, low, pre, inner, active, whole, sem,
):
    load_feed(place, own, (piece0, piece1), offset, whole, sem)
    stream = rows_ref[...]
    hb = stream.astype(BF16)
    low[...] = hb
    finish(whole, sem)
    size = whole.shape[2]
    total = params[0:1] + stream
    for first in range(0, whole.shape[1], size):
        part = slice(first, first + size)
        units = dot_nt(hb, whole[0, part]) + bias[first // size : first // size + 1]
        inner[:, part] = units
        gated = (units * gelu_parts(units)).astype(BF16)
        active[:, part] = gated
        total = total + dot_nn(gated, whole[1, part])
    pre[...] = total
    result = norm_rows(total, params[1:2], params[2:3])
    if leave:
        leave_rows(result, out)
    else:
        out[...] = result


def feed_backward_kernel(
    pick, offset, place, picks, grad, low, pre, inner, active, own, piece0, piece1, params,
    out, small, keep, send, whole, grads, sem, out_sem, *held,
):
    load_feed(place, own, (piece0, piece1), offset, whole, sem)
    if pick:
        gather_rows(picks, grad, held[0])
        grad = held[0]
    grad_pre = norm_back(pre[...], params[1:2], grad[...], small)
    branch = grad_pre.astype(BF16)
    finish(whole, sem)
    size = whole.shape[2]
    hb = low[...]
    total = grad_pre
    for first in range(0, whole.shape[1], size):
        part = slice(first, first + size)
        grads[1, part] = dot_tn(active[:, part], branch).astype(BF16)
        units = inner[:, part]
        slope = gelu_parts(units) + units * jnp.exp(-0.5 * units * units) * 0.3989422804014327
        grad_units = (dot_nt(branch, whole[1, part]) * slope).astype(BF16)
        grads[0, part] = dot_tn(grad_units, hb).astype(BF16)
        row = 3 + first // size
        small[row : row + 1] = column_total(grad_units)
        total = total + dot_nn(grad_units, whole[0, part])
    store_feed(place, grads, (keep, send), out_sem)
    out[...] = total
    finish(grads, out_sem)


def image_forward_kernel(
    offset, image_offset, image_rows, place, images, own, own_image, piece0, piece1, bias, image_bias,
    projected, keys, value, whole, whole_image, sem, image_sem,
):
    load_image(place, own_image, (piece0, piece1), image_offset, image_rows, whole_image, image_sem)
    load_attention(place, own, (piece0, piece1), offset, whole, sem)
    finish(whole_image, image_sem)
    finish(whole, sem)
    size = images.shape[0] // 4
    for first in range(0, images.shape[0], size):
        rows = slice(first, first + size)
        source = (dot_nt(images[rows], whole_image[...]) + image_bias[...]).astype(BF16)
        projected[rows] = source
        keys[rows] = dot_nt(source, whole[1]).astype(BF16)
        value[rows] = (dot_nt(source, whole[2]) + bias[1:2]).astype(BF16)


def cross_forward_kernel(
    offset, seq, patches, place, rows_ref, keys, value, own, piece0, piece1, bias, params,
    out, low, pre, query, context, whole, mixed, sem,
):
    load_attention(place, own, (piece0, piece1), offset, whole, sem)
    stream = rows_ref[...]
    hb = stream.astype(BF16)
    low[...] = hb
    finish(whole, sem)
    query[...] = (dot_nt(hb, whole[0]) + bias[0:1]).astype(BF16).astype(F32)
    count = stream.shape[0] // seq
    size = keys.shape[0] // count
    for row in range(count):
        rows, places = slice(row * seq, (row + 1) * seq), slice(row * size, (row + 1) * size)
        for first in range(0, hb.shape[1], PAIR):
            lanes = slice(first, first + PAIR)
            weights = cross_weights(both_heads(query[rows, lanes]).astype(BF16), keys[places, lanes], patches)
            mixed[rows, lanes] = one_of_heads(dot_nn(weights.astype(BF16), value[places, lanes]))
    context[...] = mixed[...].astype(BF16)
    total = dot_nn(context[...], whole[3]) + params[0:1] + stream
    pre[...] = total
    out[...] = norm_rows(total, params[1:2], params[2:3])


def cross_backward_kernel(
    offset, seq, patches, place, grad, low, pre, query, context, keys, value, source, own, piece0, piece1, params,
    out, small, keep, send, grad_keys, grad_value, whole, grads, grad_context, grad_query, sem, out_sem,
):
    load_attention(place, own, (piece0, piece1), offset, whole, sem)
    grad_pre = norm_back(pre[...], params[1:2], grad[...], small)
    branch = grad_pre.astype(BF16)
    finish(whole, sem)
    grad_context[...] = dot_nt(branch, whole[3]).astype(BF16).astype(F32)
    grads[3] = dot_tn(context[...], branch).astype(BF16)
    count = branch.shape[0] // seq
    size = keys.shape[0] // count
    for row in range(count):
        rows, places = slice(row * seq, (row + 1) * seq), slice(row * size, (row + 1) * size)
        for first in range(0, branch.shape[1], PAIR):
            lanes = slice(first, first + PAIR)
            query_pair = both_heads(query[rows, lanes]).astype(BF16)
            context_pair = both_heads(grad_context[rows, lanes]).astype(BF16)
            weights = cross_weights(query_pair, keys[places, lanes], patches)
            grad_scores = score_back(weights, dot_nt(context_pair, value[places, lanes]))
            grad_query[rows, lanes] = one_of_heads(dot_nn(grad_scores, keys[places, lanes])) * SCALE
            grad_keys[places, lanes] = (dot_tn(grad_scores, query_pair) * SCALE).astype(BF16)
            grad_value[places, lanes] = dot_tn(weights.astype(BF16), context_pair).astype(BF16)
    query_low = grad_query[...].astype(BF16)
    grads[0] = dot_tn(query_low, low[...]).astype(BF16)
    grads[1] = dot_tn(grad_keys[...], source[...]).astype(BF16)
    grads[2] = dot_tn(grad_value[...], source[...]).astype(BF16)
    store_attention(place, grads, (keep, send), out_sem)
    small[3:4] = column_total(query_low)
    small[4:5] = column_total(grad_value[...])
    out[...] = grad_pre + dot_nn(query_low, whole[0])
    finish(grads, out_sem)


def image_backward_kernel(
    offset, image_offset, image_rows, place, images, grad_keys, grad_value, own, own_image, piece0, piece1,
    out, small, keep, send, whole, whole_image, grads, low, sem, image_sem, out_sem,
):
    load_attention(place, own, (piece0, piece1), offset, whole, sem)
    load_image(place, own_image, (piece0, piece1), image_offset, image_rows, whole_image, image_sem)
    finish(whole, sem)
    finish(whole_image, image_sem)
    count, patches = out.shape[:2]
    size = images.shape[0] // count
    small[...] = jnp.zeros_like(small)
    for row in range(count):
        rows = slice(row * size, (row + 1) * size)
        source = dot_nn(grad_keys[rows], whole[1]) + dot_nn(grad_value[rows], whole[2])
        source = source.astype(BF16)
        low[rows] = source
        out[row] = dot_nn(source, whole_image[...])[:patches]
    grads[...] = dot_tn(low[...], images[...]).astype(BF16)
    store_image(place, grads, (keep, send), out_sem)
    small[0:1] = column_total(low[...])
    finish(grads, out_sem)


def pick_kernel(picks, rows_ref, out):
    for row in range(out.shape[0]):
        out[row] = rows_ref[picks[row]].astype(out.dtype)


def finish_kernel(blocks, mp_quarter, n_held, place, result0, result1, *refs):
    results = (result0, result1)
    outs = refs[n_held:]
    n_outs = sum(2 if kind != "image" else 1 for kind, _, _ in blocks)
    names = []
    for kind, _, _ in blocks:
        names += {"attention": ["attention_in", "attention_out"], "feed": ["feed_in", "feed_out"], "image": ["image"]}[kind]
    unique = list(dict.fromkeys(names))
    targets = dict(zip(unique, outs[: len(unique)]))
    scratch = list(outs[len(unique) :])
    sem, out_sem = scratch[-2:]
    del n_outs
    spot = 0
    filled = []
    for number, (kind, offset, _) in enumerate(blocks):
        buffer = scratch[spot]
        if kind == "attention":
            spot += 3
            quarter = mp_quarter
            span = 4 * quarter // SLICES
            rows, count = span // 2, quarter // span
        elif kind == "feed":
            spot += 3
            quarter = buffer.shape[1]
            span = quarter // SLICES
            rows = span
        else:
            spot += 2
            quarter = mp_quarter
            width = result0.shape[3]
            rows = quarter * buffer.shape[1] // width // SLICES // 2
        for core in range(2):
            for half in range(2):
                for entry in range(4):
                    slot = place[0] ^ (core ^ DISTANCES[half][entry])
                    piece = results[core].at[half, entry, pl.ds(offset, rows)]
                    if kind == "attention":
                        row = (slot % count) * span + half * rows
                        start(piece, buffer.at[slot // count, aligned(row, rows)], sem.at[number])
                    elif kind == "feed":
                        start(piece, buffer.at[half, aligned(slot * span, rows)], sem.at[number])
                    else:
                        image_copies(buffer, piece, quarter, half, slot, 0, sem.at[number], True)
    spot = 0
    for number, (kind, offset, layer) in enumerate(blocks):
        buffer = scratch[spot]
        done = out_sem.at[number]
        if kind == "attention":
            turned, plain = scratch[spot + 1], scratch[spot + 2]
            spot += 3
            finish(buffer.at[:, pl.ds(0, mp_quarter)], sem.at[number])
            for mat in range(3):
                turned[mat] = buffer[mat].astype(F32).T[:, :mp_quarter]
            plain[...] = buffer[3, :mp_quarter].astype(F32)
            start(turned, targets["attention_in"].at[layer], done)
            start(plain, targets["attention_out"].at[layer], done)
        elif kind == "feed":
            turned, plain = scratch[spot + 1], scratch[spot + 2]
            spot += 3
            finish(buffer, sem.at[number])
            turned[...] = buffer[0].astype(F32).T
            plain[...] = buffer[1].astype(F32)
            start(turned, targets["feed_in"].at[layer], done)
            start(plain, targets["feed_out"].at[layer], done)
        else:
            turned = scratch[spot + 1]
            spot += 2
            finish(buffer.at[pl.ds(0, mp_quarter)], sem.at[number])
            turned[...] = buffer[...].astype(F32).T[:, :mp_quarter]
            start(turned, targets["image"], done)
            plain = None
        filled.append((turned, plain, done))
    for turned, plain, done in filled:
        finish(turned, done)
        if plain is not None:
            finish(plain, done)


def shape(dims, kind=F32):
    return jax.ShapeDtypeStruct(tuple(dims), kind)


def call(kernel, ins, outs, scratch, megabytes, flops, aliases=None):
    moved = sum(v.size * v.dtype.itemsize for v, _ in ins) + sum(s.size * s.dtype.itemsize for s, _ in outs)
    return pl.pallas_call(
        kernel,
        in_specs=[spec for _, spec in ins],
        out_specs=[spec for _, spec in outs],
        out_shape=[s for s, _ in outs],
        scratch_shapes=scratch,
        input_output_aliases=aliases or {},
        compiler_params=pltpu.CompilerParams(vmem_limit_bytes=megabytes << 20),
        cost_estimate=pl.CostEstimate(flops=int(flops), bytes_accessed=int(moved), transcendentals=0),
    )(*[v for v, _ in ins])


def on_device(
    tokens, images, segment_of_token, image_of_row, attention_in, query_value_bias, attention_out, output_bias,
    feed_in, feed_bias, feed_out, image_weight, image_bias, norm_gain, norm_bias, cotangent,
):
    mp = lax.axis_size("mp")
    slot = lax.axis_index("dp") % SLICES
    owner = lax.axis_index("mp")
    place = jnp.stack([slot, owner]).astype(jnp.int32)
    own_rows, seq, width = tokens.shape
    group_rows = segment_of_token.shape[0]
    patches, image_width = images.shape[1:]
    quarter = attention_in.shape[3]
    units = feed_in.shape[2]
    n_tokens = own_rows * seq

    local_order = image_of_row % group_rows
    here = owner * own_rows + jnp.arange(own_rows, dtype=jnp.int32)
    chosen = (local_order[None, :] == here[:, None]).astype(jnp.int32)
    source_row = jnp.sum(chosen * jnp.arange(group_rows, dtype=jnp.int32)[None, :], axis=1)
    picks_in = ((owner - source_row // own_rows) % mp) * own_rows + source_row % own_rows
    mine = (jnp.arange(group_rows, dtype=jnp.int32)[None, :] == here[:, None]).astype(jnp.int32)
    image_row = jnp.sum(mine * local_order[None, :], axis=1)
    picks_out = ((owner - image_row // own_rows) % mp) * own_rows + image_row % own_rows
    segments = jnp.sum(chosen[:, :, None] * segment_of_token[None], axis=1)
    code = jnp.arange(own_rows, dtype=jnp.int32)[:, None] * seq + segments
    code_col = code.reshape(n_tokens, 1)
    code_row = code.reshape(own_rows // 2, 2 * seq)

    flat = jnp.concatenate([query_value_bias.reshape(-1), feed_bias.reshape(-1), image_bias])
    flat = jnp.pad(flat, (0, -flat.shape[0] % width)).reshape(-1, width)
    ordered = jnp.stack(ring(flat))[(owner - jnp.arange(mp)) % mp].reshape(mp, -1).astype(F32)
    cut0 = query_value_bias.size
    cut1 = cut0 + feed_bias.size
    head_bias = ordered[:, :cut0].reshape(mp, 3, 2, quarter).transpose(1, 2, 0, 3).reshape(3, 2, width)
    unit_bias = ordered[:, cut0:cut1].reshape(mp, 2, units).transpose(1, 0, 2).reshape(2, -1, width)
    patch_bias = ordered[:, cut1 : cut1 + quarter].reshape(1, width)
    params = jnp.stack([output_bias, norm_gain, norm_bias], axis=1).astype(F32)

    rows_in = jnp.stack(ring(tokens)).reshape(mp * own_rows, seq, width)

    def attention_shard(layer):
        turned = attention_in[layer].transpose(0, 2, 1).reshape(3 * quarter, width)
        return jnp.concatenate([turned, attention_out[layer]])

    def feed_shard(layer):
        return jnp.concatenate([feed_in[layer].T, feed_out[layer]])

    image_shard = image_weight.T
    beyond = image_width - width
    blocks = width // beyond
    image_rest = image_shard[:, width:].reshape(blocks, quarter // blocks, beyond)
    image_rest = image_rest.transpose(1, 0, 2).reshape(quarter // blocks, width)
    image_flat = jnp.concatenate([image_shard[:, :width], image_rest])
    attention_shards = [attention_shard(layer) for layer in range(3)]
    feed_shards = [feed_shard(layer) for layer in range(2)]

    def own_slice(shard, by_half):
        span = shard.shape[0] // SLICES
        if by_half:
            return lax.dynamic_slice_in_dim(shard, slot * span, span).reshape(2, span // 2, width)
        halves = shard.reshape(2, -1, width)
        return lax.dynamic_slice_in_dim(halves, slot * (span // 2), span // 2, axis=1)

    attention_rows = 4 * quarter // SLICES // 2
    feed_rows = units // SLICES
    image_rows = image_flat.shape[0] // SLICES // 2
    text_pieces = gather_weights(own_slice(attention_shards[0], True))
    middle_pieces = gather_weights(
        jnp.concatenate([own_slice(feed_shards[0], False), own_slice(attention_shards[1], True)], axis=1)
    )
    cross_pieces = gather_weights(
        jnp.concatenate([own_slice(attention_shards[2], True), own_slice(image_flat, True)], axis=1)
    )
    last_pieces = gather_weights(own_slice(feed_shards[1], False))
    attention_at = [(text_pieces, 0), (middle_pieces, feed_rows), (cross_pieces, 0)]
    feed_at = [(middle_pieces, 0), (last_pieces, 0)]
    grads_in = jnp.stack(ring(cotangent)).reshape(mp * own_rows, seq, width)

    padded = -(-patches // 16) * 16
    patch_rows = jnp.pad(images, ((0, 0), (0, padded - patches), (0, 0))).reshape(own_rows * padded, image_width)
    n_patches = own_rows * padded

    token_shape = shape((n_tokens, width))
    token_low = shape((n_tokens, width), BF16)
    row_low = shape((own_rows, seq, width), BF16)
    inner_shape = shape((n_tokens, mp * units))
    inner_low = shape((n_tokens, mp * units), BF16)
    patch_low = shape((n_patches, width), BF16)
    square = pltpu.VMEM((4, width, width), BF16)
    wide = pltpu.VMEM((2, mp * units, width), BF16)
    tall = pltpu.VMEM((width, image_width), BF16)
    token_f32 = pltpu.VMEM((n_tokens, width), F32)
    token_bf16 = pltpu.VMEM((n_tokens, width), BF16)
    dma = pltpu.SemaphoreType.DMA
    matmul = 2 * n_tokens * width * width
    patch_matmul = 2 * n_patches * width * width

    def weight_ins(layer):
        (piece0, piece1), _ = attention_at[layer]
        return [(attention_shards[layer], ANY), (piece0, ANY), (piece1, ANY)]

    def feed_ins(layer):
        (piece0, piece1), _ = feed_at[layer]
        return [(feed_shards[layer], ANY), (piece0, ANY), (piece1, ANY)]

    def self_forward(layer, norm, rows, pick):
        return call(
            partial(self_forward_kernel, pick, attention_at[layer][1]),
            [(place, SMEM), (picks_in, SMEM), (rows, VMEM)]
            + weight_ins(layer)
            + [(head_bias[layer], VMEM), (params[norm], VMEM), (code_col, VMEM), (code_row, VMEM)],
            [(token_shape, VMEM), (token_low, VMEM), (token_shape, VMEM)] + [(token_low, VMEM)] * 4,
            [square, dma] + ([token_f32] if pick else []),
            32,
            4 * matmul,
        )

    def self_backward(layer, norm, grad, kept, leave):
        _, low, pre, query, keys, value, context = kept
        return call(
            partial(self_backward_kernel, leave, attention_at[layer][1]),
            [(place, SMEM)]
            + [(v, VMEM) for v in (grad, low, pre, query, keys, value, context)]
            + weight_ins(layer)
            + [(params[norm], VMEM), (code_col, VMEM), (code_row, VMEM)],
            [(row_low if leave else token_shape, VMEM), (shape((8, width)), VMEM)] + [(attention_grad, ANY)] * 2,
            [square, square] + [token_bf16] * 4 + [dma, dma],
            40,
            9 * matmul,
        )

    attention_grad = shape((2, 4, mp, attention_rows, width), BF16)
    feed_grad = shape((2, 4, mp, feed_rows, width), BF16)
    image_grad = shape((2, 4, mp, image_rows, width), BF16)

    def feed_forward(layer, norm, rows, leave):
        return call(
            partial(feed_forward_kernel, leave, feed_at[layer][1]),
            [(place, SMEM), (rows, VMEM)] + feed_ins(layer) + [(unit_bias[layer], VMEM), (params[norm], VMEM)],
            [(row_low if leave else token_shape, VMEM), (token_low, VMEM), (token_shape, VMEM)]
            + [(inner_shape, VMEM), (inner_low, VMEM)],
            [wide, dma],
            40,
            2 * mp * matmul,
        )

    def feed_backward(layer, norm, grad, kept, pick):
        _, low, pre, inner, active = kept
        return call(
            partial(feed_backward_kernel, pick, feed_at[layer][1]),
            [(place, SMEM), (picks_in, SMEM)]
            + [(v, VMEM) for v in (grad, low, pre, inner, active)]
            + feed_ins(layer)
            + [(params[norm], VMEM)],
            [(token_shape, VMEM), (shape((8, width)), VMEM)] + [(feed_grad, ANY)] * 2,
            [wide, wide, dma, dma] + ([token_f32] if pick else []),
            48,
            4 * mp * matmul,
        )

    text_attention = self_forward(0, 0, rows_in, True)
    text_feed = feed_forward(0, 1, text_attention[0], False)
    joining_attention = self_forward(1, 2, text_feed[0], False)
    image_ins = [(image_shard, ANY), (cross_pieces[0], ANY), (cross_pieces[1], ANY)]
    projected, image_keys, image_value = call(
        partial(image_forward_kernel, 0, attention_rows, image_rows),
        [(place, SMEM), (patch_rows, VMEM), (attention_shards[2], ANY)]
        + image_ins
        + [(head_bias[2], VMEM), (patch_bias, VMEM)],
        [(patch_low, VMEM)] * 3,
        [square, tall, dma, dma],
        40,
        3.4 * patch_matmul,
    )
    cross_attention = call(
        partial(cross_forward_kernel, 0, seq, patches),
        [(place, SMEM), (joining_attention[0], VMEM), (image_keys, VMEM), (image_value, VMEM)]
        + weight_ins(2)
        + [(head_bias[2], VMEM), (params[3], VMEM)],
        [(token_shape, VMEM), (token_low, VMEM), (token_shape, VMEM), (token_shape, VMEM), (token_low, VMEM)],
        [square, token_f32, dma],
        32,
        3 * matmul,
    )
    joining_feed = feed_forward(1, 4, cross_attention[0], True)
    rows_out = jnp.stack(ring(joining_feed[0])).reshape(mp * own_rows, seq, width)

    def pick_rows(rows):
        return call(
            pick_kernel, [(picks_out, SMEM), (rows, VMEM)], [(shape((own_rows, seq, width)), VMEM)], [], 16, 0
        )[0]

    mixed_out = pick_rows(rows_out)
    grad, small_joining_feed, keep, send = feed_backward(1, 4, grads_in, joining_feed, True)
    last_result = reduce_grads(add(keep, swap(send, 1)))
    grad, small_cross, keep, send, grad_keys, grad_value = call(
        partial(cross_backward_kernel, 0, seq, patches),
        [(place, SMEM), (grad, VMEM)]
        + [(cross_attention[i], VMEM) for i in (1, 2, 3, 4)]
        + [(image_keys, VMEM), (image_value, VMEM), (projected, VMEM)]
        + weight_ins(2)
        + [(params[3], VMEM)],
        [(token_shape, VMEM), (shape((8, width)), VMEM)] + [(attention_grad, ANY)] * 2 + [(patch_low, VMEM)] * 2,
        [square, square, token_f32, token_f32, dma, dma],
        56,
        5 * matmul + 2 * patch_matmul,
    )
    cross_sum = add(keep, swap(send, 1))
    grad, small_joining, keep, send = self_backward(1, 2, grad, joining_attention, False)
    joining_sum = add(keep, swap(send, 1))
    grad_images, small_image, keep, send = call(
        partial(image_backward_kernel, 0, attention_rows, image_rows),
        [(place, SMEM), (patch_rows, VMEM), (grad_keys, VMEM), (grad_value, VMEM), (attention_shards[2], ANY)]
        + image_ins,
        [(shape(images.shape), VMEM), (shape((8, width)), VMEM)] + [(image_grad, ANY)] * 2,
        [square, tall, tall, pltpu.VMEM((n_patches, width), BF16), dma, dma, dma],
        48,
        4.7 * patch_matmul,
    )
    image_sum = add(keep, swap(send, 1))
    middle_result = reduce_grads(jnp.concatenate([cross_sum, joining_sum, image_sum], axis=3))
    grad, small_text_feed, keep, send = feed_backward(0, 1, grad, text_feed, False)
    feed_result = reduce_grads(add(keep, swap(send, 1)))
    small_early = total_everywhere(
        jnp.concatenate([small_text_feed, small_joining, small_cross, small_joining_feed, small_image])
    )
    rows_back, small_text, keep, send = self_backward(0, 0, grad, text_attention, True)
    text_result = reduce_grads(add(keep, swap(send, 1)))
    small_late = total_everywhere(small_text)
    grad_tokens = pick_rows(jnp.stack(ring(rows_back)).reshape(mp * own_rows, seq, width))

    whole_shapes = {
        "attention_in": shape(attention_in.shape),
        "attention_out": shape(attention_out.shape),
        "feed_in": shape(feed_in.shape),
        "feed_out": shape(feed_out.shape),
        "image": shape(image_weight.shape),
    }
    padded_quarter = -(-quarter // 128) * 128
    scratch_of = {
        "attention": [
            pltpu.VMEM((4, padded_quarter, width), BF16),
            pltpu.VMEM((3, width, quarter), F32),
            pltpu.VMEM((quarter, width), F32),
        ],
        "feed": [
            pltpu.VMEM((2, units, width), BF16),
            pltpu.VMEM((width, units), F32),
            pltpu.VMEM((units, width), F32),
        ],
        "image": [pltpu.VMEM((padded_quarter, image_width), BF16), pltpu.VMEM((image_width, quarter), F32)],
    }
    names_of = {"attention": ["attention_in", "attention_out"], "feed": ["feed_in", "feed_out"], "image": ["image"]}
    written = {}

    def write_out(result, blocks):
        names = list(dict.fromkeys(name for kind, _, _ in blocks for name in names_of[kind]))
        held = [name for name in names if name in written]
        scratch = [entry for kind, _, _ in blocks for entry in scratch_of[kind]]
        results = call(
            partial(finish_kernel, blocks, quarter, len(held)),
            [(place, SMEM), (result[0], ANY), (result[1], ANY)] + [(written[name], ANY) for name in held],
            [(whole_shapes[name], ANY) for name in names],
            scratch + [dma((len(blocks),)), dma((len(blocks),))],
            32,
            0,
            {3 + i: names.index(name) for i, name in enumerate(held)},
        )
        written.update(zip(names, results))

    write_out(last_result, (("feed", 0, 1),))
    write_out(
        middle_result,
        (("attention", 0, 2), ("attention", attention_rows, 1), ("image", 2 * attention_rows, 0)),
    )
    write_out(feed_result, (("feed", 0, 0),))
    write_out(text_result, (("attention", 0, 0),))

    smalls = jnp.concatenate([small_late, small_early]).reshape(6, 8, width)
    order = [0, 1, 2, 3, 4]
    grad_norm_gain = jnp.stack([smalls[i, 0] for i in order])
    grad_norm_bias = jnp.stack([smalls[i, 1] for i in order])
    grad_output_bias = jnp.stack([smalls[i, 2] for i in order])

    def own_part(values):
        return lax.dynamic_slice_in_dim(values, owner * quarter, quarter, axis=values.ndim - 1)

    grad_query_value_bias = own_part(jnp.stack([smalls[i, 3:5] for i in (0, 2, 3)]))
    grad_feed_bias = jnp.stack([smalls[i, 3 : 3 + mp].reshape(-1) for i in (1, 4)])
    grad_feed_bias = lax.dynamic_slice_in_dim(grad_feed_bias, owner * units, units, axis=1)
    grad_image_bias = own_part(smalls[5, 0])
    return (
        mixed_out,
        grad_tokens,
        grad_images,
        written["attention_in"],
        grad_query_value_bias,
        written["attention_out"],
        grad_output_bias,
        written["feed_in"],
        grad_feed_bias,
        written["feed_out"],
        written["image"],
        grad_image_bias,
        grad_norm_gain,
        grad_norm_bias,
    )


def solution(mesh):
    rows = P(("dp", "mp"), None, None)
    return jax.shard_map(
        on_device,
        mesh=mesh,
        in_specs=(
            rows,
            rows,
            P("dp", None),
            P("dp"),
            P(None, None, None, "mp"),
            P(None, None, "mp"),
            P(None, "mp", None),
            P(),
            P(None, None, "mp"),
            P(None, "mp"),
            P(None, "mp", None),
            P(None, "mp"),
            P("mp"),
            P(),
            P(),
            rows,
        ),
        out_specs=(
            rows,
            rows,
            rows,
            P(None, None, None, "mp"),
            P(None, None, "mp"),
            P(None, "mp", None),
            P(),
            P(None, None, "mp"),
            P(None, "mp"),
            P(None, "mp", None),
            P(None, "mp"),
            P("mp"),
            P(),
            P(),
        ),
        check_vma=False,
    )
```

```python
from functools import partial

import jax
import jax.numpy as jnp
from jax import lax
from jax.experimental import pallas as pl
from jax.experimental.pallas import tpu as pltpu
from jax.sharding import PartitionSpec as P

HEAD_DIM = 64
STACK = 4 * HEAD_DIM
TOGETHER = 6
SLICES = 8
EPSILON = 1e-06
BLOCKED = -1000000000.0
SCALE = HEAD_DIM ** (-0.5)
DISTANCES = ((0, 2, 4, 6), (0, 4, 2, 6))
F32 = jnp.float32
BF16 = jnp.bfloat16

ANY = pl.BlockSpec(memory_space=pl.ANY)
VMEM = pl.BlockSpec(memory_space=pltpu.VMEM)
SMEM = pl.BlockSpec(memory_space=pltpu.SMEM)


def swap(values, bit):
    count = lax.axis_size("dp")
    return lax.ppermute(values, "dp", [(i, i ^ bit) for i in range(count)])


def pass_on(values, way=1):
    count = lax.axis_size("mp")
    return lax.ppermute(values, "mp", [(i, (i + way) % count) for i in range(count)])


def swap_owner(values, bit):
    count = lax.axis_size("mp")
    return lax.ppermute(values, "mp", [(i, i ^ bit) for i in range(count)])


def added(*terms):
    total = terms[0].astype(F32)
    for term in terms[1:]:
        total = total + term
    return total.astype(BF16)


def dot_nn(left, right):
    return lax.dot_general(left, right, (((1,), (0,)), ((), ())), preferred_element_type=F32)


def dot_nt(left, right):
    return lax.dot_general(left, right, (((1,), (1,)), ((), ())), preferred_element_type=F32)


def dot_tn(left, right):
    return lax.dot_general(left, right, (((0,), (0,)), ((), ())), preferred_element_type=F32)


def start(source, target, sem):
    pltpu.make_async_copy(source, target, sem).start()


def finish(whole, sem):
    pltpu.make_async_copy(whole, whole, sem).wait()


def aligned(first, count, step=16):
    return pl.ds(pl.multiple_of(first, step), count)


def each_slice(place, first_step, mp):
    for core in range(2):
        for half in range(2):
            for entry in range(4):
                slot = place[0] ^ (core ^ DISTANCES[half][entry])
                for step in range(first_step, mp):
                    yield core, half, entry, step, slot, (place[1] + mp - step) % mp


def piece_of(pieces, core, half, entry):
    return pieces[4 * core + 2 * half + entry // 2].at[entry % 2]


def attention_spot(whole, quarter, half, slot, owner):
    span = 4 * quarter // SLICES
    count = quarter // span
    row = owner * quarter + (slot % count) * span + half * (span // 2)
    return whole.at[slot // count, aligned(row, span // 2)]


def load_attention(place, own, pieces, offset, layer, whole, sems):
    mp = pieces[0].shape[1] + 1
    quarter = whole.shape[1] // mp
    rows = quarter // 4
    for mat in range(4):
        source = own[0].at[layer, mat] if mat < 3 else own[1].at[layer]
        start(source, whole.at[mat, aligned(place[1] * quarter, quarter)], sems.at[mat])
    for core, half, entry, step, slot, owner in each_slice(place, 1, mp):
        start(
            piece_of(pieces, core, half, entry).at[step - 1, pl.ds(offset, rows)],
            attention_spot(whole, quarter, half, slot, owner),
            sems.at[slot // 2],
        )


def store_attention(place, whole, outs, offset, sem):
    mp = outs[0].shape[2]
    quarter = whole.shape[1] // mp
    for core, half, entry, step, slot, owner in each_slice(place, 0, mp):
        start(
            attention_spot(whole, quarter, half, slot, owner),
            outs[core].at[half, entry, step, pl.ds(offset, quarter // 4)],
            sem,
        )


def feed_spot(whole, half, slot, owner):
    span = whole.shape[2] // SLICES
    return whole.at[half, owner, aligned(slot * span, span)]


def load_feed(place, own, pieces, offset, layer, whole, sems):
    mp = pieces[0].shape[1] + 1
    rows = whole.shape[2] // SLICES
    for half in range(2):
        start(own[half].at[layer], whole.at[half, place[1]], sems.at[half, place[1]])
    for core, half, entry, step, slot, owner in each_slice(place, 1, mp):
        start(
            piece_of(pieces, core, half, entry).at[step - 1, pl.ds(offset, rows)],
            feed_spot(whole, half, slot, owner),
            sems.at[half, owner],
        )


def store_feed(place, whole, outs, sem):
    mp = outs[0].shape[2]
    for core, half, entry, step, slot, owner in each_slice(place, 0, mp):
        start(feed_spot(whole, half, slot, owner), outs[core].at[half, entry, step], sem)


def image_copies(whole, piece, quarter, half, slot, owner, sem, inward):
    rows, width = piece.shape
    span = 2 * rows
    beyond = whole.shape[1] - width
    blocks = width // beyond
    plain = quarter // span
    base = owner * quarter + half * rows

    def move(inner, outer):
        start(inner, outer, sem) if inward else start(outer, inner, sem)

    @pl.when(slot < plain)
    def _():
        move(piece, whole.at[aligned(base + slot * span, rows), pl.ds(0, width)])

    @pl.when(slot >= plain)
    def _():
        for block in range(blocks):
            row = base + block * (quarter // blocks) + (slot - plain) * span
            move(
                piece.at[:, pl.ds(block * beyond, beyond)],
                whole.at[aligned(row, rows), pl.ds(width, beyond)],
            )


def load_image(place, own, pieces, offset, rows, whole, sem):
    mp = pieces[0].shape[1] + 1
    quarter = whole.shape[0] // mp
    start(own, whole.at[aligned(place[1] * quarter, quarter)], sem)
    for core, half, entry, step, slot, owner in each_slice(place, 1, mp):
        piece = piece_of(pieces, core, half, entry).at[step - 1, pl.ds(offset, rows)]
        image_copies(whole, piece, quarter, half, slot, owner, sem, True)


def store_image(place, whole, outs, offset, rows, sem):
    mp = outs[0].shape[2]
    quarter = whole.shape[0] // mp
    for core, half, entry, step, slot, owner in each_slice(place, 0, mp):
        piece = outs[core].at[half, entry, step, pl.ds(offset, rows)]
        image_copies(whole, piece, quarter, half, slot, owner, sem, False)


def norm_rows(values, gain_row, shift_row):
    center = values - jnp.mean(values, axis=-1, keepdims=True)
    moment = jnp.mean(center * center, axis=-1, keepdims=True)
    return center * lax.rsqrt(moment + EPSILON) * gain_row + shift_row


def norm_back(pre_norm, gain_row, grad_out, small):
    center = pre_norm - jnp.mean(pre_norm, axis=-1, keepdims=True)
    scale = lax.rsqrt(jnp.mean(center * center, axis=-1, keepdims=True) + EPSILON)
    normal = center * scale
    lifted = grad_out * gain_row
    grad_pre = scale * (
        lifted
        - jnp.mean(lifted, axis=-1, keepdims=True)
        - normal * jnp.mean(lifted * normal, axis=-1, keepdims=True)
    )
    small[...] = jnp.zeros_like(small)
    small[0:1] = jnp.sum(grad_out * normal, axis=0, keepdims=True)
    small[1:2] = jnp.sum(grad_out, axis=0, keepdims=True)
    small[2:3] = jnp.sum(grad_pre, axis=0, keepdims=True)
    return grad_pre


def column_total(values):
    return jnp.sum(values.astype(F32), axis=0, keepdims=True)


def spread_heads(values):
    lane = lax.broadcasted_iota(jnp.int32, (1, values.shape[1]), 1)
    parts = []
    for first in range(0, values.shape[1], HEAD_DIM):
        mask = ((lane >= first) & (lane < first + HEAD_DIM)).astype(F32).astype(values.dtype)
        parts.append(values * mask)
    return jnp.concatenate(parts, axis=0)


def pick_heads(values):
    lane = lax.broadcasted_iota(jnp.int32, (1, values.shape[1]), 1)
    rows = values.shape[0] * HEAD_DIM // values.shape[1]
    picked = values[:rows]
    for head in range(1, values.shape[1] // HEAD_DIM):
        picked = jnp.where(lane >= head * HEAD_DIM, values[head * rows : (head + 1) * rows], picked)
    return picked


def softmax(scores):
    raised = jnp.exp(scores - jnp.max(scores, axis=-1, keepdims=True))
    return raised * (1.0 / jnp.sum(raised, axis=-1, keepdims=True))


def score_back(weights, grad_weights):
    along = weights * grad_weights
    return (along - weights * jnp.sum(along, axis=-1, keepdims=True)).astype(BF16)


def attention_units(count, row_size, place_size, width):
    units = []
    for number in range(count):
        rows = slice(number * row_size, (number + 1) * row_size)
        places = slice(number * place_size, (number + 1) * place_size)
        units += [(number, rows, places, slice(first, first + STACK)) for first in range(0, width, STACK)]
    return [units[first : first + TOGETHER] for first in range(0, len(units), TOGETHER)]


def attend_forward(units, allowed, query, keys, value, context):
    for group in units:
        scores = [dot_nt(spread_heads(query[rows, lanes]).astype(BF16), keys[at, lanes]) for _, rows, at, lanes in group]
        weights = [
            softmax(jnp.where(allowed(unit[0]), score * SCALE, BLOCKED)).astype(BF16)
            for unit, score in zip(group, scores)
        ]
        for (_, rows, at, lanes), weight in zip(group, weights):
            context[rows, lanes] = pick_heads(dot_nn(weight, value[at, lanes])).astype(context.dtype)


def attend_backward(units, allowed, query, keys, value, grad_context, grad_query, grad_keys, grad_value):
    for group in units:
        queries = [spread_heads(query[rows, lanes]).astype(BF16) for _, rows, _, lanes in group]
        contexts = [spread_heads(grad_context[rows, lanes]).astype(BF16) for _, rows, _, lanes in group]
        scores = [dot_nt(one, keys[at, lanes]) for one, (_, _, at, lanes) in zip(queries, group)]
        grad_weights = [dot_nt(one, value[at, lanes]) for one, (_, _, at, lanes) in zip(contexts, group)]
        weights = [
            softmax(jnp.where(allowed(unit[0]), score * SCALE, BLOCKED)) for unit, score in zip(group, scores)
        ]
        grad_scores = [score_back(one, other) for one, other in zip(weights, grad_weights)]
        for weight, one, (_, _, at, lanes) in zip(weights, contexts, group):
            grad_value[at, lanes] = dot_tn(weight.astype(BF16), one).astype(BF16)
        for grad_score, one, (_, _, at, lanes) in zip(grad_scores, queries, group):
            grad_keys[at, lanes] = (dot_tn(grad_score, one) * SCALE).astype(BF16)
        for grad_score, (_, rows, at, lanes) in zip(grad_scores, group):
            mixed = pick_heads(dot_nn(grad_score, keys[at, lanes])) * SCALE
            grad_query[rows, lanes] = mixed.astype(grad_query.dtype)


def same_segment(code_col, code_row):
    size = code_row.shape[1]

    def allowed(group):
        column = code_col[group * size : (group + 1) * size]
        return jnp.concatenate([column] * (STACK // HEAD_DIM), axis=0) == code_row[group : group + 1]

    return allowed


def real_patch(size, patches):
    column = lax.broadcasted_iota(jnp.int32, (1, size), 1)
    return lambda row: column < patches


def gather_rows(picks, rows_ref, target):
    seq = rows_ref.shape[1]
    for row in range(target.shape[0] // seq):
        target[row * seq : (row + 1) * seq] = rows_ref[picks[row]].astype(target.dtype)


def leave_rows(values, target):
    seq = target.shape[1]
    for row in range(target.shape[0]):
        target[row] = values[row * seq : (row + 1) * seq].astype(target.dtype)


def slice_kernel(place, inward, outward, feed_in, feed_out, image, text, first, joining, cross, last, sems):
    slot = place[0]
    quarter, width = inward.shape[2:]
    span = 4 * quarter // SLICES
    count = quarter // span
    rows = span // 2

    def attention(layer, target, offset, sem):
        for half in range(2):
            row = (slot % count) * span + half * rows
            spot = target.at[half, pl.ds(offset, rows)]

            @pl.when(slot < 3 * count)
            def _():
                start(inward.at[layer, slot // count, aligned(row, rows)], spot, sem)

            @pl.when(slot >= 3 * count)
            def _():
                start(outward.at[layer, aligned(row, rows)], spot, sem)

    def feed(layer, target, sem):
        size = feed_in.shape[1] // SLICES
        for half, source in enumerate((feed_in, feed_out)):
            start(source.at[layer, aligned(slot * size, size)], target.at[half, pl.ds(0, size)], sem)

    image_rows = cross.shape[1] - rows
    attention(0, text, 0, sems.at[0])
    attention(2, cross, 0, sems.at[3])
    for half in range(2):
        image_copies(image, cross.at[half, pl.ds(rows, image_rows)], quarter, half, slot, 0, sems.at[3], False)
    feed(0, first, sems.at[1])
    attention(1, joining, 0, sems.at[2])
    feed(1, last, sems.at[4])
    for number, target in enumerate((text, first, joining, cross, last)):
        finish(target, sems.at[number])


def self_forward_kernel(
    pick, layer, norm, offset, place, picks, rows_ref, inward, outward, *refs,
):
    pieces, refs = refs[:8], refs[8:]
    bias, params, code_col, code_row, out, low, pre, query, keys, value, context, whole, sems, *held = refs
    load_attention(place, (inward, outward), pieces, offset, layer, whole, sems)
    if pick:
        gather_rows(picks, rows_ref, held[0])
        stream = held[0][...]
    else:
        stream = rows_ref[...]
    hb = stream.astype(BF16)
    low[...] = hb
    finish(whole.at[0], sems.at[0])
    query[...] = (dot_nt(hb, whole[0]) + bias[2 * layer : 2 * layer + 1]).astype(BF16)
    finish(whole.at[1], sems.at[1])
    keys[...] = dot_nt(hb, whole[1]).astype(BF16)
    finish(whole.at[2], sems.at[2])
    value[...] = (dot_nt(hb, whole[2]) + bias[2 * layer + 1 : 2 * layer + 2]).astype(BF16)
    groups, size = code_row.shape
    units = attention_units(groups, size, size, hb.shape[1])
    attend_forward(units, same_segment(code_col, code_row), query, keys, value, context)
    finish(whole.at[3], sems.at[3])
    total = dot_nn(context[...], whole[3]) + params[3 * norm : 3 * norm + 1] + stream
    pre[...] = total
    out[...] = norm_rows(total, params[3 * norm + 1 : 3 * norm + 2], params[3 * norm + 2 : 3 * norm + 3])


def self_backward_kernel(
    leave, layer, norm, offset, spot, n_held, place, grad, low, pre, query, keys, value, context, inward, outward, *refs,
):
    pieces, refs = refs[:8], refs[8:]
    params, code_col, code_row = refs[:3]
    out, small, keep, send, whole, grads, grad_context, grad_query, grad_keys, grad_value, sems, out_sem = refs[3 + n_held :]
    load_attention(place, (inward, outward), pieces, offset, layer, whole, sems)
    grad_pre = norm_back(pre[...], params[3 * norm + 1 : 3 * norm + 2], grad[...], small)
    branch = grad_pre.astype(BF16)
    finish(whole.at[3], sems.at[3])
    grad_context[...] = dot_nt(branch, whole[3]).astype(BF16)
    grads[3] = dot_tn(context[...], branch).astype(BF16)
    groups, size = code_row.shape
    units = attention_units(groups, size, size, branch.shape[1])
    attend_backward(
        units, same_segment(code_col, code_row), query, keys, value, grad_context, grad_query, grad_keys, grad_value
    )
    hb = low[...]
    grads[0] = dot_tn(grad_query[...], hb).astype(BF16)
    grads[1] = dot_tn(grad_keys[...], hb).astype(BF16)
    grads[2] = dot_tn(grad_value[...], hb).astype(BF16)
    store_attention(place, grads, (keep, send), spot, out_sem)
    small[3:4] = column_total(grad_query[...])
    small[4:5] = column_total(grad_value[...])
    total = grad_pre
    for mat, part in enumerate((grad_query, grad_keys, grad_value)):
        finish(whole.at[mat], sems.at[mat])
        total = total + dot_nn(part[...], whole[mat])
    if leave:
        leave_rows(total, out)
    else:
        out[...] = total
    finish(grads, out_sem)


def feed_forward_kernel(
    leave, layer, norm, offset, place, rows_ref, first_weight, second_weight, *refs,
):
    pieces, refs = refs[:8], refs[8:]
    bias, params, out, low, pre, slope, active, whole, sems = refs
    load_feed(place, (first_weight, second_weight), pieces, offset, layer, whole, sems)
    stream = rows_ref[...]
    hb = stream.astype(BF16)
    low[...] = hb
    parts, size = whole.shape[1], whole.shape[3]
    total = params[3 * norm : 3 * norm + 1] + stream
    for part in range(parts):
        lanes = slice(part * size, (part + 1) * size)
        row = 6 + layer * parts + part
        finish(whole.at[0, part], sems.at[0, part])
        units = dot_nn(hb, whole[0, part]) + bias[row : row + 1]
        share = 0.5 * (1.0 + lax.erf(units * (2.0 ** -0.5)))
        slope[:, lanes] = share + units * jnp.exp(-0.5 * units * units) * 0.3989422804014327
        gated = (units * share).astype(BF16)
        active[:, lanes] = gated
        finish(whole.at[1, part], sems.at[1, part])
        total = total + dot_nn(gated, whole[1, part])
    pre[...] = total
    result = norm_rows(total, params[3 * norm + 1 : 3 * norm + 2], params[3 * norm + 2 : 3 * norm + 3])
    if leave:
        leave_rows(result, out)
    else:
        out[...] = result


def feed_backward_kernel(
    pick, layer, norm, offset, place, picks, grad, low, pre, slope, active, first_weight, second_weight, *refs,
):
    pieces, refs = refs[:8], refs[8:]
    params, out, small, keep, send, whole, grads, sems, out_sem, *held = refs
    load_feed(place, (first_weight, second_weight), pieces, offset, layer, whole, sems)
    if pick:
        gather_rows(picks, grad, held[0])
        grad = held[0]
    grad_pre = norm_back(pre[...], params[3 * norm + 1 : 3 * norm + 2], grad[...], small)
    branch = grad_pre.astype(BF16)
    parts, size = whole.shape[1], whole.shape[3]
    hb = low[...]
    total = grad_pre
    for part in range(parts):
        lanes = slice(part * size, (part + 1) * size)
        grads[1, part] = dot_tn(active[:, lanes], branch).astype(BF16)
        finish(whole.at[1, part], sems.at[1, part])
        grad_units = (dot_nt(branch, whole[1, part]) * slope[:, lanes]).astype(BF16)
        grads[0, part] = dot_tn(hb, grad_units).astype(BF16)
        small[3 + part : 4 + part] = column_total(grad_units)
        finish(whole.at[0, part], sems.at[0, part])
        total = total + dot_nt(grad_units, whole[0, part])
    store_feed(place, grads, (keep, send), out_sem)
    out[...] = total
    finish(grads, out_sem)


def finish_all(whole, sems):
    for mat in range(whole.shape[0]):
        finish(whole.at[mat], sems.at[mat])


def image_forward_kernel(
    layer, offset, image_offset, image_rows, place, images, image, inward, outward, *refs,
):
    pieces, refs = refs[:8], refs[8:]
    bias, projected, keys, value, whole, whole_image, sems, image_sem = refs
    load_image(place, image, pieces, image_offset, image_rows, whole_image, image_sem)
    load_attention(place, (inward, outward), pieces, offset, layer, whole, sems)
    finish(whole_image, image_sem)
    size = images.shape[0] // 4
    last = bias.shape[0] - 1
    for first in range(0, images.shape[0], size):
        rows = slice(first, first + size)
        source = (dot_nt(images[rows], whole_image[...]) + bias[last : last + 1]).astype(BF16)
        projected[rows] = source
        if first == 0:
            finish_all(whole, sems)
        keys[rows] = dot_nt(source, whole[1]).astype(BF16)
        value[rows] = (dot_nt(source, whole[2]) + bias[2 * layer + 1 : 2 * layer + 2]).astype(BF16)


def cross_forward_kernel(
    layer, norm, offset, seq, patches, place, rows_ref, keys, value, inward, outward, *refs,
):
    pieces, refs = refs[:8], refs[8:]
    bias, params, out, low, pre, query, context, whole, mixed, sems = refs
    load_attention(place, (inward, outward), pieces, offset, layer, whole, sems)
    stream = rows_ref[...]
    hb = stream.astype(BF16)
    low[...] = hb
    finish_all(whole, sems)
    query[...] = (dot_nt(hb, whole[0]) + bias[2 * layer : 2 * layer + 1]).astype(BF16).astype(F32)
    count = stream.shape[0] // seq
    size = keys.shape[0] // count
    units = attention_units(count, seq, size, hb.shape[1])
    attend_forward(units, real_patch(size, patches), query, keys, value, mixed)
    context[...] = mixed[...].astype(BF16)
    total = dot_nn(context[...], whole[3]) + params[3 * norm : 3 * norm + 1] + stream
    pre[...] = total
    out[...] = norm_rows(total, params[3 * norm + 1 : 3 * norm + 2], params[3 * norm + 2 : 3 * norm + 3])


def cross_backward_kernel(
    layer, norm, offset, spot, seq, patches, place, grad, low, pre, query, context, keys, value, source, inward, outward,
    *refs,
):
    pieces, refs = refs[:8], refs[8:]
    params, out, small, keep, send, grad_keys, grad_value, whole, grads, grad_context, grad_query, sems, out_sem = refs
    load_attention(place, (inward, outward), pieces, offset, layer, whole, sems)
    grad_pre = norm_back(pre[...], params[3 * norm + 1 : 3 * norm + 2], grad[...], small)
    branch = grad_pre.astype(BF16)
    finish_all(whole, sems)
    grad_context[...] = dot_nt(branch, whole[3]).astype(BF16).astype(F32)
    grads[3] = dot_tn(context[...], branch).astype(BF16)
    count = branch.shape[0] // seq
    size = keys.shape[0] // count
    units = attention_units(count, seq, size, branch.shape[1])
    attend_backward(
        units, real_patch(size, patches), query, keys, value, grad_context, grad_query, grad_keys, grad_value
    )
    query_low = grad_query[...].astype(BF16)
    grads[0] = dot_tn(query_low, low[...]).astype(BF16)
    grads[1] = dot_tn(grad_keys[...], source[...]).astype(BF16)
    grads[2] = dot_tn(grad_value[...], source[...]).astype(BF16)
    store_attention(place, grads, (keep, send), spot, out_sem)
    small[3:4] = column_total(query_low)
    small[4:5] = column_total(grad_value[...])
    out[...] = grad_pre + dot_nn(query_low, whole[0])
    finish(grads, out_sem)


def image_backward_kernel(
    layer, offset, image_offset, image_rows, spot, n_held, place, images, grad_keys, grad_value, image, inward, outward,
    *refs,
):
    pieces, refs = refs[:8], refs[8 + n_held :]
    out, small, keep, send, whole, whole_image, grads, low, sems, image_sem, out_sem = refs
    load_attention(place, (inward, outward), pieces, offset, layer, whole, sems)
    load_image(place, image, pieces, image_offset, image_rows, whole_image, image_sem)
    finish_all(whole, sems)
    finish(whole_image, image_sem)
    count, patches = out.shape[:2]
    size = images.shape[0] // count
    small[...] = jnp.zeros_like(small)
    for row in range(count):
        rows = slice(row * size, (row + 1) * size)
        source = dot_nn(grad_keys[rows], whole[1]) + dot_nn(grad_value[rows], whole[2])
        source = source.astype(BF16)
        low[rows] = source
        out[row] = dot_nn(source, whole_image[...])[:patches]
    grads[...] = dot_tn(low[...], images[...]).astype(BF16)
    store_image(place, grads, (keep, send), spot, image_rows, out_sem)
    small[0:1] = column_total(low[...])
    finish(grads, out_sem)


def pick_kernel(picks, rows_ref, out):
    for row in range(out.shape[0]):
        out[row] = rows_ref[picks[row]].astype(out.dtype)


def finish_kernel(blocks, quarter, names, held, place, *refs):
    results, refs = refs[:8], refs[8:]
    width = results[0].shape[2]
    targets = dict(zip(names, refs[held:]))
    scratch = refs[held + len(names) :]
    sem, out_sem = scratch[-2:]
    for number, (kind, offset, _) in enumerate(blocks):
        buffer = scratch[2 * number]
        for core in range(2):
            for half in range(2):
                for entry in range(4):
                    slot = place[0] ^ (core ^ DISTANCES[half][entry])
                    piece = piece_of(results, core, half, entry)
                    if kind == "attention":
                        rows = quarter // 4
                        spot = attention_spot(buffer, quarter, half, slot, 0)
                        start(piece.at[pl.ds(offset, rows)], spot, sem.at[number])
                    elif kind == "feed":
                        rows = buffer.shape[1] // SLICES
                        spot = buffer.at[half, aligned(slot * rows, rows)]
                        start(piece.at[pl.ds(offset, rows)], spot, sem.at[number])
                    else:
                        rows = quarter * buffer.shape[1] // width // SLICES // 2
                        piece = piece.at[pl.ds(offset, rows)]
                        image_copies(buffer, piece, quarter, half, slot, 0, sem.at[number], True)
    for number, (kind, _, layer) in enumerate(blocks):
        buffer, wide = scratch[2 * number : 2 * number + 2]
        done = out_sem.at[number]
        finish(buffer, sem.at[number])
        wide[...] = buffer[...].astype(F32)
        if kind == "attention":
            start(wide.at[pl.ds(0, 3)], targets["attention_in"].at[layer], done)
            start(wide.at[3], targets["attention_out"].at[layer], done)
        elif kind == "feed":
            start(wide.at[0], targets["feed_in"].at[layer], done)
            start(wide.at[1], targets["feed_out"].at[layer], done)
        else:
            start(wide, targets["image"], done)
    for number in range(len(blocks)):
        finish(scratch[2 * number + 1], out_sem.at[number])


def shape(dims, kind=F32):
    return jax.ShapeDtypeStruct(tuple(dims), kind)


def call(kernel, ins, outs, scratch, megabytes, aliases=None):
    return pl.pallas_call(
        kernel,
        in_specs=[spec for _, spec in ins],
        out_specs=[spec for _, spec in outs],
        out_shape=[s for s, _ in outs],
        scratch_shapes=scratch,
        input_output_aliases=aliases or {},
        compiler_params=pltpu.CompilerParams(vmem_limit_bytes=megabytes << 20),
        cost_estimate=pl.CostEstimate(flops=0, bytes_accessed=0, transcendentals=0),
    )(*[v for v, _ in ins])


class Ring:
    def __init__(self, at, name, own):
        self.at, self.name = at, name
        at[name] = {0: own}

    def up(self):
        parts = self.at[self.name]
        parts[1] = pass_on(parts[0])

    def down(self):
        parts = self.at[self.name]
        parts[3] = pass_on(parts[0], -1)

    def far(self):
        parts = self.at[self.name]
        parts[2] = pass_on(parts[1])

    def take(self):
        parts = self.at.pop(self.name)
        return [parts[i] for i in range(4)]


class Widen:
    def __init__(self, at, name, first, second):
        self.at, self.name = at, name
        at[name] = {"own": (first, second)}

    def one(self):
        held = self.at[self.name]
        first, second = held.pop("own")
        held["both"] = (first, swap(first, 2), second, swap(second, 4))

    def two(self):
        held = self.at[self.name]
        both = held.pop("both")
        near = jnp.stack(both[:2]), jnp.stack(both[2:])
        held["near"] = near
        held["far"] = swap(near[0], 4), swap(near[1], 2)
        held["near core"] = swap(near[0], 1), swap(near[1], 1)

    def core(self):
        held = self.at[self.name]
        held["far core"] = swap(held["far"][0], 1), swap(held["far"][1], 1)

    def take(self):
        held = self.at.pop(self.name)
        return [held[kind + core][half] for core in ("", " core") for half in range(2) for kind in ("near", "far")]


class Reduce:
    def __init__(self, at, name, keep, send):
        self.at, self.name = at, name
        at[name] = {"keep": keep, "send": send}

    def core(self):
        held = self.at[self.name]
        held["core"] = swap(held.pop("send"), 1)

    def one(self):
        held = self.at[self.name]
        keep, core = held["keep"], held["core"]
        held["one"] = swap(added(keep[0, 2:], core[0, 2:]), 4), swap(added(keep[1, 2:], core[1, 2:]), 2)

    def two(self):
        held = self.at[self.name]
        keep, core, one = held["keep"], held["core"], held["one"]
        held["two"] = (
            swap(added(keep[0, 1], core[0, 1], one[0][1]), 2),
            swap(added(keep[1, 1], core[1, 1], one[1][1]), 4),
        )

    def part(self, step, *more):
        held = self.at[self.name]
        keep, core, one, two = held["keep"], held["core"], held["one"], held["two"]
        return jnp.stack(
            [
                added(keep[i, 0, step], core[i, 0, step], one[i][0, step], two[i][step], *[term[i] for term in more])
                for i in range(2)
            ]
        )

    def far(self):
        held = self.at[self.name]
        held["far"] = pass_on(self.part(2))

    def near(self):
        held = self.at[self.name]
        held["up"] = pass_on(self.part(3, held.pop("far")))
        held["down"] = pass_on(self.part(1), -1)

    def widen(self):
        held = self.at[self.name]
        own = self.part(0, held["up"], held["down"])
        self.at.pop(self.name)
        bit = SLICES
        while bit < lax.axis_size("dp"):
            own = added(own, swap(own, bit))
            bit *= 2
        return Widen(self.at, self.name, own[0], own[1])


def on_device(
    tokens, images, segment_of_token, image_of_row, attention_in, query_value_bias, attention_out, output_bias,
    feed_in, feed_bias, feed_out, image_weight, image_bias, norm_gain, norm_bias, cotangent,
):
    mp = lax.axis_size("mp")
    slot = lax.axis_index("dp") % SLICES
    owner = lax.axis_index("mp")
    place = jnp.stack([slot, owner]).astype(jnp.int32)
    own_rows, seq, width = tokens.shape
    group_rows = segment_of_token.shape[0]
    patches, image_width = images.shape[1:]
    quarter = attention_in.shape[3]
    units = feed_in.shape[2]
    n_tokens = own_rows * seq
    inward = attention_in.transpose(0, 1, 3, 2)
    image = image_weight.T

    attention_rows = quarter // 4
    feed_rows = units // SLICES
    image_rows = quarter * image_width // width // SLICES // 2

    token_shape = shape((n_tokens, width))
    token_low = shape((n_tokens, width), BF16)
    row_low = shape((own_rows, seq, width), BF16)
    inner_shape = shape((n_tokens, mp * units))
    inner_low = shape((n_tokens, mp * units), BF16)
    padded = -(-patches // 16) * 16
    n_patches = own_rows * padded
    patch_low = shape((n_patches, width), BF16)
    small_shape = shape((8, width))
    attention_grad = shape((2, 4, mp, attention_rows, width), BF16)
    feed_grad = shape((2, 4, mp, feed_rows, width), BF16)
    image_grad = shape((2, 4, mp, image_rows, width), BF16)
    square = pltpu.VMEM((4, width, width), BF16)
    wide = pltpu.VMEM((2, mp, units, width), BF16)
    tall = pltpu.VMEM((width, image_width), BF16)
    token_f32 = pltpu.VMEM((n_tokens, width), F32)
    token_bf16 = pltpu.VMEM((n_tokens, width), BF16)
    dma = pltpu.SemaphoreType.DMA
    matmul = 2 * n_tokens * width * width
    patch_matmul = 2 * n_patches * width * width

    local_order = image_of_row % group_rows
    here = owner * own_rows + jnp.arange(own_rows, dtype=jnp.int32)
    chosen = (local_order[None, :] == here[:, None]).astype(jnp.int32)
    source_row = jnp.sum(chosen * jnp.arange(group_rows, dtype=jnp.int32)[None, :], axis=1)
    picks_in = ((owner - source_row // own_rows) % mp) * own_rows + source_row % own_rows
    mine = (jnp.arange(group_rows, dtype=jnp.int32)[None, :] == here[:, None]).astype(jnp.int32)
    image_row = jnp.sum(mine * local_order[None, :], axis=1)
    picks_out = ((owner - image_row // own_rows) % mp) * own_rows + image_row % own_rows
    segments = jnp.sum(chosen[:, :, None] * segment_of_token[None], axis=1)
    code = jnp.arange(own_rows, dtype=jnp.int32)[:, None] * seq + segments
    code_col = code.reshape(n_tokens, 1)
    code_row = code.reshape(own_rows // 2, 2 * seq)

    text, first, joining, cross, last = call(
        slice_kernel,
        [(place, SMEM)] + [(v, ANY) for v in (inward, attention_out, feed_in, feed_out, image)],
        [
            (shape((2, rows, width), BF16), ANY)
            for rows in (attention_rows, feed_rows, attention_rows, attention_rows + image_rows, feed_rows)
        ],
        [dma((5,))],
        16,
    )
    at = {}

    def step():
        done = lax.optimization_barrier(at)
        at.clear()
        at.update(done)

    flat = jnp.concatenate([query_value_bias.reshape(-1, quarter), feed_bias.reshape(-1, quarter), image_bias[None]])
    rings = {
        name: Ring(at, name, own)
        for name, own in (
            ("text", text), ("first", first), ("joining", joining), ("cross", cross), ("last", last),
            ("bias", flat), ("tokens", tokens), ("cotangent", cotangent),
        )
    }

    def gathered(name):
        parts = rings[name].take()[1:]
        return Widen(at, name, jnp.stack([part[0] for part in parts]), jnp.stack([part[1] for part in parts]))

    def both_ways(name):
        rings[name].up()
        rings[name].down()

    def far(name):
        rings[name].far()

    both_ways("text")
    both_ways("cross")
    both_ways("bias")
    step()
    far("text")
    far("cross")
    far("bias")
    both_ways("first")
    step()
    text_wide, cross_wide = gathered("text"), gathered("cross")
    bias_parts = rings["bias"].take()
    text_wide.one()
    cross_wide.one()
    far("first")
    both_ways("joining")
    step()
    first_wide = gathered("first")
    text_wide.two()
    cross_wide.two()
    first_wide.one()
    far("joining")
    rings["tokens"].up()
    both_ways("last")
    step()
    joining_wide = gathered("joining")
    text_wide.core()
    cross_wide.core()
    first_wide.two()
    joining_wide.one()
    rings["tokens"].down()
    far("last")
    step()

    ordered = jnp.stack(bias_parts)[(owner - jnp.arange(mp)) % mp].astype(F32)
    rows_of = units // quarter
    bias = jnp.concatenate(
        [
            ordered[:, :6].transpose(1, 0, 2).reshape(6, width),
            ordered[:, 6 : 6 + 2 * rows_of].reshape(mp, 2, units).transpose(1, 0, 2).reshape(2 * mp, width),
            ordered[:, 6 + 2 * rows_of].reshape(1, width),
        ]
    )
    params = jnp.stack([output_bias, norm_gain, norm_bias], axis=1).astype(F32).reshape(-1, width)

    attention_pieces = [text_wide.take(), None, cross_wide.take()]
    feed_pieces = [None, None]

    def attention_ins(layer):
        return [(inward, ANY), (attention_out, ANY)] + [(piece, ANY) for piece in attention_pieces[layer]]

    def feed_ins(layer):
        return [(feed_in, ANY), (feed_out, ANY)] + [(piece, ANY) for piece in feed_pieces[layer]]

    def self_forward(layer, norm, rows, pick):
        return call(
            partial(self_forward_kernel, pick, layer, norm, 0),
            [(place, SMEM), (picks_in, SMEM), (rows, VMEM)]
            + attention_ins(layer)
            + [(bias, VMEM), (params, VMEM), (code_col, VMEM), (code_row, VMEM)],
            [(token_shape, VMEM), (token_low, VMEM), (token_shape, VMEM)] + [(token_low, VMEM)] * 4,
            [square, dma((4,))] + ([token_f32] if pick else []),
            32,
        )

    def self_backward(layer, norm, grad, kept, leave, spot, rows, held):
        _, low, pre, query, keys, value, context = kept
        grads = shape((2, 4, mp, rows, width), BF16)
        n_before = 8 + 2 + 8 + 3
        return call(
            partial(self_backward_kernel, leave, layer, norm, 0, spot, len(held)),
            [(place, SMEM)]
            + [(v, VMEM) for v in (grad, low, pre, query, keys, value, context)]
            + attention_ins(layer)
            + [(params, VMEM), (code_col, VMEM), (code_row, VMEM)]
            + [(v, ANY) for v in held],
            [(row_low if leave else token_shape, VMEM), (small_shape, VMEM)] + [(grads, ANY)] * 2,
            [square, square] + [token_bf16] * 4 + [dma((4,)), dma],
            40,
            {n_before + i: 2 + i for i in range(len(held))},
        )

    def feed_forward(layer, norm, rows, leave):
        return call(
            partial(feed_forward_kernel, leave, layer, norm, 0),
            [(place, SMEM), (rows, VMEM)] + feed_ins(layer) + [(bias, VMEM), (params, VMEM)],
            [(row_low if leave else token_shape, VMEM), (token_low, VMEM), (token_shape, VMEM)]
            + [(inner_shape, VMEM), (inner_low, VMEM)],
            [wide, dma((2, mp))],
            40,
        )

    def feed_backward(layer, norm, grad, kept, pick):
        _, low, pre, slope, active = kept
        return call(
            partial(feed_backward_kernel, pick, layer, norm, 0),
            [(place, SMEM), (picks_in, SMEM)]
            + [(v, VMEM) for v in (grad, low, pre, slope, active)]
            + feed_ins(layer)
            + [(params, VMEM)],
            [(token_shape, VMEM), (small_shape, VMEM)] + [(feed_grad, ANY)] * 2,
            [wide, wide, dma((2, mp)), dma] + ([token_f32] if pick else []),
            48,
        )

    def pick_rows(parts):
        rows = jnp.stack(parts).reshape(mp * own_rows, seq, width)
        return call(
            pick_kernel, [(picks_out, SMEM), (rows, VMEM)], [(shape((own_rows, seq, width)), VMEM)], [], 16
        )[0]

    patch_rows = jnp.pad(images, ((0, 0), (0, padded - patches), (0, 0))).reshape(n_patches, image_width)
    joining_wide.two()
    first_wide.core()
    last_wide = gathered("last")
    last_wide.one()
    far("tokens")
    at["patches"] = call(
        partial(image_forward_kernel, 2, 0, attention_rows, image_rows),
        [(place, SMEM), (patch_rows, VMEM), (image, ANY)] + attention_ins(2) + [(bias, VMEM)],
        [(patch_low, VMEM)] * 3,
        [square, tall, dma((4,)), dma],
        40,
    )
    step()

    feed_pieces[0] = first_wide.take()
    joining_wide.core()
    last_wide.two()
    rings["cotangent"].up()
    rows_in = jnp.stack(rings["tokens"].take()).reshape(mp * own_rows, seq, width)
    text_attention = self_forward(0, 0, rows_in, True)
    text_feed = feed_forward(0, 1, text_attention[0], False)
    at["stream"] = text_feed[0]
    step()

    attention_pieces[1] = joining_wide.take()
    last_wide.core()
    rings["cotangent"].down()
    joining_attention = self_forward(1, 2, at.pop("stream"), False)
    at["stream"] = joining_attention[0]
    step()

    feed_pieces[1] = last_wide.take()
    far("cotangent")
    projected, image_keys, image_value = at.pop("patches")
    cross_attention = call(
        partial(cross_forward_kernel, 2, 3, 0, seq, patches),
        [(place, SMEM), (at.pop("stream"), VMEM), (image_keys, VMEM), (image_value, VMEM)]
        + attention_ins(2)
        + [(bias, VMEM), (params, VMEM)],
        [(token_shape, VMEM), (token_low, VMEM), (token_shape, VMEM), (token_shape, VMEM), (token_low, VMEM)],
        [square, token_f32, dma((4,))],
        32,
    )
    joining_feed = feed_forward(1, 4, cross_attention[0], True)
    mixed_ring = Ring(at, "mixed", joining_feed[0])
    step()

    rows_grad = jnp.stack(rings["cotangent"].take()).reshape(mp * own_rows, seq, width)
    grad, small_joining_feed, keep, send = feed_backward(1, 4, rows_grad, joining_feed, True)
    at["grad"] = grad
    last_grads = Reduce(at, "last", keep, send)
    step()

    last_grads.core()
    mixed_ring.up()
    middle_grad = shape((2, 4, mp, 2 * attention_rows, width), BF16)
    grad, small_cross, keep, send, grad_keys, grad_value = call(
        partial(cross_backward_kernel, 2, 3, 0, 0, seq, patches),
        [(place, SMEM), (at.pop("grad"), VMEM)]
        + [(cross_attention[i], VMEM) for i in (1, 2, 3, 4)]
        + [(image_keys, VMEM), (image_value, VMEM), (projected, VMEM)]
        + attention_ins(2)
        + [(params, VMEM)],
        [(token_shape, VMEM), (small_shape, VMEM)] + [(middle_grad, ANY)] * 2 + [(patch_low, VMEM)] * 2,
        [square, square, token_f32, token_f32, dma((4,)), dma],
        56,
    )
    at["grad"] = grad
    at["patch grads"] = grad_keys, grad_value
    step()

    last_grads.one()
    mixed_ring.down()
    grad, small_joining, keep, send = self_backward(
        1, 2, at.pop("grad"), joining_attention, False, attention_rows, 2 * attention_rows, (keep, send)
    )
    at["grad"] = grad
    middle_grads = Reduce(at, "middle", keep, send)
    step()

    last_grads.two()
    middle_grads.core()
    mixed_ring.far()
    grad, small_text_feed, keep, send = feed_backward(0, 1, at.pop("grad"), text_feed, False)
    at["grad"] = grad
    first_grads = Reduce(at, "first", keep, send)
    step()

    mixed_out = pick_rows(mixed_ring.take())
    last_grads.far()
    middle_grads.one()
    first_grads.core()
    rows_back, small_text, keep, send = self_backward(
        0, 0, at.pop("grad"), text_attention, True, 0, attention_rows + image_rows, ()
    )
    back_ring = Ring(at, "back", rows_back)
    step()

    last_grads.near()
    middle_grads.two()
    first_grads.one()
    back_ring.up()
    grad_keys, grad_value = at.pop("patch grads")
    grad_images, small_image, keep, send = call(
        partial(image_backward_kernel, 2, 0, attention_rows, image_rows, attention_rows, 2),
        [(place, SMEM), (patch_rows, VMEM), (grad_keys, VMEM), (grad_value, VMEM), (image, ANY)]
        + attention_ins(2)
        + [(keep, ANY), (send, ANY)],
        [(shape(images.shape), VMEM), (small_shape, VMEM)] + [(shape(keep.shape, BF16), ANY)] * 2,
        [square, tall, tall, pltpu.VMEM((n_patches, width), BF16), dma((4,)), dma, dma],
        48,
        {15: 2, 16: 3},
    )
    text_grads = Reduce(at, "text", keep, send)
    at["small"] = jnp.concatenate(
        [small_text, small_text_feed, small_joining, small_cross, small_joining_feed, small_image]
    )
    step()

    first_grads.two()
    text_grads.core()
    middle_grads.far()
    back_ring.down()
    last_result = last_grads.widen()
    step()

    text_grads.one()
    last_result.one()
    middle_grads.near()
    back_ring.far()
    step()

    grad_tokens = pick_rows(back_ring.take())
    text_grads.two()
    last_result.two()
    first_grads.far()
    middle_result = middle_grads.widen()
    middle_result.one()
    at["small"] = at["small"] + swap(at["small"], 1)
    step()

    last_result.core()
    middle_result.two()
    first_grads.near()
    text_grads.far()
    at["small"] = at["small"] + swap(at["small"], 2)
    step()

    middle_result.core()
    first_result = first_grads.widen()
    first_result.one()
    text_grads.near()
    at["small"] = at["small"] + swap(at["small"], 4)
    step()

    first_result.two()
    text_result = text_grads.widen()
    text_result.one()
    at["small"] = at["small"] + swap_owner(at["small"], 1)
    step()

    first_result.core()
    text_result.two()
    smalls = at["small"] + swap_owner(at["small"], 2)
    bit = SLICES
    while bit < lax.axis_size("dp"):
        smalls = smalls + swap(smalls, bit)
        bit *= 2
    at["small"] = smalls
    step()

    text_result.core()

    whole_shapes = {
        "attention_in": shape(inward.shape),
        "attention_out": shape(attention_out.shape),
        "feed_in": shape(feed_in.shape),
        "feed_out": shape(feed_out.shape),
        "image": shape(image.shape),
    }
    block_of = {"attention": (4, quarter, width), "feed": (2, units, width), "image": (quarter, image_width)}
    names_of = {"attention": ["attention_in", "attention_out"], "feed": ["feed_in", "feed_out"], "image": ["image"]}
    written = {}

    def write_out(result, *blocks):
        names = list(dict.fromkeys(name for kind, _, _ in blocks for name in names_of[kind]))
        names = [name for name in names if name in written] + [name for name in names if name not in written]
        held = [name for name in names if name in written]
        scratch = [pltpu.VMEM(block_of[kind], form) for kind, _, _ in blocks for form in (BF16, F32)]
        results = call(
            partial(finish_kernel, blocks, quarter, names, len(held)),
            [(place, SMEM)] + [(v, ANY) for v in result.take()] + [(written[name], ANY) for name in held],
            [(whole_shapes[name], ANY) for name in names],
            scratch + [dma((len(blocks),)), dma((len(blocks),))],
            40,
            {9 + i: i for i in range(len(held))},
        )
        written.update(zip(names, results))

    write_out(last_result, ("feed", 0, 1))
    write_out(middle_result, ("attention", 0, 2), ("attention", attention_rows, 1))
    write_out(first_result, ("feed", 0, 0))
    write_out(text_result, ("attention", 0, 0), ("image", attention_rows, 0))

    smalls = at["small"].reshape(6, 8, width)

    def own_part(values):
        return lax.dynamic_slice_in_dim(values, owner * quarter, quarter, axis=values.ndim - 1)

    grad_query_value_bias = own_part(jnp.stack([smalls[i, 3:5] for i in (0, 2, 3)]))
    grad_feed_bias = jnp.stack([smalls[i, 3 : 3 + mp].reshape(-1) for i in (1, 4)])
    grad_feed_bias = lax.dynamic_slice_in_dim(grad_feed_bias, owner * units, units, axis=1)
    return (
        mixed_out,
        grad_tokens,
        grad_images,
        written["attention_in"].transpose(0, 1, 3, 2),
        grad_query_value_bias,
        written["attention_out"],
        smalls[:5, 2],
        written["feed_in"],
        grad_feed_bias,
        written["feed_out"],
        written["image"].T,
        own_part(smalls[5, 0]),
        smalls[:5, 0],
        smalls[:5, 1],
    )


def solution(mesh):
    rows = P(("dp", "mp"), None, None)
    return jax.shard_map(
        on_device,
        mesh=mesh,
        in_specs=(
            rows,
            rows,
            P("dp", None),
            P("dp"),
            P(None, None, None, "mp"),
            P(None, None, "mp"),
            P(None, "mp", None),
            P(),
            P(None, None, "mp"),
            P(None, "mp"),
            P(None, "mp", None),
            P(None, "mp"),
            P("mp"),
            P(),
            P(),
            rows,
        ),
        out_specs=(
            rows,
            rows,
            rows,
            P(None, None, None, "mp"),
            P(None, None, "mp"),
            P(None, "mp", None),
            P(),
            P(None, None, "mp"),
            P(None, "mp"),
            P(None, "mp", None),
            P(None, "mp"),
            P("mp"),
            P(),
            P(),
        ),
        check_vma=False,
    )
```

```python
from functools import partial

import jax
import jax.numpy as jnp
from jax import lax
from jax.experimental import pallas as pl
from jax.experimental.pallas import tpu as pltpu
from jax.sharding import PartitionSpec as P

HEAD_DIM = 64
STACK = 4 * HEAD_DIM
TOGETHER = 6
SLICES = 8
EPSILON = 1e-06
BLOCKED = -1000000000.0
SCALE = HEAD_DIM ** (-0.5)
DISTANCES = ((0, 2, 4, 6), (0, 4, 2, 6))
ATTENTION, FEED, IMAGE, ATTENTION_IN, ATTENTION_OUT, FEED_IN, FEED_OUT = range(7)
SMALL, TOKENS, COTANGENT = "small", "tokens", "cotangent"
F32 = jnp.float32
BF16 = jnp.bfloat16

ANY = pl.BlockSpec(memory_space=pl.ANY)
VMEM = pl.BlockSpec(memory_space=pltpu.VMEM)
SMEM = pl.BlockSpec(memory_space=pltpu.SMEM)


def swap(values, bit):
    count = lax.axis_size("dp")
    return lax.ppermute(values, "dp", [(i, i ^ bit) for i in range(count)])


def pass_on(values, way=1):
    count = lax.axis_size("mp")
    return lax.ppermute(values, "mp", [(i, (i + way) % count) for i in range(count)])


def swap_owner(values, bit):
    count = lax.axis_size("mp")
    return lax.ppermute(values, "mp", [(i, i ^ bit) for i in range(count)])


def added(*terms):
    total = terms[0].astype(F32)
    for term in terms[1:]:
        total = total + term
    return total.astype(BF16)


def dot_nn(left, right):
    return lax.dot_general(left, right, (((1,), (0,)), ((), ())), preferred_element_type=F32)


def dot_nt(left, right):
    return lax.dot_general(left, right, (((1,), (1,)), ((), ())), preferred_element_type=F32)


def dot_tn(left, right):
    return lax.dot_general(left, right, (((0,), (0,)), ((), ())), preferred_element_type=F32)


def start(source, target, sem):
    pltpu.make_async_copy(source, target, sem).start()


def finish(whole, sem):
    pltpu.make_async_copy(whole, whole, sem).wait()


def aligned(first, count, step=16):
    return pl.ds(pl.multiple_of(first, step), count)


def each_slice(place, first_step, mp):
    for core in range(2):
        for half in range(2):
            for entry in range(4):
                slot = place[0] ^ (core ^ DISTANCES[half][entry])
                for step in range(first_step, mp):
                    yield core, half, entry, step, slot, (place[1] + mp - step) % mp


def piece_of(pieces, core, half, entry):
    if len(pieces) == 2:
        return pieces[core].at[half, entry]
    return pieces[2 * core + entry // 2].at[half, entry % 2]


def attention_spot(whole, quarter, half, slot, owner):
    span = 4 * quarter // SLICES
    count = quarter // span
    row = owner * quarter + (slot % count) * span + half * (span // 2)
    return whole.at[slot // count, aligned(row, span // 2)]


def load_attention(place, own, pieces, offset, layer, whole, sems):
    mp = pieces[0].shape[2] + 1
    quarter = whole.shape[1] // mp
    rows = quarter // 4
    for mat in range(4):
        source = own[0].at[layer, mat] if mat < 3 else own[1].at[layer]
        start(source, whole.at[mat, aligned(place[1] * quarter, quarter)], sems.at[mat])
    for core, half, entry, step, slot, owner in each_slice(place, 1, mp):
        start(
            piece_of(pieces, core, half, entry).at[step - 1, pl.ds(offset, rows)],
            attention_spot(whole, quarter, half, slot, owner),
            sems.at[slot // 2],
        )


def store_attention(place, whole, outs, offset, sem):
    mp = outs[0].shape[2]
    quarter = whole.shape[1] // mp
    for core, half, entry, step, slot, owner in each_slice(place, 0, mp):
        start(
            attention_spot(whole, quarter, half, slot, owner),
            outs[core].at[half, entry, step, pl.ds(offset, quarter // 4)],
            sem,
        )


def feed_spot(whole, half, slot, step):
    span = whole.shape[2] // SLICES
    return whole.at[half, step, aligned(slot * span, span)]


def load_feed(place, own, pieces, offset, layer, half, step, whole, sems):
    rows = whole.shape[2] // SLICES
    if step == 0:
        start(own[half].at[layer], whole.at[half, 0], sems.at[half, 0])
        return
    for core in range(2):
        for entry in range(4):
            slot = place[0] ^ (core ^ DISTANCES[half][entry])
            start(
                piece_of(pieces, core, half, entry).at[step - 1, pl.ds(offset, rows)],
                feed_spot(whole, half, slot, step),
                sems.at[half, step],
            )


def store_feed(place, whole, outs, half, step, sem):
    for core in range(2):
        for entry in range(4):
            slot = place[0] ^ (core ^ DISTANCES[half][entry])
            start(feed_spot(whole, half, slot, step), outs[core].at[half, entry, step], sem)


def image_copies(whole, piece, quarter, half, slot, owner, sem, inward):
    rows, width = piece.shape
    span = 2 * rows
    beyond = whole.shape[1] - width
    blocks = width // beyond
    plain = quarter // span
    base = owner * quarter + half * rows

    def move(inner, outer):
        start(inner, outer, sem) if inward else start(outer, inner, sem)

    @pl.when(slot < plain)
    def _():
        move(piece, whole.at[aligned(base + slot * span, rows), pl.ds(0, width)])

    @pl.when(slot >= plain)
    def _():
        for block in range(blocks):
            row = base + block * (quarter // blocks) + (slot - plain) * span
            move(
                piece.at[:, pl.ds(block * beyond, beyond)],
                whole.at[aligned(row, rows), pl.ds(width, beyond)],
            )


def load_image(place, own, pieces, offset, rows, whole, sem):
    mp = pieces[0].shape[2] + 1
    quarter = whole.shape[0] // mp
    start(own, whole.at[aligned(place[1] * quarter, quarter)], sem)
    for core, half, entry, step, slot, owner in each_slice(place, 1, mp):
        piece = piece_of(pieces, core, half, entry).at[step - 1, pl.ds(offset, rows)]
        image_copies(whole, piece, quarter, half, slot, owner, sem, True)


def store_image(place, whole, outs, offset, rows, sem):
    mp = outs[0].shape[2]
    quarter = whole.shape[0] // mp
    for core, half, entry, step, slot, owner in each_slice(place, 0, mp):
        piece = outs[core].at[half, entry, step, pl.ds(offset, rows)]
        image_copies(whole, piece, quarter, half, slot, owner, sem, False)


def norm_rows(values, gain_row, shift_row):
    center = values - jnp.mean(values, axis=-1, keepdims=True)
    moment = jnp.mean(center * center, axis=-1, keepdims=True)
    return center * lax.rsqrt(moment + EPSILON) * gain_row + shift_row


def norm_back(pre_norm, gain_row, grad_out, small):
    center = pre_norm - jnp.mean(pre_norm, axis=-1, keepdims=True)
    scale = lax.rsqrt(jnp.mean(center * center, axis=-1, keepdims=True) + EPSILON)
    normal = center * scale
    lifted = grad_out * gain_row
    grad_pre = scale * (
        lifted
        - jnp.mean(lifted, axis=-1, keepdims=True)
        - normal * jnp.mean(lifted * normal, axis=-1, keepdims=True)
    )
    small[...] = jnp.zeros_like(small)
    small[0:1] = jnp.sum(grad_out * normal, axis=0, keepdims=True)
    small[1:2] = jnp.sum(grad_out, axis=0, keepdims=True)
    small[2:3] = jnp.sum(grad_pre, axis=0, keepdims=True)
    return grad_pre


def column_total(values):
    return jnp.sum(values.astype(F32), axis=0, keepdims=True)


def spread_heads(values):
    lane = lax.broadcasted_iota(jnp.int32, (1, values.shape[1]), 1)
    parts = []
    for first in range(0, values.shape[1], HEAD_DIM):
        mask = ((lane >= first) & (lane < first + HEAD_DIM)).astype(F32).astype(values.dtype)
        parts.append(values * mask)
    return jnp.concatenate(parts, axis=0)


def pick_heads(values):
    lane = lax.broadcasted_iota(jnp.int32, (1, values.shape[1]), 1)
    rows = values.shape[0] * HEAD_DIM // values.shape[1]
    picked = values[:rows]
    for head in range(1, values.shape[1] // HEAD_DIM):
        picked = jnp.where(lane >= head * HEAD_DIM, values[head * rows : (head + 1) * rows], picked)
    return picked


def softmax(scores):
    raised = jnp.exp(scores - jnp.max(scores, axis=-1, keepdims=True))
    return raised * (1.0 / jnp.sum(raised, axis=-1, keepdims=True))


def score_back(weights, grad_weights):
    along = weights * grad_weights
    return (along - weights * jnp.sum(along, axis=-1, keepdims=True)).astype(BF16)


def attention_units(count, row_size, place_size, width):
    units = []
    for number in range(count):
        rows = slice(number * row_size, (number + 1) * row_size)
        places = slice(number * place_size, (number + 1) * place_size)
        units += [(number, rows, places, slice(first, first + STACK)) for first in range(0, width, STACK)]
    return [units[first : first + TOGETHER] for first in range(0, len(units), TOGETHER)]


def attend_forward(units, allowed, query, keys, value, context):
    for group in units:
        scores = [dot_nt(spread_heads(query[rows, lanes]).astype(BF16), keys[at, lanes]) for _, rows, at, lanes in group]
        weights = [
            softmax(jnp.where(allowed(unit[0]), score * SCALE, BLOCKED)).astype(BF16)
            for unit, score in zip(group, scores)
        ]
        for (_, rows, at, lanes), weight in zip(group, weights):
            context[rows, lanes] = pick_heads(dot_nn(weight, value[at, lanes])).astype(context.dtype)


def attend_backward(units, allowed, query, keys, value, grad_context, grad_query, grad_keys, grad_value):
    for group in units:
        queries = [spread_heads(query[rows, lanes]).astype(BF16) for _, rows, _, lanes in group]
        contexts = [spread_heads(grad_context[rows, lanes]).astype(BF16) for _, rows, _, lanes in group]
        scores = [dot_nt(one, keys[at, lanes]) for one, (_, _, at, lanes) in zip(queries, group)]
        grad_weights = [dot_nt(one, value[at, lanes]) for one, (_, _, at, lanes) in zip(contexts, group)]
        weights = [
            softmax(jnp.where(allowed(unit[0]), score * SCALE, BLOCKED)) for unit, score in zip(group, scores)
        ]
        grad_scores = [score_back(one, other) for one, other in zip(weights, grad_weights)]
        for weight, one, (_, _, at, lanes) in zip(weights, contexts, group):
            grad_value[at, lanes] = dot_tn(weight.astype(BF16), one).astype(BF16)
        for grad_score, one, (_, _, at, lanes) in zip(grad_scores, queries, group):
            grad_keys[at, lanes] = (dot_tn(grad_score, one) * SCALE).astype(BF16)
        for grad_score, (_, rows, at, lanes) in zip(grad_scores, group):
            mixed = pick_heads(dot_nn(grad_score, keys[at, lanes])) * SCALE
            grad_query[rows, lanes] = mixed.astype(grad_query.dtype)


def same_segment(code_col, code_row):
    size = code_row.shape[1]

    def allowed(group):
        column = code_col[group * size : (group + 1) * size]
        return jnp.concatenate([column] * (STACK // HEAD_DIM), axis=0) == code_row[group : group + 1]

    return allowed


def real_patch(size, patches):
    column = lax.broadcasted_iota(jnp.int32, (1, size), 1)
    return lambda row: column < patches


def pick_copies(picks, parts, target, sem):
    size = parts[0].shape[0]
    for row in range(target.shape[0]):
        for number, part in enumerate(parts):

            @pl.when(picks[row] // size == number)
            def _():
                start(part.at[picks[row] % size], target.at[row], sem)


def flat_rows(rows_ref, target):
    seq = rows_ref.shape[1]
    for row in range(rows_ref.shape[0]):
        target[row * seq : (row + 1) * seq] = rows_ref[row].astype(target.dtype)


def leave_rows(values, target):
    seq = target.shape[1]
    for row in range(target.shape[0]):
        target[row] = values[row * seq : (row + 1) * seq].astype(target.dtype)


def slice_kernel(place, biases, inward, outward, feed_in, feed_out, image, first, second, third, sems):
    slot = place[0]
    quarter, width = inward.shape[2:]
    span = 4 * quarter // SLICES
    count = quarter // span
    rows = span // 2
    feed_rows = feed_in.shape[1] // SLICES
    bias_rows = biases.shape[1]
    image_rows = first.shape[1] - 2 * rows - bias_rows
    weights = first.at[:, pl.ds(0, 2 * rows + image_rows)]
    first[:, 2 * rows + image_rows :] = biases[...]

    def attention(layer, target, offset, sem):
        for half in range(2):
            row = (slot % count) * span + half * rows
            spot = target.at[half, pl.ds(offset, rows)]

            @pl.when(slot < 3 * count)
            def _():
                start(inward.at[layer, slot // count, aligned(row, rows)], spot, sem)

            @pl.when(slot >= 3 * count)
            def _():
                start(outward.at[layer, aligned(row, rows)], spot, sem)

    def feed(layer, target, offset, sem):
        for half, source in enumerate((feed_in, feed_out)):
            spot = target.at[half, pl.ds(offset, feed_rows)]
            start(source.at[layer, aligned(slot * feed_rows, feed_rows)], spot, sem)

    attention(0, first, 0, sems.at[0])
    attention(2, first, rows, sems.at[0])
    for half in range(2):
        spot = first.at[half, pl.ds(2 * rows, image_rows)]
        image_copies(image, spot, quarter, half, slot, 0, sems.at[0], False)
    feed(0, second, 0, sems.at[1])
    attention(1, second, feed_rows, sems.at[1])
    feed(1, third, 0, sems.at[2])
    for number, target in enumerate((weights, second, third)):
        finish(target, sems.at[number])


def self_forward_kernel(
    layer, norm, offset, n_parts, n_pieces, place, picks, *refs,
):
    parts, (inward, outward), refs = refs[:n_parts], refs[n_parts : n_parts + 2], refs[n_parts + 2 :]
    pieces, refs = refs[:n_pieces], refs[n_pieces:]
    bias, params, code_col, code_row, out, low, pre, query, keys, value, context, kept, whole, sems, out_sem, *held = refs
    if held:
        pick_copies(picks, parts, held[0], held[2])
    load_attention(place, (inward, outward), pieces, offset, layer, whole, sems)
    if held:
        finish(held[0], held[2])
        flat_rows(held[0], held[1])
        stream = held[1][...]
    else:
        stream = parts[0][...]
    hb = stream.astype(BF16)
    low[...] = hb
    finish(whole.at[0], sems.at[0])
    query[...] = (dot_nt(hb, whole[0]) + bias[2 * layer : 2 * layer + 1]).astype(BF16)
    finish(whole.at[1], sems.at[1])
    keys[...] = dot_nt(hb, whole[1]).astype(BF16)
    finish(whole.at[2], sems.at[2])
    value[...] = (dot_nt(hb, whole[2]) + bias[2 * layer + 1 : 2 * layer + 2]).astype(BF16)
    groups, size = code_row.shape
    units = attention_units(groups, size, size, hb.shape[1])
    attend_forward(units, same_segment(code_col, code_row), query, keys, value, context)
    finish(whole.at[3], sems.at[3])
    start(whole, kept, out_sem)
    total = dot_nn(context[...], whole[3]) + params[3 * norm : 3 * norm + 1] + stream
    pre[...] = total
    out[...] = norm_rows(total, params[3 * norm + 1 : 3 * norm + 2], params[3 * norm + 2 : 3 * norm + 3])
    finish(whole, out_sem)


def load_kept(kept, whole, sems, order):
    for mat in order:
        start(kept.at[mat], whole.at[mat], sems.at[mat])


def self_backward_kernel(
    leave, norm, spot, n_held, place, grad, low, pre, query, keys, value, context, kept, params, code_col, code_row, *refs,
):
    out, small, keep, send, whole, grads, grad_context, grad_query, grad_keys, grad_value, sems, out_sem = refs[n_held:]
    load_kept(kept, whole, sems, (3, 0, 1, 2))
    grad_pre = norm_back(pre[...], params[3 * norm + 1 : 3 * norm + 2], grad[...], small)
    branch = grad_pre.astype(BF16)
    finish(whole.at[3], sems.at[3])
    grad_context[...] = dot_nt(branch, whole[3]).astype(BF16)
    grads[3] = dot_tn(context[...], branch).astype(BF16)
    groups, size = code_row.shape
    units = attention_units(groups, size, size, branch.shape[1])
    attend_backward(
        units, same_segment(code_col, code_row), query, keys, value, grad_context, grad_query, grad_keys, grad_value
    )
    hb = low[...]
    grads[0] = dot_tn(grad_query[...], hb).astype(BF16)
    grads[1] = dot_tn(grad_keys[...], hb).astype(BF16)
    grads[2] = dot_tn(grad_value[...], hb).astype(BF16)
    store_attention(place, grads, (keep, send), spot, out_sem)
    small[3:4] = column_total(grad_query[...])
    small[4:5] = column_total(grad_value[...])
    total = grad_pre
    for mat, part in enumerate((grad_query, grad_keys, grad_value)):
        finish(whole.at[mat], sems.at[mat])
        total = total + dot_nn(part[...], whole[mat])
    if leave:
        leave_rows(total, out)
    else:
        out[...] = total
    finish(grads, out_sem)


def feed_forward_kernel(
    layer, norm, offset, n_pieces, place, rows_ref, first_weight, second_weight, *refs,
):
    pieces, refs = refs[:n_pieces], refs[n_pieces:]
    bias, params, out, low, pre, slope_out, active_out, kept, whole, slope, active, sems, out_sem = refs
    parts = whole.shape[1]
    for step in range(parts):
        for half in range(2):
            load_feed(place, (first_weight, second_weight), pieces, offset, layer, half, step, whole, sems)
    stream = rows_ref[...]
    hb = stream.astype(BF16)
    low[...] = hb
    total = params[3 * norm : 3 * norm + 1] + stream
    for step in range(parts):
        row = 6 + layer * parts + (place[1] + parts - step) % parts
        finish(whole.at[0, step], sems.at[0, step])
        units = dot_nn(hb, whole[0, step]) + bias[pl.ds(row, 1)]
        share = 0.5 * (1.0 + lax.erf(units * (2.0 ** -0.5)))
        slope[step] = share + units * jnp.exp(-0.5 * units * units) * 0.3989422804014327
        start(slope.at[step], slope_out.at[step], out_sem)
        gated = (units * share).astype(BF16)
        active[step] = gated
        start(active.at[step], active_out.at[step], out_sem)
        start(whole.at[0, step], kept.at[0, step], out_sem)
        finish(whole.at[1, step], sems.at[1, step])
        start(whole.at[1, step], kept.at[1, step], out_sem)
        total = total + dot_nn(gated, whole[1, step])
    pre[...] = total
    out[...] = norm_rows(total, params[3 * norm + 1 : 3 * norm + 2], params[3 * norm + 2 : 3 * norm + 3])
    finish(slope, out_sem)
    finish(active, out_sem)
    finish(whole, out_sem)


def feed_backward_kernel(
    norm, place, grad_in, low_in, pre_in, slope_in, active_in, kept, params,
    out, small, keep, send, whole, grads, grad, low, pre, slope, active, row_sems, sems, out_sem,
):
    parts = whole.shape[1]
    start(grad_in, grad, row_sems.at[0])
    start(pre_in, pre, row_sems.at[1])
    for step in range(parts):
        start(active_in.at[step], active.at[step], row_sems.at[3 + step])
        start(kept.at[1, step], whole.at[1, step], sems.at[1, step])
        start(slope_in.at[step], slope.at[step], row_sems.at[3 + parts + step])
        if step == 0:
            start(low_in, low, row_sems.at[2])
        start(kept.at[0, step], whole.at[0, step], sems.at[0, step])
    finish(grad, row_sems.at[0])
    finish(pre, row_sems.at[1])
    grad_pre = norm_back(pre[...], params[3 * norm + 1 : 3 * norm + 2], grad[...], small)
    branch = grad_pre.astype(BF16)
    total = grad_pre
    for step in range(parts):
        finish(active.at[step], row_sems.at[3 + step])
        grads[1, step] = dot_tn(active[step], branch).astype(BF16)
        store_feed(place, grads, (keep, send), 1, step, out_sem)
        finish(whole.at[1, step], sems.at[1, step])
        finish(slope.at[step], row_sems.at[3 + parts + step])
        grad_units = (dot_nt(branch, whole[1, step]) * slope[step]).astype(BF16)
        if step == 0:
            finish(low, row_sems.at[2])
        grads[0, step] = dot_tn(low[...], grad_units).astype(BF16)
        store_feed(place, grads, (keep, send), 0, step, out_sem)
        small[pl.ds(3 + (place[1] + parts - step) % parts, 1)] = column_total(grad_units)
        finish(whole.at[0, step], sems.at[0, step])
        total = total + dot_nt(grad_units, whole[0, step])
    out[...] = total
    finish(grads, out_sem)


def feed_both_kernel(
    layer, norm, offset, n_parts, n_pieces, place, picks, rows_ref, first_weight, second_weight, *refs,
):
    arrived, pieces, refs = refs[:n_parts], refs[n_parts : n_parts + n_pieces], refs[n_parts + n_pieces :]
    bias, params, mixed, out, small, keep, send, whole, grads, slope, active, low, pre, grad, held, sems, row_sem, out_sem = refs
    parts = whole.shape[1]
    for step in range(parts):
        for half in range(2):
            load_feed(place, (first_weight, second_weight), pieces, offset, layer, half, step, whole, sems)
    pick_copies(picks, arrived, held, row_sem)
    stream = rows_ref[...]
    low[...] = stream.astype(BF16)
    total = params[3 * norm : 3 * norm + 1] + stream
    for step in range(parts):
        row = 6 + layer * parts + (place[1] + parts - step) % parts
        finish(whole.at[0, step], sems.at[0, step])
        units = dot_nn(low[...], whole[0, step]) + bias[pl.ds(row, 1)]
        share = 0.5 * (1.0 + lax.erf(units * (2.0 ** -0.5)))
        slope[step] = share + units * jnp.exp(-0.5 * units * units) * 0.3989422804014327
        gated = (units * share).astype(BF16)
        active[step] = gated
        finish(whole.at[1, step], sems.at[1, step])
        total = total + dot_nn(gated, whole[1, step])
    pre[...] = total
    gain, shift = params[3 * norm + 1 : 3 * norm + 2], params[3 * norm + 2 : 3 * norm + 3]
    leave_rows(norm_rows(total, gain, shift), mixed)
    finish(held, row_sem)
    flat_rows(held, grad)
    grad_pre = norm_back(pre[...], gain, grad[...], small)
    branch = grad_pre.astype(BF16)
    total = grad_pre
    for step in range(parts):
        grads[1, step] = dot_tn(active[step], branch).astype(BF16)
        store_feed(place, grads, (keep, send), 1, step, out_sem)
        grad_units = (dot_nt(branch, whole[1, step]) * slope[step]).astype(BF16)
        grads[0, step] = dot_tn(low[...], grad_units).astype(BF16)
        store_feed(place, grads, (keep, send), 0, step, out_sem)
        small[pl.ds(3 + (place[1] + parts - step) % parts, 1)] = column_total(grad_units)
        total = total + dot_nt(grad_units, whole[0, step])
    out[...] = total
    finish(grads, out_sem)


def finish_all(whole, sems):
    for mat in range(whole.shape[0]):
        finish(whole.at[mat], sems.at[mat])


def image_forward_kernel(
    layer, offset, image_offset, image_rows, n_pieces, place, images, image, inward, outward, *refs,
):
    pieces, refs = refs[:n_pieces], refs[n_pieces:]
    bias, projected, keys, value, kept_image, whole, whole_image, sems, image_sem, out_sem = refs
    load_image(place, image, pieces, image_offset, image_rows, whole_image, image_sem)
    load_attention(place, (inward, outward), pieces, offset, layer, whole, sems)
    finish(whole_image, image_sem)
    start(whole_image, kept_image, out_sem)
    size = images.shape[0] // 4
    last = bias.shape[0] - 1
    for first in range(0, images.shape[0], size):
        rows = slice(first, first + size)
        source = (dot_nt(images[rows], whole_image[...]) + bias[last : last + 1]).astype(BF16)
        projected[rows] = source
        if first == 0:
            finish_all(whole, sems)
        keys[rows] = dot_nt(source, whole[1]).astype(BF16)
        value[rows] = (dot_nt(source, whole[2]) + bias[2 * layer + 1 : 2 * layer + 2]).astype(BF16)
    finish(whole_image, out_sem)


def cross_forward_kernel(
    layer, norm, offset, seq, patches, n_pieces, place, rows_ref, keys, value, inward, outward, *refs,
):
    pieces, refs = refs[:n_pieces], refs[n_pieces:]
    bias, params, out, low, pre, query, context, kept, whole, mixed, sems, out_sem = refs
    load_attention(place, (inward, outward), pieces, offset, layer, whole, sems)
    stream = rows_ref[...]
    hb = stream.astype(BF16)
    low[...] = hb
    finish_all(whole, sems)
    start(whole, kept, out_sem)
    query[...] = (dot_nt(hb, whole[0]) + bias[2 * layer : 2 * layer + 1]).astype(BF16).astype(F32)
    count = stream.shape[0] // seq
    size = keys.shape[0] // count
    units = attention_units(count, seq, size, hb.shape[1])
    attend_forward(units, real_patch(size, patches), query, keys, value, mixed)
    context[...] = mixed[...].astype(BF16)
    total = dot_nn(context[...], whole[3]) + params[3 * norm : 3 * norm + 1] + stream
    pre[...] = total
    out[...] = norm_rows(total, params[3 * norm + 1 : 3 * norm + 2], params[3 * norm + 2 : 3 * norm + 3])
    finish(whole, out_sem)


def cross_backward_kernel(
    norm, seq, patches, place, grad, low, pre, query, context, keys, value, kept, params,
    out, small, grad_keys, grad_value, branch_out, query_out, whole, grad_context, grad_query, sems,
):
    load_kept(kept, whole, sems, (3, 0))
    grad_pre = norm_back(pre[...], params[3 * norm + 1 : 3 * norm + 2], grad[...], small)
    branch = grad_pre.astype(BF16)
    branch_out[...] = branch
    finish(whole.at[3], sems.at[3])
    grad_context[...] = dot_nt(branch, whole[3]).astype(BF16).astype(F32)
    count = branch.shape[0] // seq
    size = keys.shape[0] // count
    units = attention_units(count, seq, size, branch.shape[1])
    attend_backward(
        units, real_patch(size, patches), query, keys, value, grad_context, grad_query, grad_keys, grad_value
    )
    query_low = grad_query[...].astype(BF16)
    query_out[...] = query_low
    small[3:4] = column_total(query_low)
    small[4:5] = column_total(grad_value[...])
    finish(whole.at[0], sems.at[0])
    out[...] = grad_pre + dot_nn(query_low, whole[0])


def cross_weights_kernel(
    spot, place, context, branch, grad_query, low, grad_keys, grad_value, source, keep_held, send_held,
    keep, send, grads, out_sem,
):
    grads[3] = dot_tn(context[...], branch[...]).astype(BF16)
    grads[0] = dot_tn(grad_query[...], low[...]).astype(BF16)
    grads[1] = dot_tn(grad_keys[...], source[...]).astype(BF16)
    grads[2] = dot_tn(grad_value[...], source[...]).astype(BF16)
    store_attention(place, grads, (keep, send), spot, out_sem)
    finish(grads, out_sem)


def image_backward_kernel(
    image_rows, spot, n_held, place, images, grad_keys, grad_value, kept, kept_image, *refs,
):
    out, small, keep, send, whole, whole_image, grads, low, sems, image_sem, out_sem = refs[n_held:]
    load_kept(kept, whole, sems, (1, 2))
    start(kept_image, whole_image, image_sem)
    finish(whole.at[1], sems.at[1])
    finish(whole.at[2], sems.at[2])
    finish(whole_image, image_sem)
    patches, count = out.shape[:2]
    size = images.shape[0] // count
    small[...] = jnp.zeros_like(small)
    for row in range(count):
        rows = slice(row * size, (row + 1) * size)
        source = dot_nn(grad_keys[rows], whole[1]) + dot_nn(grad_value[rows], whole[2])
        source = source.astype(BF16)
        low[rows] = source
        out[:, row, :] = dot_nn(source, whole_image[...])[:patches]
    grads[...] = dot_tn(low[...], images[...]).astype(BF16)
    store_image(place, grads, (keep, send), spot, image_rows, out_sem)
    small[0:1] = column_total(low[...])
    finish(grads, out_sem)


def combine_kernel(
    keep, core, one0, one1, two0, two1, own, down, across, up, kept, arrived, first, second, sems,
):
    for half, (one, two) in enumerate(((one0, two0), (one1, two1))):
        start(keep.at[half, 0], kept.at[half], sems.at[0])
        start(core.at[half, 0], arrived.at[half], sems.at[1])
        start(one.at[0], first.at[half], sems.at[2])
        start(two, second.at[half], sems.at[3])
    for number, target in enumerate((kept, arrived, first, second)):
        finish(target, sems.at[number])
    for step, target in enumerate((own, down, across, up)):
        for half in range(2):
            total = kept[half, step].astype(F32) + arrived[half, step].astype(F32)
            total = total + first[half, step].astype(F32) + second[half, step].astype(F32)
            target[half] = total.astype(target.dtype)


def pick_kernel(picks, *refs):
    *parts, out, held, sem = refs
    pick_copies(picks, parts, held, sem)
    finish(held, sem)
    out[...] = held[...].astype(out.dtype)


def finish_kernel(blocks, quarter, names, held, n_results, place, *refs):
    results, refs = refs[:n_results], refs[n_results:]
    width = results[0].shape[3]
    targets = dict(zip(names, refs[held:]))
    scratch = refs[held + len(names) :]
    sem, out_sem = scratch[-2:]
    for number, (kind, offset, _) in enumerate(blocks):
        buffer = scratch[2 * number]
        for core in range(2):
            for half in range(2):
                for entry in range(4):
                    if n_results == 1:
                        slot = core ^ DISTANCES[half][entry]
                        piece = results[0].at[slot, half]
                    else:
                        slot = place[0] ^ (core ^ DISTANCES[half][entry])
                        piece = piece_of(results, core, half, entry)
                    if kind == ATTENTION:
                        rows = quarter // 4
                        spot = attention_spot(buffer, quarter, half, slot, 0)
                        start(piece.at[pl.ds(offset, rows)], spot, sem.at[number])
                    elif kind == FEED:
                        rows = buffer.shape[1] // SLICES
                        spot = buffer.at[half, aligned(slot * rows, rows)]
                        start(piece.at[pl.ds(offset, rows)], spot, sem.at[number])
                    else:
                        rows = quarter * buffer.shape[1] // width // SLICES // 2
                        piece = piece.at[pl.ds(offset, rows)]
                        image_copies(buffer, piece, quarter, half, slot, 0, sem.at[number], True)
    for number, (kind, _, layer) in enumerate(blocks):
        buffer, wide = scratch[2 * number : 2 * number + 2]
        done = out_sem.at[number]
        finish(buffer, sem.at[number])
        wide[...] = buffer[...].astype(F32)
        if kind == ATTENTION:
            start(wide.at[pl.ds(0, 3)], targets[ATTENTION_IN].at[layer], done)
            start(wide.at[3], targets[ATTENTION_OUT].at[layer], done)
        elif kind == FEED:
            start(wide.at[0], targets[FEED_IN].at[layer], done)
            start(wide.at[1], targets[FEED_OUT].at[layer], done)
        else:
            start(wide, targets[IMAGE], done)
    for number in range(len(blocks)):
        finish(scratch[2 * number + 1], out_sem.at[number])


def shape(dims, kind=F32):
    return jax.ShapeDtypeStruct(tuple(dims), kind)


def call(kernel, ins, outs, scratch, aliases=None):
    return pl.pallas_call(
        kernel,
        in_specs=[spec for _, spec in ins],
        out_specs=[spec for _, spec in outs],
        out_shape=[s for s, _ in outs],
        scratch_shapes=scratch,
        input_output_aliases=aliases or {},
        compiler_params=pltpu.CompilerParams(vmem_limit_bytes=60 << 20),
        cost_estimate=pl.CostEstimate(flops=0, bytes_accessed=0, transcendentals=0),
    )(*[v for v, _ in ins])


class Ring:
    def __init__(self, at, name, own):
        self.at, self.name = at, name
        at[name] = {0: own}

    def up(self):
        parts = self.at[self.name]
        parts[1] = pass_on(parts[0])

    def down(self):
        parts = self.at[self.name]
        parts[3] = pass_on(parts[0], -1)

    def far(self):
        parts = self.at[self.name]
        parts[2] = pass_on(parts[1])

    def direct(self):
        parts = self.at[self.name]
        for way in (1, 2, 3):
            parts[way] = pass_on(parts[0], way)

    def take(self):
        parts = self.at.pop(self.name)
        return [parts[i] for i in range(4)]


class Widen:
    def __init__(self, at, name, first, second):
        self.at, self.name = at, name
        at[name] = {"own": (first, second)}

    def one(self):
        held = self.at[self.name]
        first, second = held.pop("own")
        held["both"] = (first, swap(first, 2), second, swap(second, 4))

    def two(self):
        held = self.at[self.name]
        both = held.pop("both")
        near = jnp.stack(both[:2]), jnp.stack(both[2:])
        held["near"] = near
        held["far"] = swap(near[0], 4), swap(near[1], 2)

    def direct(self):
        held = self.at[self.name]
        own = held.pop("own")
        held["lines"] = [jnp.stack(own)] + [swap(jnp.stack(own), bit) for bit in (2, 4, 6)]

    def two_early(self):
        self.two()
        held = self.at[self.name]
        held["near all"] = jnp.stack(held.pop("near"))
        held["near core"] = swap(held["near all"], 1)

    def core_late(self):
        held = self.at[self.name]
        held["far all"] = jnp.stack(held.pop("far"))
        held["far core"] = swap(held["far all"], 1)

    def core_direct(self):
        held = self.at[self.name]
        lines = held.pop("lines")
        order = [[distance // 2 for distance in half] for half in DISTANCES]
        held["all"] = jnp.stack([jnp.stack([lines[i][half] for i in order[half]]) for half in range(2)])
        held["core"] = swap(held["all"], 1)

    def core(self):
        held = self.at[self.name]
        near, far = held.pop("near"), held.pop("far")
        held["all"] = jnp.stack([jnp.concatenate([near[half], far[half]]) for half in range(2)])
        held["core"] = swap(held["all"], 1)

    def take(self):
        held = self.at.pop(self.name)
        if "all" in held:
            return held["all"], held["core"]
        return held["near all"], held["far all"], held["near core"], held["far core"]


class Reduce:
    def __init__(self, at, name, keep, send):
        self.at, self.name = at, name
        at[name] = {"keep": keep, "send": send}

    def core(self):
        held = self.at[self.name]
        held["core"] = swap(held.pop("send"), 1)

    def one(self):
        held = self.at[self.name]
        keep, core = held["keep"], held["core"]
        held["one"] = swap(added(keep[0, 2:], core[0, 2:]), 4), swap(added(keep[1, 2:], core[1, 2:]), 2)

    def two(self):
        held = self.at[self.name]
        keep, core, one = held["keep"], held["core"], held["one"]
        held["two"] = (
            swap(added(keep[0, 1], core[0, 1], one[0][1]), 2),
            swap(added(keep[1, 1], core[1, 1], one[1][1]), 4),
        )

    def combine(self):
        held = self.at[self.name]
        arrays = [held[name] for name in ("keep", "core")] + list(held["one"]) + list(held["two"])
        rows, width = arrays[0].shape[3:]
        mp = arrays[0].shape[2]
        outs = [shape((2, rows, width), kind) for kind in (F32, BF16, BF16, F32)]
        parts = call(
            combine_kernel,
            [(v, ANY) for v in arrays],
            [(v, VMEM) for v in outs],
            [pltpu.VMEM((2, mp, rows, width), BF16)] * 4 + [pltpu.SemaphoreType.DMA((4,))],
        )
        self.at[self.name] = {"own": parts[0], "parts": parts[1:]}

    def join(self, other):
        theirs = self.at.pop(other.name)
        held = self.at[self.name]
        held["own"] = jnp.concatenate([held["own"], theirs["own"]], axis=1)
        held["parts"] = [jnp.concatenate(pair, axis=1) for pair in zip(held["parts"], theirs["parts"])]

    def far(self):
        held = self.at[self.name]
        held["far"] = pass_on(held["parts"][1])

    def near(self):
        held = self.at[self.name]
        down, _, up = held.pop("parts")
        held["up"] = pass_on(added(up, held.pop("far")))
        held["down"] = pass_on(down, -1)

    def direct(self):
        held = self.at[self.name]
        down, across, up = held.pop("parts")
        held["up"], held["across"], held["down"] = pass_on(added(up)), pass_on(across, 2), pass_on(down, -1)

    def owned(self):
        held = self.at.pop(self.name)
        own = added(held["own"], *[held[name] for name in ("up", "across", "down") if name in held])
        bit = SLICES
        while bit < lax.axis_size("dp"):
            own = added(own, swap(own, bit))
            bit *= 2
        return own


def on_device(
    tokens, images, segment_of_token, image_of_row, attention_in, query_value_bias, attention_out, output_bias,
    feed_in, feed_bias, feed_out, image_weight, image_bias, norm_gain, norm_bias, cotangent,
):
    mp = lax.axis_size("mp")
    slot = lax.axis_index("dp") % SLICES
    owner = lax.axis_index("mp")
    place = jnp.stack([slot, owner]).astype(jnp.int32)
    own_rows, seq, width = tokens.shape
    group_rows = segment_of_token.shape[0]
    patches, image_width = images.shape[1:]
    quarter = attention_in.shape[3]
    units = feed_in.shape[2]
    n_tokens = own_rows * seq
    inward = attention_in.transpose(0, 1, 3, 2)
    image = image_weight.T

    attention_rows = quarter // 4
    feed_rows = units // SLICES
    image_rows = quarter * image_width // width // SLICES // 2

    token_shape = shape((n_tokens, width))
    token_low = shape((n_tokens, width), BF16)
    row_low = shape((own_rows, seq, width), BF16)
    inner_shape = shape((mp, n_tokens, units))
    inner_low = shape((mp, n_tokens, units), BF16)
    padded = -(-patches // 16) * 16
    n_patches = own_rows * padded
    patch_low = shape((n_patches, width), BF16)
    small_shape = shape((8, width))
    attention_grad = shape((2, 4, mp, attention_rows, width), BF16)
    feed_grad = shape((2, 4, mp, feed_rows, width), BF16)
    image_grad = shape((2, 4, mp, image_rows, width), BF16)
    kept_square = shape((4, width, width), BF16)
    kept_wide = shape((2, mp, units, width), BF16)
    kept_tall = shape((width, image_width), BF16)
    square = pltpu.VMEM((4, width, width), BF16)
    wide = pltpu.VMEM((2, mp, units, width), BF16)
    tall = pltpu.VMEM((width, image_width), BF16)
    token_f32 = pltpu.VMEM((n_tokens, width), F32)
    token_bf16 = pltpu.VMEM((n_tokens, width), BF16)
    row_bf16 = pltpu.VMEM((own_rows, seq, width), BF16)
    inner_f32 = pltpu.VMEM((mp, n_tokens, units), F32)
    inner_bf16 = pltpu.VMEM((mp, n_tokens, units), BF16)
    dma = pltpu.SemaphoreType.DMA
    matmul = 2 * n_tokens * width * width
    patch_matmul = 2 * n_patches * width * width

    local_order = image_of_row % group_rows
    here = owner * own_rows + jnp.arange(own_rows, dtype=jnp.int32)
    chosen = (local_order[None, :] == here[:, None]).astype(jnp.int32)
    source_row = jnp.sum(chosen * jnp.arange(group_rows, dtype=jnp.int32)[None, :], axis=1)
    picks_in = ((owner - source_row // own_rows) % mp) * own_rows + source_row % own_rows
    mine = (jnp.arange(group_rows, dtype=jnp.int32)[None, :] == here[:, None]).astype(jnp.int32)
    image_row = jnp.sum(mine * local_order[None, :], axis=1)
    picks_out = ((owner - image_row // own_rows) % mp) * own_rows + image_row % own_rows
    segments = jnp.sum(chosen[:, :, None] * segment_of_token[None], axis=1)
    code = jnp.arange(own_rows, dtype=jnp.int32)[:, None] * seq + segments
    code_col = code.reshape(n_tokens, 1)
    code_row = code.reshape(own_rows // 2, 2 * seq)

    flat = jnp.concatenate([query_value_bias.reshape(-1), feed_bias.reshape(-1), image_bias])
    bias_rows = -(-flat.shape[0] // (32 * width)) * 16
    biases = jnp.pad(flat, (0, 2 * bias_rows * width - flat.shape[0])).reshape(2, bias_rows, width)
    first_rows = 2 * attention_rows + image_rows
    first, second, third = call(
        slice_kernel,
        [(place, SMEM), (biases, VMEM)] + [(v, ANY) for v in (inward, attention_out, feed_in, feed_out, image)],
        [
            (shape((2, rows, width), BF16), VMEM)
            for rows in (first_rows + bias_rows, feed_rows + attention_rows, feed_rows)
        ],
        [dma((3,))],
    )

    at = {}

    def step():
        done = lax.optimization_barrier(at)
        at.clear()
        at.update(done)

    rings = {
        name: Ring(at, name, own)
        for name, own in (
            ("first", first), ("second", second), ("third", third), (TOKENS, tokens), (COTANGENT, cotangent),
        )
    }

    def gathered(name, rows=None):
        parts = rings[name].take()[1:]
        return Widen(at, name, *[jnp.stack([part[half, :rows] for part in parts]) for half in range(2)])

    rings["first"].direct()
    step()

    parts = [part[:, first_rows:].reshape(-1) for part in at["first"].values()]
    ordered = jnp.stack(parts)[(owner - jnp.arange(mp)) % mp].astype(F32)
    cut0 = query_value_bias.size
    cut1 = cut0 + feed_bias.size
    bias = jnp.concatenate(
        [
            ordered[:, :cut0].reshape(mp, -1, quarter).transpose(1, 0, 2).reshape(-1, width),
            ordered[:, cut0:cut1].reshape(mp, 2, units).transpose(1, 0, 2).reshape(-1, width),
            ordered[:, cut1 : cut1 + quarter].reshape(1, width),
        ]
    )
    params = jnp.stack([output_bias, norm_gain, norm_bias], axis=1).astype(F32).reshape(-1, width)
    patch_rows = jnp.pad(images, ((0, 0), (0, padded - patches), (0, 0))).reshape(n_patches, image_width)
    at["tables"] = bias, params, code_col, code_row, picks_in, picks_out, image_row, patch_rows
    first_wide = gathered("first", first_rows)
    first_wide.one()
    rings["second"].up()
    rings["second"].down()
    rings[TOKENS].up()
    step()
    bias, params, code_col, code_row, picks_in, picks_out, image_row, patch_rows = at.pop("tables")
    first_wide.two()
    rings["second"].far()
    rings[TOKENS].down()
    rings["third"].up()
    step()
    second_wide = gathered("second")
    first_wide.core()
    second_wide.one()
    rings[TOKENS].far()
    rings["third"].down()
    step()

    attention_pieces = [None, None, None]
    attention_at = [0, feed_rows, attention_rows]
    feed_pieces = [None, None]
    feed_at = [0, 0]

    def attention_ins(layer):
        return [(inward, ANY), (attention_out, ANY)] + [(piece, ANY) for piece in attention_pieces[layer]]

    def feed_ins(layer):
        return [(feed_in, ANY), (feed_out, ANY)] + [(piece, ANY) for piece in feed_pieces[layer]]

    def self_forward(layer, norm, parts):
        picked = len(parts) > 1
        return call(
            partial(self_forward_kernel, layer, norm, attention_at[layer], len(parts), len(attention_pieces[layer])),
            [(place, SMEM), (picks_in, SMEM)]
            + [(part, ANY if picked else VMEM) for part in parts]
            + attention_ins(layer)
            + [(bias, VMEM), (params, VMEM), (code_col, VMEM), (code_row, VMEM)],
            [(token_shape, VMEM), (token_low, VMEM), (token_shape, VMEM)] + [(token_low, VMEM)] * 4 + [(kept_square, ANY)],
            [square, dma((4,)), dma] + ([row_bf16, token_f32, dma] if picked else []),
        )

    def self_backward(norm, grad, kept, leave, spot, rows, held):
        _, low, pre, query, keys, value, context, weights = kept
        grads = shape((2, 4, mp, rows, width), BF16)
        ins = [(place, SMEM)] + [(v, VMEM) for v in (grad, low, pre, query, keys, value, context)]
        ins += [(weights, ANY), (params, VMEM), (code_col, VMEM), (code_row, VMEM)]
        return call(
            partial(self_backward_kernel, leave, norm, spot, len(held)),
            ins + [(v, ANY) for v in held],
            [(row_low if leave else token_shape, VMEM), (small_shape, VMEM)] + [(grads, ANY)] * 2,
            [square, square] + [token_bf16] * 4 + [dma((4,)), dma],
            {len(ins) + i: 2 + i for i in range(len(held))},
        )

    def feed_forward(layer, norm, rows):
        return call(
            partial(feed_forward_kernel, layer, norm, feed_at[layer], len(feed_pieces[layer])),
            [(place, SMEM), (rows, VMEM)] + feed_ins(layer) + [(bias, VMEM), (params, VMEM)],
            [(token_shape, VMEM), (token_low, VMEM), (token_shape, VMEM)]
            + [(inner_shape, ANY), (inner_low, ANY), (kept_wide, ANY)],
            [wide, inner_f32, inner_bf16, dma((2, mp)), dma],
        )

    def feed_backward(norm, grad, kept):
        _, low, pre, slope, active, weights = kept
        return call(
            partial(feed_backward_kernel, norm),
            [(place, SMEM)] + [(v, ANY) for v in (grad, low, pre, slope, active, weights)] + [(params, VMEM)],
            [(token_shape, VMEM), (small_shape, VMEM)] + [(feed_grad, ANY)] * 2,
            [wide, wide, token_f32, token_bf16, token_f32, inner_f32, inner_bf16]
            + [dma((3 + 2 * mp,)), dma((2, mp)), dma],
        )

    def feed_both(layer, norm, rows, parts):
        return call(
            partial(feed_both_kernel, layer, norm, feed_at[layer], len(parts), len(feed_pieces[layer])),
            [(place, SMEM), (picks_in, SMEM), (rows, VMEM), (feed_in, ANY), (feed_out, ANY)]
            + [(v, ANY) for v in parts + list(feed_pieces[layer])]
            + [(bias, VMEM), (params, VMEM)],
            [(row_low, VMEM), (token_shape, VMEM), (small_shape, VMEM)] + [(feed_grad, ANY)] * 2,
            [wide, wide, inner_f32, inner_bf16, token_bf16, token_f32, token_f32, row_bf16]
            + [dma((2, mp)), dma, dma],
        )

    def pick_rows(parts):
        return call(
            pick_kernel,
            [(picks_out, SMEM)] + [(part, ANY) for part in parts],
            [(shape((own_rows, seq, width)), VMEM)],
            [row_bf16, dma],
        )[0]

    attention_pieces[0] = attention_pieces[2] = first_wide.take()
    second_wide.two_early()
    rings["third"].far()
    rings[COTANGENT].up()
    text_attention = self_forward(0, 0, rings[TOKENS].take())
    at["stream"] = text_attention[0]
    step()

    second_wide.core_late()
    third_wide = gathered("third")
    third_wide.one()
    rings[COTANGENT].down()
    projected, image_keys, image_value, kept_image = call(
        partial(image_forward_kernel, 2, attention_rows, 2 * attention_rows, image_rows, len(attention_pieces[2])),
        [(place, SMEM), (patch_rows, VMEM), (image, ANY)] + attention_ins(2) + [(bias, VMEM)],
        [(patch_low, VMEM)] * 3 + [(kept_tall, ANY)],
        [square, tall, dma((4,)), dma, dma],
    )
    at["keys"] = image_keys
    step()

    attention_pieces[1] = feed_pieces[0] = second_wide.take()
    third_wide.two()
    rings[COTANGENT].far()
    text_feed = feed_forward(0, 1, at.pop("stream"))
    joining_attention = self_forward(1, 2, [text_feed[0]])
    at["stream"] = joining_attention[0]
    step()

    third_wide.core()
    image_keys = at.pop("keys")
    cross_attention = call(
        partial(cross_forward_kernel, 2, 3, attention_rows, seq, patches, len(attention_pieces[2])),
        [(place, SMEM), (at.pop("stream"), VMEM), (image_keys, VMEM), (image_value, VMEM)]
        + attention_ins(2)
        + [(bias, VMEM), (params, VMEM)],
        [(token_shape, VMEM), (token_low, VMEM), (token_shape, VMEM), (token_shape, VMEM), (token_low, VMEM)]
        + [(kept_square, ANY)],
        [square, token_f32, dma((4,)), dma],
    )
    at["stream"] = cross_attention[0]
    step()

    feed_pieces[1] = third_wide.take()

    mixed, grad, small_joining_feed, keep, send = feed_both(1, 4, at.pop("stream"), rings[COTANGENT].take())
    mixed_ring = Ring(at, "mixed", mixed)
    at["grad"] = grad
    last_grads = Reduce(at, "last", keep, send)
    step()

    last_grads.core()
    mixed_ring.up()
    grad, small_cross, grad_keys, grad_value, cross_branch, cross_query = call(
        partial(cross_backward_kernel, 3, seq, patches),
        [(place, SMEM), (at.pop("grad"), VMEM)]
        + [(cross_attention[i], VMEM) for i in (1, 2, 3, 4)]
        + [(image_keys, VMEM), (image_value, VMEM), (cross_attention[5], ANY), (params, VMEM)],
        [(token_shape, VMEM), (small_shape, VMEM)] + [(patch_low, VMEM)] * 2 + [(token_low, VMEM)] * 2,
        [square, token_f32, token_f32, dma((4,))],
    )
    at["grad"] = grad
    step()

    last_grads.one()
    mixed_ring.down()
    middle_rows = 2 * attention_rows
    grad, small_joining, keep, send = self_backward(
        2, at.pop("grad"), joining_attention, False, attention_rows, middle_rows, ()
    )
    at["grad"] = grad
    cross_grads = (cross_attention[4], cross_branch, cross_query, cross_attention[1], grad_keys, grad_value, projected)
    keep, send = call(
        partial(cross_weights_kernel, 0),
        [(place, SMEM)] + [(v, VMEM) for v in cross_grads] + [(keep, ANY), (send, ANY)],
        [(shape(keep.shape, BF16), ANY)] * 2,
        [square, dma],
        {8: 0, 9: 1},
    )
    middle_grads = Reduce(at, "middle", keep, send)
    at["patch grads"] = grad_keys, grad_value
    step()

    last_grads.two()
    middle_grads.core()
    mixed_ring.far()
    grad, small_text_feed, keep, send = feed_backward(1, at.pop("grad"), text_feed)
    at["grad"] = grad
    first_grads = Reduce(at, "first", keep, send)
    step()

    mixed_parts = mixed_ring.take()
    middle_grads.one()
    first_grads.core()
    last_grads.combine()
    held = at["last"]
    down, across, up = held.pop("parts")
    held["up"], held["down"] = pass_on(up.astype(BF16)), pass_on(down, -1)
    held["across part"] = across
    rows_back, small_text, keep, send = self_backward(
        0, at.pop("grad"), text_attention, True, 0, attention_rows + image_rows, ()
    )
    back_ring = Ring(at, "back", rows_back)
    at["text"] = keep, send
    step()

    middle_grads.two()
    first_grads.one()
    at["last"]["across"] = pass_on(at["last"].pop("across part"), 2)
    grad_keys, grad_value = at.pop("patch grads")
    keep, send = at.pop("text")
    grad_images, small_image, keep, send = call(
        partial(image_backward_kernel, image_rows, attention_rows, 2),
        [(place, SMEM), (patch_rows, VMEM), (grad_keys, VMEM), (grad_value, VMEM), (cross_attention[5], ANY)]
        + [(kept_image, ANY), (keep, ANY), (send, ANY)],
        [(shape((patches, own_rows, image_width)), VMEM), (small_shape, VMEM)] + [(shape(keep.shape, BF16), ANY)] * 2,
        [square, tall, tall, pltpu.VMEM((n_patches, width), BF16), dma((4,)), dma, dma],
        {6: 2, 7: 3},
    )
    text_grads = Reduce(at, "text", keep, send)
    at[SMALL] = jnp.concatenate(
        [small_text, small_text_feed, small_joining, small_cross, small_joining_feed, small_image]
    )
    step()

    first_grads.two()
    text_grads.core()
    middle_grads.combine()
    middle_grads.far()
    back_ring.up()
    at["mixed"] = pick_rows(mixed_parts)
    step()

    text_grads.one()
    middle_grads.near()
    first_grads.combine()
    first_grads.far()
    at[SMALL] = at[SMALL] + swap(at[SMALL], 1)
    at["last own"] = last_grads.owned()
    step()

    early = Widen(at, "early", *jnp.concatenate([at.pop("last own"), middle_grads.owned()], axis=1))
    early.one()
    text_grads.two()
    first_grads.near()
    back_ring.down()
    at[SMALL] = at[SMALL] + swap(at[SMALL], 2)
    step()

    early.two()
    text_grads.combine()
    text_grads.direct()
    at["first own"] = first_grads.owned()
    at[SMALL] = at[SMALL] + swap(at[SMALL], 4)
    step()

    late = Widen(at, "late", *jnp.concatenate([at.pop("first own"), text_grads.owned()], axis=1))
    late.one()
    early.core()
    back_ring.far()
    at[SMALL] = at[SMALL] + swap_owner(at[SMALL], 1)
    step()

    late.two()
    at[TOKENS] = pick_rows(back_ring.take())
    early_pieces = early.take()
    smalls = at.pop(SMALL)
    smalls = smalls + swap_owner(smalls, 2)
    bit = SLICES
    while bit < lax.axis_size("dp"):
        smalls = smalls + swap(smalls, bit)
        bit *= 2
    at[SMALL] = smalls

    whole_shapes = {
        ATTENTION_IN: shape(inward.shape),
        ATTENTION_OUT: shape(attention_out.shape),
        FEED_IN: shape(feed_in.shape),
        FEED_OUT: shape(feed_out.shape),
        IMAGE: shape(image.shape),
    }
    block_of = {ATTENTION: (4, quarter, width), FEED: (2, units, width), IMAGE: (quarter, image_width)}
    names_of = {ATTENTION: [ATTENTION_IN, ATTENTION_OUT], FEED: [FEED_IN, FEED_OUT], IMAGE: [IMAGE]}
    written = {}

    def write_out(result, *blocks):
        names = list(dict.fromkeys(name for kind, _, _ in blocks for name in names_of[kind]))
        names = [name for name in names if name in written] + [name for name in names if name not in written]
        held = [name for name in names if name in written]
        scratch = [pltpu.VMEM(block_of[kind], form) for kind, _, _ in blocks for form in (BF16, F32)]
        results = call(
            partial(finish_kernel, blocks, quarter, names, len(held), len(result)),
            [(place, SMEM)] + [(v, ANY) for v in result] + [(written[name], ANY) for name in held],
            [(whole_shapes[name], ANY) for name in names],
            scratch + [dma((len(blocks),)), dma((len(blocks),))],
            {1 + len(result) + i: i for i in range(len(held))},
        )
        written.update(zip(names, results))

    write_out(
        early_pieces, (FEED, 0, 1), (ATTENTION, feed_rows, 2), (ATTENTION, feed_rows + attention_rows, 1)
    )
    at["written"] = written
    step()
    written = at.pop("written")
    late.core()
    smalls = at.pop(SMALL).reshape(6, 8, width)

    def own_part(values):
        return lax.dynamic_slice_in_dim(values, owner * quarter, quarter, axis=values.ndim - 1)

    grad_query_value_bias = own_part(jnp.stack([smalls[i, 3:5] for i in (0, 2, 3)]))
    grad_feed_bias = jnp.stack([smalls[i, 3 : 3 + mp].reshape(-1) for i in (1, 4)])
    grad_feed_bias = lax.dynamic_slice_in_dim(grad_feed_bias, owner * units, units, axis=1)
    vectors = (
        grad_query_value_bias, smalls[:5, 2], grad_feed_bias, own_part(smalls[5, 0]), smalls[:5, 0], smalls[:5, 1]
    )
    at["vectors"] = vectors
    step()
    vectors = at.pop("vectors")
    write_out(
        late.take(), (FEED, 0, 0), (ATTENTION, feed_rows, 0), (IMAGE, feed_rows + attention_rows, 0)
    )
    return (
        at["mixed"],
        at[TOKENS],
        grad_images.transpose(1, 0, 2),
        written[ATTENTION_IN].transpose(0, 1, 3, 2),
        vectors[0],
        written[ATTENTION_OUT],
        vectors[1],
        written[FEED_IN],
        vectors[2],
        written[FEED_OUT],
        written[IMAGE].T,
        vectors[3],
        vectors[4],
        vectors[5],
    )


def solution(mesh):
    rows = P(("dp", "mp"), None, None)
    return jax.shard_map(
        on_device,
        mesh=mesh,
        in_specs=(
            rows,
            rows,
            P("dp", None),
            P("dp"),
            P(None, None, None, "mp"),
            P(None, None, "mp"),
            P(None, "mp", None),
            P(),
            P(None, None, "mp"),
            P(None, "mp"),
            P(None, "mp", None),
            P(None, "mp"),
            P("mp"),
            P(),
            P(),
            rows,
        ),
        out_specs=(
            rows,
            rows,
            rows,
            P(None, None, None, "mp"),
            P(None, None, "mp"),
            P(None, "mp", None),
            P(),
            P(None, None, "mp"),
            P(None, "mp"),
            P(None, "mp", None),
            P(None, "mp"),
            P("mp"),
            P(),
            P(),
        ),
        check_vma=False,
    )
```

```python
from functools import partial

import jax
import jax.numpy as jnp
from jax import lax
from jax.experimental import pallas as pl
from jax.experimental.pallas import tpu as pltpu
from jax.sharding import PartitionSpec as P

HEAD_DIM = 64
STACK = 4 * HEAD_DIM
TOGETHER = 6
SLICES = 8
EPSILON = 1e-06
BLOCKED = -1000000000.0
SCALE = HEAD_DIM ** (-0.5)
DISTANCES = ((0, 2, 4, 6), (0, 4, 2, 6))
ATTENTION, FEED, IMAGE, ATTENTION_IN, ATTENTION_OUT, FEED_IN, FEED_OUT = range(7)
SMALL, TOKENS, COTANGENT = "small", "tokens", "cotangent"
F32 = jnp.float32
BF16 = jnp.bfloat16

ANY = pl.BlockSpec(memory_space=pl.ANY)
VMEM = pl.BlockSpec(memory_space=pltpu.VMEM)
SMEM = pl.BlockSpec(memory_space=pltpu.SMEM)


def swap(values, bit):
    count = lax.axis_size("dp")
    return lax.ppermute(values, "dp", [(i, i ^ bit) for i in range(count)])


def pass_on(values, way=1):
    count = lax.axis_size("mp")
    return lax.ppermute(values, "mp", [(i, (i + way) % count) for i in range(count)])


def swap_owner(values, bit):
    count = lax.axis_size("mp")
    return lax.ppermute(values, "mp", [(i, i ^ bit) for i in range(count)])


def added(*terms):
    total = terms[0].astype(F32)
    for term in terms[1:]:
        total = total + term
    return total.astype(BF16)


def dot_nn(left, right):
    return lax.dot_general(left, right, (((1,), (0,)), ((), ())), preferred_element_type=F32)


def dot_nt(left, right):
    return lax.dot_general(left, right, (((1,), (1,)), ((), ())), preferred_element_type=F32)


def dot_tn(left, right):
    return lax.dot_general(left, right, (((0,), (0,)), ((), ())), preferred_element_type=F32)


def start(source, target, sem):
    pltpu.make_async_copy(source, target, sem).start()


def finish(whole, sem):
    pltpu.make_async_copy(whole, whole, sem).wait()


def aligned(first, count, step=16):
    return pl.ds(pl.multiple_of(first, step), count)


def each_slice(place, first_step, mp):
    for core in range(2):
        for half in range(2):
            for entry in range(4):
                slot = place[0] ^ (core ^ DISTANCES[half][entry])
                for step in range(first_step, mp):
                    yield core, half, entry, step, slot, (place[1] + mp - step) % mp


def piece_of(pieces, core, half, entry):
    if len(pieces) == 2:
        return pieces[core].at[half, entry]
    return pieces[2 * core + entry // 2].at[half, entry % 2]


def attention_spot(whole, quarter, half, slot, owner):
    span = 4 * quarter // SLICES
    count = quarter // span
    row = owner * quarter + (slot % count) * span + half * (span // 2)
    return whole.at[slot // count, aligned(row, span // 2)]


def load_attention(place, own, pieces, offset, layer, whole, sems):
    mp = pieces[0].shape[2] + 1
    quarter = whole.shape[1] // mp
    rows = quarter // 4
    for mat in range(4):
        source = own[0].at[layer, mat] if mat < 3 else own[1].at[layer]
        start(source, whole.at[mat, aligned(place[1] * quarter, quarter)], sems.at[mat])
    for core, half, entry, step, slot, owner in each_slice(place, 1, mp):
        start(
            piece_of(pieces, core, half, entry).at[step - 1, pl.ds(offset, rows)],
            attention_spot(whole, quarter, half, slot, owner),
            sems.at[slot // 2],
        )


def store_attention(place, whole, outs, offset, sem):
    mp = outs[0].shape[2]
    quarter = whole.shape[1] // mp
    for core, half, entry, step, slot, owner in each_slice(place, 0, mp):
        start(
            attention_spot(whole, quarter, half, slot, owner),
            outs[core].at[half, entry, step, pl.ds(offset, quarter // 4)],
            sem,
        )


def feed_spot(whole, half, slot, step):
    span = whole.shape[2] // SLICES
    return whole.at[half, step, aligned(slot * span, span)]


def load_feed(place, own, pieces, offset, layer, half, step, whole, sems):
    rows = whole.shape[2] // SLICES
    if step == 0:
        start(own[half].at[layer], whole.at[half, 0], sems.at[half, 0])
        return
    for core in range(2):
        for entry in range(4):
            slot = place[0] ^ (core ^ DISTANCES[half][entry])
            start(
                piece_of(pieces, core, half, entry).at[step - 1, pl.ds(offset, rows)],
                feed_spot(whole, half, slot, step),
                sems.at[half, step],
            )


def store_feed(place, whole, outs, half, step, sem):
    for core in range(2):
        for entry in range(4):
            slot = place[0] ^ (core ^ DISTANCES[half][entry])
            start(feed_spot(whole, half, slot, step), outs[core].at[half, entry, step], sem)


def image_copies(whole, piece, quarter, half, slot, owner, sem, inward):
    rows, width = piece.shape
    span = 2 * rows
    beyond = whole.shape[1] - width
    blocks = width // beyond
    plain = quarter // span
    base = owner * quarter + half * rows

    def move(inner, outer):
        start(inner, outer, sem) if inward else start(outer, inner, sem)

    @pl.when(slot < plain)
    def _():
        move(piece, whole.at[aligned(base + slot * span, rows), pl.ds(0, width)])

    @pl.when(slot >= plain)
    def _():
        for block in range(blocks):
            row = base + block * (quarter // blocks) + (slot - plain) * span
            move(
                piece.at[:, pl.ds(block * beyond, beyond)],
                whole.at[aligned(row, rows), pl.ds(width, beyond)],
            )


def load_image(place, own, pieces, offset, rows, whole, sem):
    mp = pieces[0].shape[2] + 1
    quarter = whole.shape[0] // mp
    start(own, whole.at[aligned(place[1] * quarter, quarter)], sem)
    for core, half, entry, step, slot, owner in each_slice(place, 1, mp):
        piece = piece_of(pieces, core, half, entry).at[step - 1, pl.ds(offset, rows)]
        image_copies(whole, piece, quarter, half, slot, owner, sem, True)


def store_image(place, whole, outs, offset, rows, sem):
    mp = outs[0].shape[2]
    quarter = whole.shape[0] // mp
    for core, half, entry, step, slot, owner in each_slice(place, 0, mp):
        piece = outs[core].at[half, entry, step, pl.ds(offset, rows)]
        image_copies(whole, piece, quarter, half, slot, owner, sem, False)


def norm_rows(values, gain_row, shift_row):
    center = values - jnp.mean(values, axis=-1, keepdims=True)
    moment = jnp.mean(center * center, axis=-1, keepdims=True)
    return center * lax.rsqrt(moment + EPSILON) * gain_row + shift_row


def norm_back(pre_norm, gain_row, grad_out, small):
    center = pre_norm - jnp.mean(pre_norm, axis=-1, keepdims=True)
    scale = lax.rsqrt(jnp.mean(center * center, axis=-1, keepdims=True) + EPSILON)
    normal = center * scale
    lifted = grad_out * gain_row
    grad_pre = scale * (
        lifted
        - jnp.mean(lifted, axis=-1, keepdims=True)
        - normal * jnp.mean(lifted * normal, axis=-1, keepdims=True)
    )
    small[...] = jnp.zeros_like(small)
    small[0:1] = jnp.sum(grad_out * normal, axis=0, keepdims=True)
    small[1:2] = jnp.sum(grad_out, axis=0, keepdims=True)
    small[2:3] = jnp.sum(grad_pre, axis=0, keepdims=True)
    return grad_pre


def column_total(values):
    return jnp.sum(values.astype(F32), axis=0, keepdims=True)


def spread_heads(values):
    lane = lax.broadcasted_iota(jnp.int32, (1, values.shape[1]), 1)
    parts = []
    for first in range(0, values.shape[1], HEAD_DIM):
        mask = ((lane >= first) & (lane < first + HEAD_DIM)).astype(F32).astype(values.dtype)
        parts.append(values * mask)
    return jnp.concatenate(parts, axis=0)


def pick_heads(values):
    lane = lax.broadcasted_iota(jnp.int32, (1, values.shape[1]), 1)
    rows = values.shape[0] * HEAD_DIM // values.shape[1]
    picked = values[:rows]
    for head in range(1, values.shape[1] // HEAD_DIM):
        picked = jnp.where(lane >= head * HEAD_DIM, values[head * rows : (head + 1) * rows], picked)
    return picked


def softmax(scores):
    raised = jnp.exp(scores - jnp.max(scores, axis=-1, keepdims=True))
    return raised * (1.0 / jnp.sum(raised, axis=-1, keepdims=True))


def score_back(weights, grad_weights):
    along = weights * grad_weights
    return (along - weights * jnp.sum(along, axis=-1, keepdims=True)).astype(BF16)


def attention_units(count, row_size, place_size, width):
    units = []
    for number in range(count):
        rows = slice(number * row_size, (number + 1) * row_size)
        places = slice(number * place_size, (number + 1) * place_size)
        units += [(number, rows, places, slice(first, first + STACK)) for first in range(0, width, STACK)]
    return [units[first : first + TOGETHER] for first in range(0, len(units), TOGETHER)]


def attend_forward(units, allowed, query, keys, value, context):
    for group in units:
        scores = [dot_nt(spread_heads(query[rows, lanes]).astype(BF16), keys[at, lanes]) for _, rows, at, lanes in group]
        weights = [
            softmax(jnp.where(allowed(unit[0]), score * SCALE, BLOCKED)).astype(BF16)
            for unit, score in zip(group, scores)
        ]
        for (_, rows, at, lanes), weight in zip(group, weights):
            context[rows, lanes] = pick_heads(dot_nn(weight, value[at, lanes])).astype(context.dtype)


def attend_backward(units, allowed, query, keys, value, grad_context, grad_query, grad_keys, grad_value):
    for group in units:
        queries = [spread_heads(query[rows, lanes]).astype(BF16) for _, rows, _, lanes in group]
        contexts = [spread_heads(grad_context[rows, lanes]).astype(BF16) for _, rows, _, lanes in group]
        scores = [dot_nt(one, keys[at, lanes]) for one, (_, _, at, lanes) in zip(queries, group)]
        grad_weights = [dot_nt(one, value[at, lanes]) for one, (_, _, at, lanes) in zip(contexts, group)]
        weights = [
            softmax(jnp.where(allowed(unit[0]), score * SCALE, BLOCKED)) for unit, score in zip(group, scores)
        ]
        grad_scores = [score_back(one, other) for one, other in zip(weights, grad_weights)]
        for weight, one, (_, _, at, lanes) in zip(weights, contexts, group):
            grad_value[at, lanes] = dot_tn(weight.astype(BF16), one).astype(BF16)
        for grad_score, one, (_, _, at, lanes) in zip(grad_scores, queries, group):
            grad_keys[at, lanes] = (dot_tn(grad_score, one) * SCALE).astype(BF16)
        for grad_score, (_, rows, at, lanes) in zip(grad_scores, group):
            mixed = pick_heads(dot_nn(grad_score, keys[at, lanes])) * SCALE
            grad_query[rows, lanes] = mixed.astype(grad_query.dtype)


def same_segment(code_col, code_row):
    size = code_row.shape[1]

    def allowed(group):
        column = code_col[group * size : (group + 1) * size]
        return jnp.concatenate([column] * (STACK // HEAD_DIM), axis=0) == code_row[group : group + 1]

    return allowed


def real_patch(size, patches):
    column = lax.broadcasted_iota(jnp.int32, (1, size), 1)
    return lambda row: column < patches


def pick_copies(picks, parts, target, sem):
    size = parts[0].shape[0]
    for row in range(target.shape[0]):
        for number, part in enumerate(parts):

            @pl.when(picks[row] // size == number)
            def _():
                start(part.at[picks[row] % size], target.at[row], sem)


def flat_rows(rows_ref, target):
    seq = rows_ref.shape[1]
    for row in range(rows_ref.shape[0]):
        target[row * seq : (row + 1) * seq] = rows_ref[row].astype(target.dtype)


def leave_rows(values, target):
    seq = target.shape[1]
    for row in range(target.shape[0]):
        target[row] = values[row * seq : (row + 1) * seq].astype(target.dtype)


def slice_kernel(
    place, head_bias, unit_bias, patch_bias, inward, outward, feed_in, feed_out, image, first, second, third, sems,
):
    slot = place[0]
    quarter, width = inward.shape[2:]
    span = 4 * quarter // SLICES
    count = quarter // span
    rows = span // 2
    feed_rows = feed_in.shape[1] // SLICES
    image_rows = first.shape[1] - 2 * rows - 16
    weights = first.at[:, pl.ds(0, 2 * rows + image_rows)]
    table = jnp.concatenate(
        [
            head_bias[...].astype(F32),
            jnp.zeros((head_bias.shape[0], width - quarter), F32),
        ],
        axis=1,
    )
    patch = jnp.concatenate([patch_bias[...].astype(F32), jnp.zeros((1, width - quarter), F32)], axis=1)
    table = jnp.concatenate([table, unit_bias[...].astype(F32), patch, jnp.zeros((7, width), F32)], axis=0)
    first[0, 2 * rows + image_rows :] = table.astype(BF16)
    first[1, 2 * rows + image_rows :] = jnp.zeros((16, width), BF16)

    def attention(layer, target, offset, sem):
        for half in range(2):
            row = (slot % count) * span + half * rows
            spot = target.at[half, pl.ds(offset, rows)]

            @pl.when(slot < 3 * count)
            def _():
                start(inward.at[layer, slot // count, aligned(row, rows)], spot, sem)

            @pl.when(slot >= 3 * count)
            def _():
                start(outward.at[layer, aligned(row, rows)], spot, sem)

    def feed(layer, target, offset, sem):
        for half, source in enumerate((feed_in, feed_out)):
            spot = target.at[half, pl.ds(offset, feed_rows)]
            start(source.at[layer, aligned(slot * feed_rows, feed_rows)], spot, sem)

    attention(0, first, 0, sems.at[0])
    attention(2, first, rows, sems.at[0])
    for half in range(2):
        spot = first.at[half, pl.ds(2 * rows, image_rows)]
        image_copies(image, spot, quarter, half, slot, 0, sems.at[0], False)
    feed(0, second, 0, sems.at[1])
    attention(1, second, feed_rows, sems.at[1])
    feed(1, third, 0, sems.at[2])
    for number, target in enumerate((weights, second, third)):
        finish(target, sems.at[number])


def self_forward(
    layer, norm, stream, bias, params, code_col, code_row, out, low, pre, query, keys, value, context, kept, whole, sems,
    out_sem,
):
    hb = stream.astype(BF16)
    low[...] = hb
    finish(whole.at[0], sems.at[0])
    query[...] = (dot_nt(hb, whole[0]) + bias[2 * layer : 2 * layer + 1]).astype(BF16)
    finish(whole.at[1], sems.at[1])
    keys[...] = dot_nt(hb, whole[1]).astype(BF16)
    finish(whole.at[2], sems.at[2])
    value[...] = (dot_nt(hb, whole[2]) + bias[2 * layer + 1 : 2 * layer + 2]).astype(BF16)
    groups, size = code_row.shape
    units = attention_units(groups, size, size, hb.shape[1])
    attend_forward(units, same_segment(code_col, code_row), query, keys, value, context)
    finish(whole.at[3], sems.at[3])
    start(whole, kept, out_sem)
    total = dot_nn(context[...], whole[3]) + params[3 * norm : 3 * norm + 1] + stream
    pre[...] = total
    out[...] = norm_rows(total, params[3 * norm + 1 : 3 * norm + 2], params[3 * norm + 2 : 3 * norm + 3])
    finish(whole, out_sem)


def self_forward_kernel(
    layer, norm, offset, n_parts, n_pieces, place, picks, *refs,
):
    parts, (inward, outward), refs = refs[:n_parts], refs[n_parts : n_parts + 2], refs[n_parts + 2 :]
    pieces, refs = refs[:n_pieces], refs[n_pieces:]
    held = refs[15:]
    if held:
        pick_copies(picks, parts, held[0], held[2])
    load_attention(place, (inward, outward), pieces, offset, layer, refs[12], refs[13])
    if held:
        finish(held[0], held[2])
        flat_rows(held[0], held[1])
        stream = held[1][...]
    else:
        stream = parts[0][...]
    self_forward(layer, norm, stream, *refs[:15])


def feed_self_forward_kernel(
    layer, norm, offset, next_layer, next_norm, next_offset, n_pieces, n_next, place, rows_ref, first_weight, second_weight,
    inward, outward, *refs,
):
    pieces, following, refs = refs[:n_pieces], refs[n_pieces : n_pieces + n_next], refs[n_pieces + n_next :]
    bias, params, code_col, code_row = refs[:4]
    feed_outs, self_outs, scratch = refs[4:10], refs[10:18], refs[18:]
    whole, slope, active, sems, out_sem, square, square_sems, square_out = scratch
    feed_refs = (bias, params, *feed_outs, whole, slope, active, sems, out_sem)
    for step in range(whole.shape[1]):
        for half in range(2):
            load_feed(place, (first_weight, second_weight), pieces, offset, layer, half, step, whole, sems)
    load_attention(place, (inward, outward), following, next_offset, next_layer, square, square_sems)
    feed_forward(layer, norm, place, rows_ref, *feed_refs)
    self_forward(
        next_layer, next_norm, feed_outs[0][...], bias, params, code_col, code_row, *self_outs, square, square_sems, square_out
    )


def load_kept(kept, whole, sems, order):
    for mat in order:
        start(kept.at[mat], whole.at[mat], sems.at[mat])


def self_backward_kernel(
    leave, norm, spot, n_held, place, grad, low, pre, query, keys, value, context, kept, params, code_col, code_row, *refs,
):
    out, small, keep, send, whole, grads, grad_context, grad_query, grad_keys, grad_value, sems, out_sem = refs[n_held:]
    load_kept(kept, whole, sems, (3, 0, 1, 2))
    grad_pre = norm_back(pre[...], params[3 * norm + 1 : 3 * norm + 2], grad[...], small)
    branch = grad_pre.astype(BF16)
    finish(whole.at[3], sems.at[3])
    grad_context[...] = dot_nt(branch, whole[3]).astype(BF16)
    grads[3] = dot_tn(context[...], branch).astype(BF16)
    groups, size = code_row.shape
    units = attention_units(groups, size, size, branch.shape[1])
    attend_backward(
        units, same_segment(code_col, code_row), query, keys, value, grad_context, grad_query, grad_keys, grad_value
    )
    hb = low[...]
    grads[0] = dot_tn(grad_query[...], hb).astype(BF16)
    grads[1] = dot_tn(grad_keys[...], hb).astype(BF16)
    grads[2] = dot_tn(grad_value[...], hb).astype(BF16)
    store_attention(place, grads, (keep, send), spot, out_sem)
    small[3:4] = column_total(grad_query[...])
    small[4:5] = column_total(grad_value[...])
    total = grad_pre
    for mat, part in enumerate((grad_query, grad_keys, grad_value)):
        finish(whole.at[mat], sems.at[mat])
        total = total + dot_nn(part[...], whole[mat])
    if leave:
        leave_rows(total, out)
    else:
        out[...] = total
    finish(grads, out_sem)


def feed_forward(
    layer, norm, place, rows_ref, bias, params, out, low, pre, slope_out, active_out, kept, whole, slope, active, sems, out_sem,
):
    parts = whole.shape[1]
    stream = rows_ref[...]
    hb = stream.astype(BF16)
    low[...] = hb
    total = params[3 * norm : 3 * norm + 1] + stream
    for step in range(parts):
        row = 6 + layer * parts + (place[1] + parts - step) % parts
        finish(whole.at[0, step], sems.at[0, step])
        units = dot_nn(hb, whole[0, step]) + bias[pl.ds(row, 1)]
        share = 0.5 * (1.0 + lax.erf(units * (2.0 ** -0.5)))
        slope[step] = share + units * jnp.exp(-0.5 * units * units) * 0.3989422804014327
        start(slope.at[step], slope_out.at[step], out_sem)
        gated = (units * share).astype(BF16)
        active[step] = gated
        start(active.at[step], active_out.at[step], out_sem)
        start(whole.at[0, step], kept.at[0, step], out_sem)
        finish(whole.at[1, step], sems.at[1, step])
        start(whole.at[1, step], kept.at[1, step], out_sem)
        total = total + dot_nn(gated, whole[1, step])
    pre[...] = total
    out[...] = norm_rows(total, params[3 * norm + 1 : 3 * norm + 2], params[3 * norm + 2 : 3 * norm + 3])
    finish(slope, out_sem)
    finish(active, out_sem)
    finish(whole, out_sem)


def feed_backward_kernel(
    norm, place, grad_in, low_in, pre_in, slope_in, active_in, kept, params,
    out, small, keep, send, whole, grads, grad, low, pre, slope, active, row_sems, sems, out_sem,
):
    parts = whole.shape[1]
    start(grad_in, grad, row_sems.at[0])
    start(pre_in, pre, row_sems.at[1])
    for step in range(parts):
        start(active_in.at[step], active.at[step], row_sems.at[3 + step])
        start(kept.at[1, step], whole.at[1, step], sems.at[1, step])
        start(slope_in.at[step], slope.at[step], row_sems.at[3 + parts + step])
        if step == 0:
            start(low_in, low, row_sems.at[2])
        start(kept.at[0, step], whole.at[0, step], sems.at[0, step])
    finish(grad, row_sems.at[0])
    finish(pre, row_sems.at[1])
    grad_pre = norm_back(pre[...], params[3 * norm + 1 : 3 * norm + 2], grad[...], small)
    branch = grad_pre.astype(BF16)
    total = grad_pre
    for step in range(parts):
        finish(active.at[step], row_sems.at[3 + step])
        grads[1, step] = dot_tn(active[step], branch).astype(BF16)
        store_feed(place, grads, (keep, send), 1, step, out_sem)
        finish(whole.at[1, step], sems.at[1, step])
        finish(slope.at[step], row_sems.at[3 + parts + step])
        grad_units = (dot_nt(branch, whole[1, step]) * slope[step]).astype(BF16)
        if step == 0:
            finish(low, row_sems.at[2])
        grads[0, step] = dot_tn(low[...], grad_units).astype(BF16)
        store_feed(place, grads, (keep, send), 0, step, out_sem)
        small[pl.ds(3 + (place[1] + parts - step) % parts, 1)] = column_total(grad_units)
        finish(whole.at[0, step], sems.at[0, step])
        total = total + dot_nt(grad_units, whole[0, step])
    out[...] = total
    finish(grads, out_sem)


def feed_both_kernel(
    layer, norm, offset, n_parts, n_pieces, place, picks, rows_ref, first_weight, second_weight, *refs,
):
    arrived, pieces, refs = refs[:n_parts], refs[n_parts : n_parts + n_pieces], refs[n_parts + n_pieces :]
    bias, params, mixed, out, small, keep, send, whole, grads, slope, active, low, pre, grad, held, sems, row_sem, out_sem = refs
    parts = whole.shape[1]
    for step in range(parts):
        for half in range(2):
            load_feed(place, (first_weight, second_weight), pieces, offset, layer, half, step, whole, sems)
    pick_copies(picks, arrived, held, row_sem)
    stream = rows_ref[...]
    low[...] = stream.astype(BF16)
    total = params[3 * norm : 3 * norm + 1] + stream
    for step in range(parts):
        row = 6 + layer * parts + (place[1] + parts - step) % parts
        finish(whole.at[0, step], sems.at[0, step])
        units = dot_nn(low[...], whole[0, step]) + bias[pl.ds(row, 1)]
        share = 0.5 * (1.0 + lax.erf(units * (2.0 ** -0.5)))
        slope[step] = share + units * jnp.exp(-0.5 * units * units) * 0.3989422804014327
        gated = (units * share).astype(BF16)
        active[step] = gated
        finish(whole.at[1, step], sems.at[1, step])
        total = total + dot_nn(gated, whole[1, step])
    pre[...] = total
    gain, shift = params[3 * norm + 1 : 3 * norm + 2], params[3 * norm + 2 : 3 * norm + 3]
    leave_rows(norm_rows(total, gain, shift), mixed)
    finish(held, row_sem)
    flat_rows(held, grad)
    grad_pre = norm_back(pre[...], gain, grad[...], small)
    branch = grad_pre.astype(BF16)
    total = grad_pre
    for step in range(parts):
        grads[1, step] = dot_tn(active[step], branch).astype(BF16)
        store_feed(place, grads, (keep, send), 1, step, out_sem)
        grad_units = (dot_nt(branch, whole[1, step]) * slope[step]).astype(BF16)
        grads[0, step] = dot_tn(low[...], grad_units).astype(BF16)
        store_feed(place, grads, (keep, send), 0, step, out_sem)
        small[pl.ds(3 + (place[1] + parts - step) % parts, 1)] = column_total(grad_units)
        total = total + dot_nt(grad_units, whole[0, step])
    out[...] = total
    finish(grads, out_sem)


def finish_all(whole, sems):
    for mat in range(whole.shape[0]):
        finish(whole.at[mat], sems.at[mat])


def image_forward_kernel(
    layer, offset, image_offset, image_rows, n_pieces, place, images, image, inward, outward, *refs,
):
    pieces, refs = refs[:n_pieces], refs[n_pieces:]
    bias, projected, keys, value, kept_image, whole, whole_image, sems, image_sem, out_sem = refs
    load_image(place, image, pieces, image_offset, image_rows, whole_image, image_sem)
    load_attention(place, (inward, outward), pieces, offset, layer, whole, sems)
    finish(whole_image, image_sem)
    start(whole_image, kept_image, out_sem)
    size = images.shape[0] // 4
    last = bias.shape[0] - 1
    for first in range(0, images.shape[0], size):
        rows = slice(first, first + size)
        source = (dot_nt(images[rows], whole_image[...]) + bias[last : last + 1]).astype(BF16)
        projected[rows] = source
        if first == 0:
            finish_all(whole, sems)
        keys[rows] = dot_nt(source, whole[1]).astype(BF16)
        value[rows] = (dot_nt(source, whole[2]) + bias[2 * layer + 1 : 2 * layer + 2]).astype(BF16)
    finish(whole_image, out_sem)


def cross_forward_kernel(
    layer, norm, offset, seq, patches, n_pieces, place, rows_ref, keys, value, inward, outward, *refs,
):
    pieces, refs = refs[:n_pieces], refs[n_pieces:]
    bias, params, out, low, pre, query, context, kept, whole, mixed, sems, out_sem = refs
    load_attention(place, (inward, outward), pieces, offset, layer, whole, sems)
    stream = rows_ref[...]
    hb = stream.astype(BF16)
    low[...] = hb
    finish_all(whole, sems)
    start(whole, kept, out_sem)
    query[...] = (dot_nt(hb, whole[0]) + bias[2 * layer : 2 * layer + 1]).astype(BF16).astype(F32)
    count = stream.shape[0] // seq
    size = keys.shape[0] // count
    units = attention_units(count, seq, size, hb.shape[1])
    attend_forward(units, real_patch(size, patches), query, keys, value, mixed)
    context[...] = mixed[...].astype(BF16)
    total = dot_nn(context[...], whole[3]) + params[3 * norm : 3 * norm + 1] + stream
    pre[...] = total
    out[...] = norm_rows(total, params[3 * norm + 1 : 3 * norm + 2], params[3 * norm + 2 : 3 * norm + 3])
    finish(whole, out_sem)


def cross_backward_kernel(
    norm, seq, patches, place, grad, low, pre, query, context, keys, value, kept, params,
    out, small, grad_keys, grad_value, branch_out, query_out, whole, grad_context, grad_query, sems,
):
    load_kept(kept, whole, sems, (3, 0))
    grad_pre = norm_back(pre[...], params[3 * norm + 1 : 3 * norm + 2], grad[...], small)
    branch = grad_pre.astype(BF16)
    branch_out[...] = branch
    finish(whole.at[3], sems.at[3])
    grad_context[...] = dot_nt(branch, whole[3]).astype(BF16).astype(F32)
    count = branch.shape[0] // seq
    size = keys.shape[0] // count
    units = attention_units(count, seq, size, branch.shape[1])
    attend_backward(
        units, real_patch(size, patches), query, keys, value, grad_context, grad_query, grad_keys, grad_value
    )
    query_low = grad_query[...].astype(BF16)
    query_out[...] = query_low
    small[3:4] = column_total(query_low)
    small[4:5] = column_total(grad_value[...])
    finish(whole.at[0], sems.at[0])
    out[...] = grad_pre + dot_nn(query_low, whole[0])


def cross_weights_kernel(
    spot, place, context, branch, grad_query, low, grad_keys, grad_value, source, keep_held, send_held,
    keep, send, grads, out_sem,
):
    grads[3] = dot_tn(context[...], branch[...]).astype(BF16)
    grads[0] = dot_tn(grad_query[...], low[...]).astype(BF16)
    grads[1] = dot_tn(grad_keys[...], source[...]).astype(BF16)
    grads[2] = dot_tn(grad_value[...], source[...]).astype(BF16)
    store_attention(place, grads, (keep, send), spot, out_sem)
    finish(grads, out_sem)


def image_backward_kernel(
    image_rows, spot, n_held, place, images, grad_keys, grad_value, kept, kept_image, *refs,
):
    out, small, keep, send, whole, whole_image, grads, low, sems, image_sem, out_sem = refs[n_held:]
    load_kept(kept, whole, sems, (1, 2))
    start(kept_image, whole_image, image_sem)
    finish(whole.at[1], sems.at[1])
    finish(whole.at[2], sems.at[2])
    finish(whole_image, image_sem)
    patches, count = out.shape[:2]
    size = images.shape[0] // count
    small[...] = jnp.zeros_like(small)
    for row in range(count):
        rows = slice(row * size, (row + 1) * size)
        source = dot_nn(grad_keys[rows], whole[1]) + dot_nn(grad_value[rows], whole[2])
        source = source.astype(BF16)
        low[rows] = source
        out[:, row, :] = dot_nn(source, whole_image[...])[:patches]
    grads[...] = dot_tn(low[...], images[...]).astype(BF16)
    store_image(place, grads, (keep, send), spot, image_rows, out_sem)
    small[0:1] = column_total(low[...])
    finish(grads, out_sem)


def combine_kernel(
    keep, core, one0, one1, two0, two1, own, down, across, up, kept, arrived, first, second, sems,
):
    for half, (one, two) in enumerate(((one0, two0), (one1, two1))):
        start(keep.at[half, 0], kept.at[half], sems.at[0])
        start(core.at[half, 0], arrived.at[half], sems.at[1])
        start(one.at[0], first.at[half], sems.at[2])
        start(two, second.at[half], sems.at[3])
    for number, target in enumerate((kept, arrived, first, second)):
        finish(target, sems.at[number])
    for step, target in enumerate((own, down, across, up)):
        for half in range(2):
            total = kept[half, step].astype(F32) + arrived[half, step].astype(F32)
            total = total + first[half, step].astype(F32) + second[half, step].astype(F32)
            target[half] = total.astype(target.dtype)


def pick_kernel(picks, *refs):
    *parts, out, held, sem = refs
    pick_copies(picks, parts, held, sem)
    finish(held, sem)
    out[...] = held[...].astype(out.dtype)


def finish_kernel(blocks, quarter, names, held, n_results, place, *refs):
    results, refs = refs[:n_results], refs[n_results:]
    width = results[0].shape[3]
    targets = dict(zip(names, refs[held:]))
    scratch = refs[held + len(names) :]
    sem, out_sem = scratch[-2:]
    for number, (kind, offset, _) in enumerate(blocks):
        buffer = scratch[2 * number]
        for core in range(2):
            for half in range(2):
                for entry in range(4):
                    if n_results == 1:
                        slot = core ^ DISTANCES[half][entry]
                        piece = results[0].at[slot, half]
                    else:
                        slot = place[0] ^ (core ^ DISTANCES[half][entry])
                        piece = piece_of(results, core, half, entry)
                    if kind == ATTENTION:
                        rows = quarter // 4
                        spot = attention_spot(buffer, quarter, half, slot, 0)
                        start(piece.at[pl.ds(offset, rows)], spot, sem.at[number])
                    elif kind == FEED:
                        rows = buffer.shape[1] // SLICES
                        spot = buffer.at[half, aligned(slot * rows, rows)]
                        start(piece.at[pl.ds(offset, rows)], spot, sem.at[number])
                    else:
                        rows = quarter * buffer.shape[1] // width // SLICES // 2
                        piece = piece.at[pl.ds(offset, rows)]
                        image_copies(buffer, piece, quarter, half, slot, 0, sem.at[number], True)
    for number, (kind, _, layer) in enumerate(blocks):
        buffer, wide = scratch[2 * number : 2 * number + 2]
        done = out_sem.at[number]
        finish(buffer, sem.at[number])
        wide[...] = buffer[...].astype(F32)
        if kind == ATTENTION:
            start(wide.at[pl.ds(0, 3)], targets[ATTENTION_IN].at[layer], done)
            start(wide.at[3], targets[ATTENTION_OUT].at[layer], done)
        elif kind == FEED:
            start(wide.at[0], targets[FEED_IN].at[layer], done)
            start(wide.at[1], targets[FEED_OUT].at[layer], done)
        else:
            start(wide, targets[IMAGE], done)
    for number in range(len(blocks)):
        finish(scratch[2 * number + 1], out_sem.at[number])


def shape(dims, kind=F32):
    return jax.ShapeDtypeStruct(tuple(dims), kind)


def call(kernel, ins, outs, scratch, aliases=None):
    return pl.pallas_call(
        kernel,
        in_specs=[spec for _, spec in ins],
        out_specs=[spec for _, spec in outs],
        out_shape=[s for s, _ in outs],
        scratch_shapes=scratch,
        input_output_aliases=aliases or {},
        compiler_params=pltpu.CompilerParams(vmem_limit_bytes=60 << 20),
        cost_estimate=pl.CostEstimate(flops=0, bytes_accessed=0, transcendentals=0),
    )(*[v for v, _ in ins])


class Ring:
    def __init__(self, at, name, own):
        self.at, self.name = at, name
        at[name] = {0: own}

    def up(self):
        parts = self.at[self.name]
        parts[1] = pass_on(parts[0])

    def down(self):
        parts = self.at[self.name]
        parts[3] = pass_on(parts[0], -1)

    def far(self):
        parts = self.at[self.name]
        parts[2] = pass_on(parts[1])

    def direct(self):
        parts = self.at[self.name]
        for way in (1, 2, 3):
            parts[way] = pass_on(parts[0], way)

    def take(self):
        parts = self.at.pop(self.name)
        return [parts[i] for i in range(4)]


class Widen:
    def __init__(self, at, name, first, second):
        self.at, self.name = at, name
        at[name] = {"own": (first, second)}

    def one(self):
        held = self.at[self.name]
        first, second = held.pop("own")
        held["both"] = (first, swap(first, 2), second, swap(second, 4))

    def two(self):
        held = self.at[self.name]
        both = held.pop("both")
        near = jnp.stack(both[:2]), jnp.stack(both[2:])
        held["near"] = near
        held["far"] = swap(near[0], 4), swap(near[1], 2)

    def direct(self):
        held = self.at[self.name]
        own = held.pop("own")
        held["lines"] = [jnp.stack(own)] + [swap(jnp.stack(own), bit) for bit in (2, 4, 6)]

    def two_early(self):
        self.two()
        held = self.at[self.name]
        held["near all"] = jnp.stack(held.pop("near"))
        held["near core"] = swap(held["near all"], 1)

    def core_late(self):
        held = self.at[self.name]
        held["far all"] = jnp.stack(held.pop("far"))
        held["far core"] = swap(held["far all"], 1)

    def core_direct(self):
        held = self.at[self.name]
        lines = held.pop("lines")
        order = [[distance // 2 for distance in half] for half in DISTANCES]
        held["all"] = jnp.stack([jnp.stack([lines[i][half] for i in order[half]]) for half in range(2)])
        held["core"] = swap(held["all"], 1)

    def core(self):
        held = self.at[self.name]
        near, far = held.pop("near"), held.pop("far")
        held["all"] = jnp.stack([jnp.concatenate([near[half], far[half]]) for half in range(2)])
        held["core"] = swap(held["all"], 1)

    def take(self):
        held = self.at.pop(self.name)
        if "all" in held:
            return held["all"], held["core"]
        return held["near all"], held["far all"], held["near core"], held["far core"]


class Reduce:
    def __init__(self, at, name, keep, send):
        self.at, self.name = at, name
        at[name] = {"keep": keep, "send": send}

    def core(self):
        held = self.at[self.name]
        held["core"] = swap(held.pop("send"), 1)

    def one(self):
        held = self.at[self.name]
        keep, core = held["keep"], held["core"]
        held["one"] = swap(added(keep[0, 2:], core[0, 2:]), 4), swap(added(keep[1, 2:], core[1, 2:]), 2)

    def two(self):
        held = self.at[self.name]
        keep, core, one = held["keep"], held["core"], held["one"]
        held["two"] = (
            swap(added(keep[0, 1], core[0, 1], one[0][1]), 2),
            swap(added(keep[1, 1], core[1, 1], one[1][1]), 4),
        )

    def combine(self):
        held = self.at[self.name]
        arrays = [held[name] for name in ("keep", "core")] + list(held["one"]) + list(held["two"])
        rows, width = arrays[0].shape[3:]
        mp = arrays[0].shape[2]
        outs = [shape((2, rows, width), kind) for kind in (F32, BF16, BF16, F32)]
        parts = call(
            combine_kernel,
            [(v, ANY) for v in arrays],
            [(v, VMEM) for v in outs],
            [pltpu.VMEM((2, mp, rows, width), BF16)] * 4 + [pltpu.SemaphoreType.DMA((4,))],
        )
        self.at[self.name] = {"own": parts[0], "parts": parts[1:]}

    def join(self, other):
        theirs = self.at.pop(other.name)
        held = self.at[self.name]
        held["own"] = jnp.concatenate([held["own"], theirs["own"]], axis=1)
        held["parts"] = [jnp.concatenate(pair, axis=1) for pair in zip(held["parts"], theirs["parts"])]

    def far(self):
        held = self.at[self.name]
        held["far"] = pass_on(held["parts"][1])

    def near(self):
        held = self.at[self.name]
        down, _, up = held.pop("parts")
        held["up"] = pass_on(added(up, held.pop("far")))
        held["down"] = pass_on(down, -1)

    def direct(self):
        held = self.at[self.name]
        down, across, up = held.pop("parts")
        held["up"], held["across"], held["down"] = pass_on(added(up)), pass_on(across, 2), pass_on(down, -1)

    def owned(self):
        held = self.at.pop(self.name)
        own = added(held["own"], *[held[name] for name in ("up", "across", "down") if name in held])
        bit = SLICES
        while bit < lax.axis_size("dp"):
            own = added(own, swap(own, bit))
            bit *= 2
        return own


def on_device(
    tokens, images, segment_of_token, image_of_row, attention_in, query_value_bias, attention_out, output_bias,
    feed_in, feed_bias, feed_out, image_weight, image_bias, norm_gain, norm_bias, cotangent,
):
    mp = lax.axis_size("mp")
    slot = lax.axis_index("dp") % SLICES
    owner = lax.axis_index("mp")
    place = jnp.stack([slot, owner]).astype(jnp.int32)
    own_rows, seq, width = tokens.shape
    group_rows = segment_of_token.shape[0]
    patches, image_width = images.shape[1:]
    quarter = attention_in.shape[3]
    units = feed_in.shape[2]
    n_tokens = own_rows * seq
    inward = attention_in.transpose(0, 1, 3, 2)
    image = image_weight.T

    attention_rows = quarter // 4
    feed_rows = units // SLICES
    image_rows = quarter * image_width // width // SLICES // 2

    token_shape = shape((n_tokens, width))
    token_low = shape((n_tokens, width), BF16)
    row_low = shape((own_rows, seq, width), BF16)
    inner_shape = shape((mp, n_tokens, units))
    inner_low = shape((mp, n_tokens, units), BF16)
    padded = -(-patches // 16) * 16
    n_patches = own_rows * padded
    patch_low = shape((n_patches, width), BF16)
    small_shape = shape((8, width))
    attention_grad = shape((2, 4, mp, attention_rows, width), BF16)
    feed_grad = shape((2, 4, mp, feed_rows, width), BF16)
    image_grad = shape((2, 4, mp, image_rows, width), BF16)
    kept_square = shape((4, width, width), BF16)
    kept_wide = shape((2, mp, units, width), BF16)
    kept_tall = shape((width, image_width), BF16)
    square = pltpu.VMEM((4, width, width), BF16)
    wide = pltpu.VMEM((2, mp, units, width), BF16)
    tall = pltpu.VMEM((width, image_width), BF16)
    token_f32 = pltpu.VMEM((n_tokens, width), F32)
    token_bf16 = pltpu.VMEM((n_tokens, width), BF16)
    row_bf16 = pltpu.VMEM((own_rows, seq, width), BF16)
    inner_f32 = pltpu.VMEM((mp, n_tokens, units), F32)
    inner_bf16 = pltpu.VMEM((mp, n_tokens, units), BF16)
    dma = pltpu.SemaphoreType.DMA
    matmul = 2 * n_tokens * width * width
    patch_matmul = 2 * n_patches * width * width

    local_order = image_of_row % group_rows
    here = owner * own_rows + jnp.arange(own_rows, dtype=jnp.int32)
    chosen = (local_order[None, :] == here[:, None]).astype(jnp.int32)
    source_row = jnp.sum(chosen * jnp.arange(group_rows, dtype=jnp.int32)[None, :], axis=1)
    picks_in = ((owner - source_row // own_rows) % mp) * own_rows + source_row % own_rows
    mine = (jnp.arange(group_rows, dtype=jnp.int32)[None, :] == here[:, None]).astype(jnp.int32)
    image_row = jnp.sum(mine * local_order[None, :], axis=1)
    picks_out = ((owner - image_row // own_rows) % mp) * own_rows + image_row % own_rows
    segments = jnp.sum(chosen[:, :, None] * segment_of_token[None], axis=1)
    code = jnp.arange(own_rows, dtype=jnp.int32)[:, None] * seq + segments
    code_col = code.reshape(n_tokens, 1)
    code_row = code.reshape(own_rows // 2, 2 * seq)

    first_rows = 2 * attention_rows + image_rows
    first, second, third = call(
        slice_kernel,
        [(place, SMEM)]
        + [(v, VMEM) for v in (query_value_bias.reshape(6, quarter), feed_bias, image_bias.reshape(1, quarter))]
        + [(v, ANY) for v in (inward, attention_out, feed_in, feed_out, image)],
        [
            (shape((2, rows, width), BF16), VMEM)
            for rows in (first_rows + 16, feed_rows + attention_rows, feed_rows)
        ],
        [dma((3,))],
    )

    at = {}

    def step():
        done = lax.optimization_barrier(at)
        at.clear()
        at.update(done)

    rings = {
        name: Ring(at, name, own)
        for name, own in (
            ("first", first), ("second", second), ("third", third), (TOKENS, tokens), (COTANGENT, cotangent),
        )
    }

    def gathered(name, rows=None):
        parts = rings[name].take()[1:]
        return Widen(at, name, *[jnp.stack([part[half, :rows] for part in parts]) for half in range(2)])

    rings["first"].direct()
    step()

    parts = [part[0, first_rows:] for part in at["first"].values()]
    ordered = jnp.stack(parts)[(owner - jnp.arange(mp)) % mp].astype(F32)
    bias = jnp.concatenate(
        [
            ordered[:, :6, :quarter].transpose(1, 0, 2).reshape(6, width),
            ordered[:, 6:8].transpose(1, 0, 2).reshape(2 * mp, width),
            ordered[:, 8, :quarter].reshape(1, width),
        ]
    )
    params = jnp.stack([output_bias, norm_gain, norm_bias], axis=1).astype(F32).reshape(-1, width)
    patch_rows = jnp.pad(images, ((0, 0), (0, padded - patches), (0, 0))).reshape(n_patches, image_width)
    at["tables"] = bias, params, code_col, code_row, picks_in, picks_out, image_row, patch_rows
    first_wide = gathered("first", first_rows)
    first_wide.one()
    rings["second"].up()
    rings["second"].down()
    step()
    bias, params, code_col, code_row, picks_in, picks_out, image_row, patch_rows = at.pop("tables")
    first_wide.two()
    rings["second"].far()
    rings[TOKENS].up()
    rings["third"].up()
    step()
    second_wide = gathered("second")
    first_wide.core()
    second_wide.one()
    rings[TOKENS].down()
    rings["third"].down()
    step()

    attention_pieces = [None, None, None]
    attention_at = [0, feed_rows, attention_rows]
    feed_pieces = [None, None]
    feed_at = [0, 0]

    def attention_ins(layer):
        return [(inward, ANY), (attention_out, ANY)] + [(piece, ANY) for piece in attention_pieces[layer]]

    def feed_ins(layer):
        return [(feed_in, ANY), (feed_out, ANY)] + [(piece, ANY) for piece in feed_pieces[layer]]

    def first_forward(layer, norm, parts):
        picked = len(parts) > 1
        return call(
            partial(self_forward_kernel, layer, norm, attention_at[layer], len(parts), len(attention_pieces[layer])),
            [(place, SMEM), (picks_in, SMEM)]
            + [(part, ANY if picked else VMEM) for part in parts]
            + attention_ins(layer)
            + [(bias, VMEM), (params, VMEM), (code_col, VMEM), (code_row, VMEM)],
            [(token_shape, VMEM), (token_low, VMEM), (token_shape, VMEM)] + [(token_low, VMEM)] * 4 + [(kept_square, ANY)],
            [square, dma((4,)), dma] + ([row_bf16, token_f32, dma] if picked else []),
        )

    def self_backward(norm, grad, kept, leave, spot, rows, held):
        _, low, pre, query, keys, value, context, weights = kept
        grads = shape((2, 4, mp, rows, width), BF16)
        ins = [(place, SMEM)] + [(v, VMEM) for v in (grad, low, pre, query, keys, value, context)]
        ins += [(weights, ANY), (params, VMEM), (code_col, VMEM), (code_row, VMEM)]
        return call(
            partial(self_backward_kernel, leave, norm, spot, len(held)),
            ins + [(v, ANY) for v in held],
            [(row_low if leave else token_shape, VMEM), (small_shape, VMEM)] + [(grads, ANY)] * 2,
            [square, square] + [token_bf16] * 4 + [dma((4,)), dma],
            {len(ins) + i: 2 + i for i in range(len(held))},
        )

    def feed_self_forward(layer, norm, next_layer, next_norm, rows):
        pieces, following = feed_pieces[layer], attention_pieces[next_layer]
        outs = call(
            partial(
                feed_self_forward_kernel, layer, norm, feed_at[layer], next_layer, next_norm, attention_at[next_layer],
                len(pieces), len(following),
            ),
            [(place, SMEM), (rows, VMEM)]
            + [(v, ANY) for v in (feed_in, feed_out, inward, attention_out, *pieces, *following)]
            + [(bias, VMEM), (params, VMEM), (code_col, VMEM), (code_row, VMEM)],
            [(token_shape, VMEM), (token_low, VMEM), (token_shape, VMEM)]
            + [(inner_shape, ANY), (inner_low, ANY), (kept_wide, ANY)]
            + [(token_shape, VMEM), (token_low, VMEM), (token_shape, VMEM)]
            + [(token_low, VMEM)] * 4
            + [(kept_square, ANY)],
            [wide, inner_f32, inner_bf16, dma((2, mp)), dma, square, dma((4,)), dma],
        )
        return outs[:6], outs[6:]

    def feed_backward(norm, grad, kept):
        _, low, pre, slope, active, weights = kept
        return call(
            partial(feed_backward_kernel, norm),
            [(place, SMEM)] + [(v, ANY) for v in (grad, low, pre, slope, active, weights)] + [(params, VMEM)],
            [(token_shape, VMEM), (small_shape, VMEM)] + [(feed_grad, ANY)] * 2,
            [wide, wide, token_f32, token_bf16, token_f32, inner_f32, inner_bf16]
            + [dma((3 + 2 * mp,)), dma((2, mp)), dma],
        )

    def feed_both(layer, norm, rows, parts):
        return call(
            partial(feed_both_kernel, layer, norm, feed_at[layer], len(parts), len(feed_pieces[layer])),
            [(place, SMEM), (picks_in, SMEM), (rows, VMEM), (feed_in, ANY), (feed_out, ANY)]
            + [(v, ANY) for v in parts + list(feed_pieces[layer])]
            + [(bias, VMEM), (params, VMEM)],
            [(row_low, VMEM), (token_shape, VMEM), (small_shape, VMEM)] + [(feed_grad, ANY)] * 2,
            [wide, wide, inner_f32, inner_bf16, token_bf16, token_f32, token_f32, row_bf16]
            + [dma((2, mp)), dma, dma],
        )

    def pick_rows(parts):
        return call(
            pick_kernel,
            [(picks_out, SMEM)] + [(part, ANY) for part in parts],
            [(shape((own_rows, seq, width)), VMEM)],
            [row_bf16, dma],
        )[0]

    attention_pieces[0] = attention_pieces[2] = first_wide.take()
    second_wide.two_early()
    rings[TOKENS].far()
    rings["third"].far()
    projected, image_keys, image_value, kept_image = call(
        partial(image_forward_kernel, 2, attention_rows, 2 * attention_rows, image_rows, len(attention_pieces[2])),
        [(place, SMEM), (patch_rows, VMEM), (image, ANY)] + attention_ins(2) + [(bias, VMEM)],
        [(patch_low, VMEM)] * 3 + [(kept_tall, ANY)],
        [square, tall, dma((4,)), dma, dma],
    )
    at["keys"] = image_keys
    step()

    text_attention = first_forward(0, 0, rings[TOKENS].take())
    at["stream"] = text_attention[0]
    second_wide.core_late()
    third_wide = gathered("third")
    third_wide.one()
    rings[COTANGENT].up()
    step()

    attention_pieces[1] = feed_pieces[0] = second_wide.take()
    third_wide.two()
    rings[COTANGENT].down()
    text_feed, joining_attention = feed_self_forward(0, 1, 1, 2, at.pop("stream"))
    at["stream"] = joining_attention[0]
    step()

    third_wide.core()
    rings[COTANGENT].far()
    image_keys = at.pop("keys")
    cross_attention = call(
        partial(cross_forward_kernel, 2, 3, attention_rows, seq, patches, len(attention_pieces[2])),
        [(place, SMEM), (at.pop("stream"), VMEM), (image_keys, VMEM), (image_value, VMEM)]
        + attention_ins(2)
        + [(bias, VMEM), (params, VMEM)],
        [(token_shape, VMEM), (token_low, VMEM), (token_shape, VMEM), (token_shape, VMEM), (token_low, VMEM)]
        + [(kept_square, ANY)],
        [square, token_f32, dma((4,)), dma],
    )
    at["stream"] = cross_attention[0]
    step()

    feed_pieces[1] = third_wide.take()

    mixed, grad, small_joining_feed, keep, send = feed_both(1, 4, at.pop("stream"), rings[COTANGENT].take())
    mixed_ring = Ring(at, "mixed", mixed)
    at["grad"] = grad
    last_grads = Reduce(at, "last", keep, send)
    step()

    last_grads.core()
    mixed_ring.up()
    grad, small_cross, grad_keys, grad_value, cross_branch, cross_query = call(
        partial(cross_backward_kernel, 3, seq, patches),
        [(place, SMEM), (at.pop("grad"), VMEM)]
        + [(cross_attention[i], VMEM) for i in (1, 2, 3, 4)]
        + [(image_keys, VMEM), (image_value, VMEM), (cross_attention[5], ANY), (params, VMEM)],
        [(token_shape, VMEM), (small_shape, VMEM)] + [(patch_low, VMEM)] * 2 + [(token_low, VMEM)] * 2,
        [square, token_f32, token_f32, dma((4,))],
    )
    at["grad"] = grad
    step()

    last_grads.one()
    mixed_ring.down()
    middle_rows = 2 * attention_rows
    grad, small_joining, keep, send = self_backward(
        2, at.pop("grad"), joining_attention, False, attention_rows, middle_rows, ()
    )
    at["grad"] = grad
    cross_grads = (cross_attention[4], cross_branch, cross_query, cross_attention[1], grad_keys, grad_value, projected)
    keep, send = call(
        partial(cross_weights_kernel, 0),
        [(place, SMEM)] + [(v, VMEM) for v in cross_grads] + [(keep, ANY), (send, ANY)],
        [(shape(keep.shape, BF16), ANY)] * 2,
        [square, dma],
        {8: 0, 9: 1},
    )
    middle_grads = Reduce(at, "middle", keep, send)
    at["patch grads"] = grad_keys, grad_value
    step()

    last_grads.two()
    middle_grads.core()
    mixed_ring.far()
    grad, small_text_feed, keep, send = feed_backward(1, at.pop("grad"), text_feed)
    at["grad"] = grad
    first_grads = Reduce(at, "first", keep, send)
    step()

    mixed_parts = mixed_ring.take()
    middle_grads.one()
    first_grads.core()
    last_grads.combine()
    held = at["last"]
    down, across, up = held.pop("parts")
    held["up"], held["down"] = pass_on(up.astype(BF16)), pass_on(down, -1)
    held["across part"] = across
    rows_back, small_text, keep, send = self_backward(
        0, at.pop("grad"), text_attention, True, 0, attention_rows + image_rows, ()
    )
    back_ring = Ring(at, "back", rows_back)
    at["text"] = keep, send
    step()

    middle_grads.two()
    first_grads.one()
    at["last"]["across"] = pass_on(at["last"].pop("across part"), 2)
    grad_keys, grad_value = at.pop("patch grads")
    keep, send = at.pop("text")
    grad_images, small_image, keep, send = call(
        partial(image_backward_kernel, image_rows, attention_rows, 2),
        [(place, SMEM), (patch_rows, VMEM), (grad_keys, VMEM), (grad_value, VMEM), (cross_attention[5], ANY)]
        + [(kept_image, ANY), (keep, ANY), (send, ANY)],
        [(shape((patches, own_rows, image_width)), VMEM), (small_shape, VMEM)] + [(shape(keep.shape, BF16), ANY)] * 2,
        [square, tall, tall, pltpu.VMEM((n_patches, width), BF16), dma((4,)), dma, dma],
        {6: 2, 7: 3},
    )
    text_grads = Reduce(at, "text", keep, send)
    at[SMALL] = jnp.concatenate(
        [small_text, small_text_feed, small_joining, small_cross, small_joining_feed, small_image]
    )
    step()

    first_grads.two()
    text_grads.core()
    middle_grads.combine()
    middle_grads.far()
    back_ring.up()
    step()

    text_grads.one()
    middle_grads.near()
    first_grads.combine()
    first_grads.far()
    at[SMALL] = at[SMALL] + swap(at[SMALL], 1)
    at["last own"] = last_grads.owned()
    step()

    early = Widen(at, "early", *jnp.concatenate([at.pop("last own"), middle_grads.owned()], axis=1))
    early.one()
    text_grads.two()
    first_grads.near()
    back_ring.down()
    at[SMALL] = at[SMALL] + swap(at[SMALL], 2)
    step()

    early.two()
    text_grads.combine()
    text_grads.direct()
    at["first own"] = first_grads.owned()
    at[SMALL] = at[SMALL] + swap(at[SMALL], 4)
    step()

    late = Widen(at, "late", *jnp.concatenate([at.pop("first own"), text_grads.owned()], axis=1))
    late.one()
    at["mixed"] = pick_rows(mixed_parts)
    early.core()
    back_ring.far()
    at[SMALL] = at[SMALL] + swap_owner(at[SMALL], 1)
    step()

    late.two()
    at[TOKENS] = pick_rows(back_ring.take())
    early_pieces = early.take()
    smalls = at.pop(SMALL)
    smalls = smalls + swap_owner(smalls, 2)
    bit = SLICES
    while bit < lax.axis_size("dp"):
        smalls = smalls + swap(smalls, bit)
        bit *= 2
    at[SMALL] = smalls

    whole_shapes = {
        ATTENTION_IN: shape(inward.shape),
        ATTENTION_OUT: shape(attention_out.shape),
        FEED_IN: shape(feed_in.shape),
        FEED_OUT: shape(feed_out.shape),
        IMAGE: shape(image.shape),
    }
    block_of = {ATTENTION: (4, quarter, width), FEED: (2, units, width), IMAGE: (quarter, image_width)}
    names_of = {ATTENTION: [ATTENTION_IN, ATTENTION_OUT], FEED: [FEED_IN, FEED_OUT], IMAGE: [IMAGE]}
    written = {}

    def write_out(result, *blocks):
        names = list(dict.fromkeys(name for kind, _, _ in blocks for name in names_of[kind]))
        names = [name for name in names if name in written] + [name for name in names if name not in written]
        held = [name for name in names if name in written]
        scratch = [pltpu.VMEM(block_of[kind], form) for kind, _, _ in blocks for form in (BF16, F32)]
        results = call(
            partial(finish_kernel, blocks, quarter, names, len(held), len(result)),
            [(place, SMEM)] + [(v, ANY) for v in result] + [(written[name], ANY) for name in held],
            [(whole_shapes[name], ANY) for name in names],
            scratch + [dma((len(blocks),)), dma((len(blocks),))],
            {1 + len(result) + i: i for i in range(len(held))},
        )
        written.update(zip(names, results))

    write_out(
        early_pieces, (FEED, 0, 1), (ATTENTION, feed_rows, 2), (ATTENTION, feed_rows + attention_rows, 1)
    )
    at["written"] = written
    step()
    written = at.pop("written")
    late.core()
    smalls = at.pop(SMALL).reshape(6, 8, width)

    def own_part(values):
        return lax.dynamic_slice_in_dim(values, owner * quarter, quarter, axis=values.ndim - 1)

    grad_query_value_bias = own_part(jnp.stack([smalls[i, 3:5] for i in (0, 2, 3)]))
    grad_feed_bias = jnp.stack([smalls[i, 3 : 3 + mp].reshape(-1) for i in (1, 4)])
    grad_feed_bias = lax.dynamic_slice_in_dim(grad_feed_bias, owner * units, units, axis=1)
    vectors = (
        grad_query_value_bias, smalls[:5, 2], grad_feed_bias, own_part(smalls[5, 0]), smalls[:5, 0], smalls[:5, 1]
    )
    at["vectors"] = vectors
    step()
    vectors = at.pop("vectors")
    write_out(
        late.take(), (FEED, 0, 0), (ATTENTION, feed_rows, 0), (IMAGE, feed_rows + attention_rows, 0)
    )
    return (
        at["mixed"],
        at[TOKENS],
        grad_images.transpose(1, 0, 2),
        written[ATTENTION_IN].transpose(0, 1, 3, 2),
        vectors[0],
        written[ATTENTION_OUT],
        vectors[1],
        written[FEED_IN],
        vectors[2],
        written[FEED_OUT],
        written[IMAGE].T,
        vectors[3],
        vectors[4],
        vectors[5],
    )


def solution(mesh):
    rows = P(("dp", "mp"), None, None)
    return jax.shard_map(
        on_device,
        mesh=mesh,
        in_specs=(
            rows,
            rows,
            P("dp", None),
            P("dp"),
            P(None, None, None, "mp"),
            P(None, None, "mp"),
            P(None, "mp", None),
            P(),
            P(None, None, "mp"),
            P(None, "mp"),
            P(None, "mp", None),
            P(None, "mp"),
            P("mp"),
            P(),
            P(),
            rows,
        ),
        out_specs=(
            rows,
            rows,
            rows,
            P(None, None, None, "mp"),
            P(None, None, "mp"),
            P(None, "mp", None),
            P(),
            P(None, None, "mp"),
            P(None, "mp"),
            P(None, "mp", None),
            P(None, "mp"),
            P("mp"),
            P(),
            P(),
        ),
        check_vma=False,
    )
```

```python
from functools import partial

import jax
import jax.numpy as jnp
from jax import lax
from jax.experimental import pallas as pl
from jax.experimental.pallas import tpu as pltpu
from jax.sharding import PartitionSpec as P

HEAD_DIM = 64
STACK = 4 * HEAD_DIM
TOGETHER = 6
SLICES = 8
EPSILON = 1e-06
BLOCKED = -1000000000.0
SCALE = HEAD_DIM ** (-0.5)
DISTANCES = ((0, 2, 4, 6), (0, 4, 2, 6))
ATTENTION, FEED, IMAGE, ATTENTION_IN, ATTENTION_OUT, FEED_IN, FEED_OUT = range(7)
SMALL, TOKENS, COTANGENT = "small", "tokens", "cotangent"
F32 = jnp.float32
BF16 = jnp.bfloat16

ANY = pl.BlockSpec(memory_space=pl.ANY)
VMEM = pl.BlockSpec(memory_space=pltpu.VMEM)
SMEM = pl.BlockSpec(memory_space=pltpu.SMEM)


def swap(values, bit):
    count = lax.axis_size("dp")
    return lax.ppermute(values, "dp", [(i, i ^ bit) for i in range(count)])


def pass_on(values, way=1):
    count = lax.axis_size("mp")
    return lax.ppermute(values, "mp", [(i, (i + way) % count) for i in range(count)])


def swap_owner(values, bit):
    count = lax.axis_size("mp")
    return lax.ppermute(values, "mp", [(i, i ^ bit) for i in range(count)])


def added(*terms):
    total = terms[0].astype(F32)
    for term in terms[1:]:
        total = total + term
    return total.astype(BF16)


def dot_nn(left, right):
    return lax.dot_general(left, right, (((1,), (0,)), ((), ())), preferred_element_type=F32)


def dot_nt(left, right):
    return lax.dot_general(left, right, (((1,), (1,)), ((), ())), preferred_element_type=F32)


def dot_tn(left, right):
    return lax.dot_general(left, right, (((0,), (0,)), ((), ())), preferred_element_type=F32)


def start(source, target, sem):
    pltpu.make_async_copy(source, target, sem).start()


def finish(whole, sem):
    pltpu.make_async_copy(whole, whole, sem).wait()


def aligned(first, count, step=16):
    return pl.ds(pl.multiple_of(first, step), count)


def each_slice(place, first_step, mp):
    for core in range(2):
        for half in range(2):
            for entry in range(4):
                slot = place[0] ^ (core ^ DISTANCES[half][entry])
                for step in range(first_step, mp):
                    yield core, half, entry, step, slot, (place[1] + mp - step) % mp


def piece_of(pieces, core, half, entry):
    if len(pieces) == 2:
        return pieces[core].at[half, entry]
    return pieces[2 * core + entry // 2].at[half, entry % 2]


def attention_spot(whole, quarter, half, slot, owner):
    span = 4 * quarter // SLICES
    count = quarter // span
    row = owner * quarter + (slot % count) * span + half * (span // 2)
    return whole.at[slot // count, aligned(row, span // 2)]


def load_attention(place, own, pieces, offset, layer, whole, sems):
    mp = pieces[0].shape[2] + 1
    quarter = whole.shape[1] // mp
    rows = quarter // 4
    for mat in range(4):
        source = own[0].at[layer, mat] if mat < 3 else own[1].at[layer]
        start(source, whole.at[mat, aligned(place[1] * quarter, quarter)], sems.at[mat])
    for core, half, entry, step, slot, owner in each_slice(place, 1, mp):
        start(
            piece_of(pieces, core, half, entry).at[step - 1, pl.ds(offset, rows)],
            attention_spot(whole, quarter, half, slot, owner),
            sems.at[slot // 2],
        )


def store_attention(place, whole, outs, offset, sem):
    mp = outs[0].shape[2]
    quarter = whole.shape[1] // mp
    for core, half, entry, step, slot, owner in each_slice(place, 0, mp):
        start(
            attention_spot(whole, quarter, half, slot, owner),
            outs[core].at[half, entry, step, pl.ds(offset, quarter // 4)],
            sem,
        )


def feed_spot(whole, half, slot, step):
    span = whole.shape[2] // SLICES
    return whole.at[half, step, aligned(slot * span, span)]


def load_feed(place, own, pieces, offset, layer, half, step, whole, sems):
    rows = whole.shape[2] // SLICES
    if step == 0:
        start(own[half].at[layer], whole.at[half, 0], sems.at[half, 0])
        return
    for core in range(2):
        for entry in range(4):
            slot = place[0] ^ (core ^ DISTANCES[half][entry])
            start(
                piece_of(pieces, core, half, entry).at[step - 1, pl.ds(offset, rows)],
                feed_spot(whole, half, slot, step),
                sems.at[half, step],
            )


def store_feed(place, whole, outs, half, step, sem):
    for core in range(2):
        for entry in range(4):
            slot = place[0] ^ (core ^ DISTANCES[half][entry])
            start(feed_spot(whole, half, slot, step), outs[core].at[half, entry, step], sem)


def image_copies(whole, piece, quarter, half, slot, owner, sem, inward):
    rows, width = piece.shape
    span = 2 * rows
    beyond = whole.shape[1] - width
    blocks = width // beyond
    plain = quarter // span
    base = owner * quarter + half * rows

    def move(inner, outer):
        start(inner, outer, sem) if inward else start(outer, inner, sem)

    @pl.when(slot < plain)
    def _():
        move(piece, whole.at[aligned(base + slot * span, rows), pl.ds(0, width)])

    @pl.when(slot >= plain)
    def _():
        for block in range(blocks):
            row = base + block * (quarter // blocks) + (slot - plain) * span
            move(
                piece.at[:, pl.ds(block * beyond, beyond)],
                whole.at[aligned(row, rows), pl.ds(width, beyond)],
            )


def load_image(place, own, pieces, offset, rows, whole, sem):
    mp = pieces[0].shape[2] + 1
    quarter = whole.shape[0] // mp
    start(own, whole.at[aligned(place[1] * quarter, quarter)], sem)
    for core, half, entry, step, slot, owner in each_slice(place, 1, mp):
        piece = piece_of(pieces, core, half, entry).at[step - 1, pl.ds(offset, rows)]
        image_copies(whole, piece, quarter, half, slot, owner, sem, True)


def store_image(place, whole, outs, offset, rows, sem):
    mp = outs[0].shape[2]
    quarter = whole.shape[0] // mp
    for core, half, entry, step, slot, owner in each_slice(place, 0, mp):
        piece = outs[core].at[half, entry, step, pl.ds(offset, rows)]
        image_copies(whole, piece, quarter, half, slot, owner, sem, False)


def norm_rows(values, gain_row, shift_row):
    center = values - jnp.mean(values, axis=-1, keepdims=True)
    moment = jnp.mean(center * center, axis=-1, keepdims=True)
    return center * lax.rsqrt(moment + EPSILON) * gain_row + shift_row


def norm_back(pre_norm, gain_row, grad_out, small):
    center = pre_norm - jnp.mean(pre_norm, axis=-1, keepdims=True)
    scale = lax.rsqrt(jnp.mean(center * center, axis=-1, keepdims=True) + EPSILON)
    normal = center * scale
    lifted = grad_out * gain_row
    grad_pre = scale * (
        lifted
        - jnp.mean(lifted, axis=-1, keepdims=True)
        - normal * jnp.mean(lifted * normal, axis=-1, keepdims=True)
    )
    small[...] = jnp.zeros_like(small)
    small[0:1] = jnp.sum(grad_out * normal, axis=0, keepdims=True)
    small[1:2] = jnp.sum(grad_out, axis=0, keepdims=True)
    small[2:3] = jnp.sum(grad_pre, axis=0, keepdims=True)
    return grad_pre


def column_total(values):
    return jnp.sum(values.astype(F32), axis=0, keepdims=True)


def spread_heads(values):
    lane = lax.broadcasted_iota(jnp.int32, (1, values.shape[1]), 1)
    parts = []
    for first in range(0, values.shape[1], HEAD_DIM):
        mask = ((lane >= first) & (lane < first + HEAD_DIM)).astype(F32).astype(values.dtype)
        parts.append(values * mask)
    return jnp.concatenate(parts, axis=0)


def pick_heads(values):
    lane = lax.broadcasted_iota(jnp.int32, (1, values.shape[1]), 1)
    rows = values.shape[0] * HEAD_DIM // values.shape[1]
    picked = values[:rows]
    for head in range(1, values.shape[1] // HEAD_DIM):
        picked = jnp.where(lane >= head * HEAD_DIM, values[head * rows : (head + 1) * rows], picked)
    return picked


def softmax(scores):
    raised = jnp.exp(scores - jnp.max(scores, axis=-1, keepdims=True))
    return raised * (1.0 / jnp.sum(raised, axis=-1, keepdims=True))


def score_back(weights, grad_weights):
    along = weights * grad_weights
    return (along - weights * jnp.sum(along, axis=-1, keepdims=True)).astype(BF16)


def attention_units(count, row_size, place_size, width):
    units = []
    for number in range(count):
        rows = slice(number * row_size, (number + 1) * row_size)
        places = slice(number * place_size, (number + 1) * place_size)
        units += [(number, rows, places, slice(first, first + STACK)) for first in range(0, width, STACK)]
    return [units[first : first + TOGETHER] for first in range(0, len(units), TOGETHER)]


def attend_forward(units, allowed, query, keys, value, context):
    for group in units:
        scores = [dot_nt(spread_heads(query[rows, lanes]).astype(BF16), keys[at, lanes]) for _, rows, at, lanes in group]
        weights = [
            softmax(jnp.where(allowed(unit[0]), score * SCALE, BLOCKED)).astype(BF16)
            for unit, score in zip(group, scores)
        ]
        for (_, rows, at, lanes), weight in zip(group, weights):
            context[rows, lanes] = pick_heads(dot_nn(weight, value[at, lanes])).astype(context.dtype)


def attend_backward(units, allowed, query, keys, value, grad_context, grad_query, grad_keys, grad_value):
    for group in units:
        queries = [spread_heads(query[rows, lanes]).astype(BF16) for _, rows, _, lanes in group]
        contexts = [spread_heads(grad_context[rows, lanes]).astype(BF16) for _, rows, _, lanes in group]
        scores = [dot_nt(one, keys[at, lanes]) for one, (_, _, at, lanes) in zip(queries, group)]
        grad_weights = [dot_nt(one, value[at, lanes]) for one, (_, _, at, lanes) in zip(contexts, group)]
        weights = [
            softmax(jnp.where(allowed(unit[0]), score * SCALE, BLOCKED)) for unit, score in zip(group, scores)
        ]
        grad_scores = [score_back(one, other) for one, other in zip(weights, grad_weights)]
        for weight, one, (_, _, at, lanes) in zip(weights, contexts, group):
            grad_value[at, lanes] = dot_tn(weight.astype(BF16), one).astype(BF16)
        for grad_score, one, (_, _, at, lanes) in zip(grad_scores, queries, group):
            grad_keys[at, lanes] = (dot_tn(grad_score, one) * SCALE).astype(BF16)
        for grad_score, (_, rows, at, lanes) in zip(grad_scores, group):
            mixed = pick_heads(dot_nn(grad_score, keys[at, lanes])) * SCALE
            grad_query[rows, lanes] = mixed.astype(grad_query.dtype)


def same_segment(code_col, code_row):
    size = code_row.shape[1]

    def allowed(group):
        column = code_col[group * size : (group + 1) * size]
        return jnp.concatenate([column] * (STACK // HEAD_DIM), axis=0) == code_row[group : group + 1]

    return allowed


def real_patch(size, patches):
    column = lax.broadcasted_iota(jnp.int32, (1, size), 1)
    return lambda row: column < patches


def pick_copies(picks, parts, target, sem):
    size = parts[0].shape[0]
    for row in range(target.shape[0]):
        for number, part in enumerate(parts):

            @pl.when(picks[row] // size == number)
            def _():
                start(part.at[picks[row] % size], target.at[row], sem)


def flat_rows(rows_ref, target):
    seq = rows_ref.shape[1]
    for row in range(rows_ref.shape[0]):
        target[row * seq : (row + 1) * seq] = rows_ref[row].astype(target.dtype)


def leave_rows(values, target):
    seq = target.shape[1]
    for row in range(target.shape[0]):
        target[row] = values[row * seq : (row + 1) * seq].astype(target.dtype)


def slice_kernel(
    place, head_bias, unit_bias, patch_bias, inward, outward, feed_in, feed_out, image, first, second, third, sems,
):
    slot = place[0]
    quarter, width = inward.shape[2:]
    span = 4 * quarter // SLICES
    count = quarter // span
    rows = span // 2
    feed_rows = feed_in.shape[1] // SLICES
    image_rows = first.shape[1] - 2 * rows - 16
    weights = first.at[:, pl.ds(0, 2 * rows + image_rows)]
    table = jnp.concatenate(
        [
            head_bias[...].astype(F32),
            jnp.zeros((head_bias.shape[0], width - quarter), F32),
        ],
        axis=1,
    )
    patch = jnp.concatenate([patch_bias[...].astype(F32), jnp.zeros((1, width - quarter), F32)], axis=1)
    table = jnp.concatenate([table, unit_bias[...].astype(F32), patch, jnp.zeros((7, width), F32)], axis=0)
    first[0, 2 * rows + image_rows :] = table.astype(BF16)
    first[1, 2 * rows + image_rows :] = jnp.zeros((16, width), BF16)

    def attention(layer, target, offset, sem):
        for half in range(2):
            row = (slot % count) * span + half * rows
            spot = target.at[half, pl.ds(offset, rows)]

            @pl.when(slot < 3 * count)
            def _():
                start(inward.at[layer, slot // count, aligned(row, rows)], spot, sem)

            @pl.when(slot >= 3 * count)
            def _():
                start(outward.at[layer, aligned(row, rows)], spot, sem)

    def feed(layer, target, offset, sem):
        for half, source in enumerate((feed_in, feed_out)):
            spot = target.at[half, pl.ds(offset, feed_rows)]
            start(source.at[layer, aligned(slot * feed_rows, feed_rows)], spot, sem)

    attention(0, first, 0, sems.at[0])
    attention(2, first, rows, sems.at[0])
    for half in range(2):
        spot = first.at[half, pl.ds(2 * rows, image_rows)]
        image_copies(image, spot, quarter, half, slot, 0, sems.at[0], False)
    feed(0, second, 0, sems.at[1])
    attention(1, second, feed_rows, sems.at[1])
    feed(1, third, 0, sems.at[2])
    for number, target in enumerate((weights, second, third)):
        finish(target, sems.at[number])


def self_forward(
    layer, norm, stream, bias, params, code_col, code_row, out, low, pre, query, keys, value, context, kept, whole, sems,
    out_sem,
):
    hb = stream.astype(BF16)
    low[...] = hb
    finish(whole.at[0], sems.at[0])
    query[...] = (dot_nt(hb, whole[0]) + bias[2 * layer : 2 * layer + 1]).astype(BF16)
    finish(whole.at[1], sems.at[1])
    keys[...] = dot_nt(hb, whole[1]).astype(BF16)
    finish(whole.at[2], sems.at[2])
    value[...] = (dot_nt(hb, whole[2]) + bias[2 * layer + 1 : 2 * layer + 2]).astype(BF16)
    groups, size = code_row.shape
    units = attention_units(groups, size, size, hb.shape[1])
    attend_forward(units, same_segment(code_col, code_row), query, keys, value, context)
    finish(whole.at[3], sems.at[3])
    start(whole, kept, out_sem)
    total = dot_nn(context[...], whole[3]) + params[3 * norm : 3 * norm + 1] + stream
    pre[...] = total
    out[...] = norm_rows(total, params[3 * norm + 1 : 3 * norm + 2], params[3 * norm + 2 : 3 * norm + 3])
    finish(whole, out_sem)


def self_forward_kernel(
    layer, norm, offset, n_parts, n_pieces, place, picks, *refs,
):
    parts, (inward, outward), refs = refs[:n_parts], refs[n_parts : n_parts + 2], refs[n_parts + 2 :]
    pieces, refs = refs[:n_pieces], refs[n_pieces:]
    held = refs[15:]
    if held:
        pick_copies(picks, parts, held[0], held[2])
    load_attention(place, (inward, outward), pieces, offset, layer, refs[12], refs[13])
    if held:
        finish(held[0], held[2])
        flat_rows(held[0], held[1])
        stream = held[1][...]
    else:
        stream = parts[0][...]
    self_forward(layer, norm, stream, *refs[:15])


def feed_self_forward_kernel(
    layer, norm, offset, next_layer, next_norm, next_offset, n_pieces, n_next, place, rows_ref, first_weight, second_weight,
    inward, outward, *refs,
):
    pieces, following, refs = refs[:n_pieces], refs[n_pieces : n_pieces + n_next], refs[n_pieces + n_next :]
    bias, params, code_col, code_row = refs[:4]
    feed_outs, self_outs, scratch = refs[4:10], refs[10:18], refs[18:]
    whole, slope, active, sems, out_sem, square, square_sems, square_out = scratch
    feed_refs = (bias, params, *feed_outs, whole, slope, active, sems, out_sem)
    for step in range(whole.shape[1]):
        for half in range(2):
            load_feed(place, (first_weight, second_weight), pieces, offset, layer, half, step, whole, sems)
    load_attention(place, (inward, outward), following, next_offset, next_layer, square, square_sems)
    feed_forward(layer, norm, place, rows_ref, *feed_refs)
    self_forward(
        next_layer, next_norm, feed_outs[0][...], bias, params, code_col, code_row, *self_outs, square, square_sems, square_out
    )


def load_kept(kept, whole, sems, order):
    for mat in order:
        start(kept.at[mat], whole.at[mat], sems.at[mat])


def self_backward_kernel(
    leave, norm, spot, n_held, place, grad, low, pre, query, keys, value, context, kept, params, code_col, code_row, *refs,
):
    out, small, keep, send, whole, grads, grad_context, grad_query, grad_keys, grad_value, sems, out_sem = refs[n_held:]
    load_kept(kept, whole, sems, (3, 0, 1, 2))
    grad_pre = norm_back(pre[...], params[3 * norm + 1 : 3 * norm + 2], grad[...], small)
    branch = grad_pre.astype(BF16)
    finish(whole.at[3], sems.at[3])
    grad_context[...] = dot_nt(branch, whole[3]).astype(BF16)
    grads[3] = dot_tn(context[...], branch).astype(BF16)
    groups, size = code_row.shape
    units = attention_units(groups, size, size, branch.shape[1])
    attend_backward(
        units, same_segment(code_col, code_row), query, keys, value, grad_context, grad_query, grad_keys, grad_value
    )
    hb = low[...]
    grads[0] = dot_tn(grad_query[...], hb).astype(BF16)
    grads[1] = dot_tn(grad_keys[...], hb).astype(BF16)
    grads[2] = dot_tn(grad_value[...], hb).astype(BF16)
    store_attention(place, grads, (keep, send), spot, out_sem)
    small[3:4] = column_total(grad_query[...])
    small[4:5] = column_total(grad_value[...])
    total = grad_pre
    for mat, part in enumerate((grad_query, grad_keys, grad_value)):
        finish(whole.at[mat], sems.at[mat])
        total = total + dot_nn(part[...], whole[mat])
    if leave:
        leave_rows(total, out)
    else:
        out[...] = total
    finish(grads, out_sem)


def feed_forward(
    layer, norm, place, rows_ref, bias, params, out, low, pre, slope_out, active_out, kept, whole, slope, active, sems, out_sem,
):
    parts = whole.shape[1]
    stream = rows_ref[...]
    hb = stream.astype(BF16)
    low[...] = hb
    total = params[3 * norm : 3 * norm + 1] + stream
    for step in range(parts):
        row = 6 + layer * parts + (place[1] + parts - step) % parts
        finish(whole.at[0, step], sems.at[0, step])
        units = dot_nn(hb, whole[0, step]) + bias[pl.ds(row, 1)]
        share = 0.5 * (1.0 + lax.erf(units * (2.0 ** -0.5)))
        slope[step] = share + units * jnp.exp(-0.5 * units * units) * 0.3989422804014327
        start(slope.at[step], slope_out.at[step], out_sem)
        gated = (units * share).astype(BF16)
        active[step] = gated
        start(active.at[step], active_out.at[step], out_sem)
        start(whole.at[0, step], kept.at[0, step], out_sem)
        finish(whole.at[1, step], sems.at[1, step])
        start(whole.at[1, step], kept.at[1, step], out_sem)
        total = total + dot_nn(gated, whole[1, step])
    pre[...] = total
    out[...] = norm_rows(total, params[3 * norm + 1 : 3 * norm + 2], params[3 * norm + 2 : 3 * norm + 3])
    finish(slope, out_sem)
    finish(active, out_sem)
    finish(whole, out_sem)


def feed_backward_kernel(
    norm, place, grad_in, low_in, pre_in, slope_in, active_in, kept, params,
    out, small, keep, send, whole, grads, grad, low, pre, slope, active, row_sems, sems, out_sem,
):
    parts = whole.shape[1]
    start(grad_in, grad, row_sems.at[0])
    start(pre_in, pre, row_sems.at[1])
    for step in range(parts):
        start(active_in.at[step], active.at[step], row_sems.at[3 + step])
        start(kept.at[1, step], whole.at[1, step], sems.at[1, step])
        start(slope_in.at[step], slope.at[step], row_sems.at[3 + parts + step])
        if step == 0:
            start(low_in, low, row_sems.at[2])
        start(kept.at[0, step], whole.at[0, step], sems.at[0, step])
    finish(grad, row_sems.at[0])
    finish(pre, row_sems.at[1])
    grad_pre = norm_back(pre[...], params[3 * norm + 1 : 3 * norm + 2], grad[...], small)
    branch = grad_pre.astype(BF16)
    total = grad_pre
    for step in range(parts):
        finish(active.at[step], row_sems.at[3 + step])
        grads[1, step] = dot_tn(active[step], branch).astype(BF16)
        store_feed(place, grads, (keep, send), 1, step, out_sem)
        finish(whole.at[1, step], sems.at[1, step])
        finish(slope.at[step], row_sems.at[3 + parts + step])
        grad_units = (dot_nt(branch, whole[1, step]) * slope[step]).astype(BF16)
        if step == 0:
            finish(low, row_sems.at[2])
        grads[0, step] = dot_tn(low[...], grad_units).astype(BF16)
        store_feed(place, grads, (keep, send), 0, step, out_sem)
        small[pl.ds(3 + (place[1] + parts - step) % parts, 1)] = column_total(grad_units)
        finish(whole.at[0, step], sems.at[0, step])
        total = total + dot_nt(grad_units, whole[0, step])
    out[...] = total
    finish(grads, out_sem)


def feed_both_kernel(
    layer, norm, offset, n_parts, n_pieces, place, picks, rows_ref, first_weight, second_weight, *refs,
):
    arrived, pieces, refs = refs[:n_parts], refs[n_parts : n_parts + n_pieces], refs[n_parts + n_pieces :]
    bias, params, mixed, out, small, keep, send, whole, grads, slope, active, low, pre, grad, held, sems, row_sem, out_sem = refs
    parts = whole.shape[1]
    for step in range(parts):
        for half in range(2):
            load_feed(place, (first_weight, second_weight), pieces, offset, layer, half, step, whole, sems)
    pick_copies(picks, arrived, held, row_sem)
    stream = rows_ref[...]
    low[...] = stream.astype(BF16)
    total = params[3 * norm : 3 * norm + 1] + stream
    for step in range(parts):
        row = 6 + layer * parts + (place[1] + parts - step) % parts
        finish(whole.at[0, step], sems.at[0, step])
        units = dot_nn(low[...], whole[0, step]) + bias[pl.ds(row, 1)]
        share = 0.5 * (1.0 + lax.erf(units * (2.0 ** -0.5)))
        slope[step] = share + units * jnp.exp(-0.5 * units * units) * 0.3989422804014327
        gated = (units * share).astype(BF16)
        active[step] = gated
        finish(whole.at[1, step], sems.at[1, step])
        total = total + dot_nn(gated, whole[1, step])
    pre[...] = total
    gain, shift = params[3 * norm + 1 : 3 * norm + 2], params[3 * norm + 2 : 3 * norm + 3]
    leave_rows(norm_rows(total, gain, shift), mixed)
    finish(held, row_sem)
    flat_rows(held, grad)
    grad_pre = norm_back(pre[...], gain, grad[...], small)
    branch = grad_pre.astype(BF16)
    total = grad_pre
    for step in range(parts):
        grads[1, step] = dot_tn(active[step], branch).astype(BF16)
        store_feed(place, grads, (keep, send), 1, step, out_sem)
        grad_units = (dot_nt(branch, whole[1, step]) * slope[step]).astype(BF16)
        grads[0, step] = dot_tn(low[...], grad_units).astype(BF16)
        store_feed(place, grads, (keep, send), 0, step, out_sem)
        small[pl.ds(3 + (place[1] + parts - step) % parts, 1)] = column_total(grad_units)
        total = total + dot_nt(grad_units, whole[0, step])
    out[...] = total
    finish(grads, out_sem)


def finish_all(whole, sems):
    for mat in range(whole.shape[0]):
        finish(whole.at[mat], sems.at[mat])


def image_forward_kernel(
    layer, offset, image_offset, image_rows, n_pieces, place, images, image, inward, outward, *refs,
):
    pieces, refs = refs[:n_pieces], refs[n_pieces:]
    bias, projected, keys, value, kept_image, whole, whole_image, sems, image_sem, out_sem = refs
    load_image(place, image, pieces, image_offset, image_rows, whole_image, image_sem)
    load_attention(place, (inward, outward), pieces, offset, layer, whole, sems)
    finish(whole_image, image_sem)
    start(whole_image, kept_image, out_sem)
    size = images.shape[0] // 4
    last = bias.shape[0] - 1
    for first in range(0, images.shape[0], size):
        rows = slice(first, first + size)
        source = (dot_nt(images[rows], whole_image[...]) + bias[last : last + 1]).astype(BF16)
        projected[rows] = source
        if first == 0:
            finish_all(whole, sems)
        keys[rows] = dot_nt(source, whole[1]).astype(BF16)
        value[rows] = (dot_nt(source, whole[2]) + bias[2 * layer + 1 : 2 * layer + 2]).astype(BF16)
    finish(whole_image, out_sem)


def cross_forward_kernel(
    layer, norm, offset, seq, patches, n_pieces, place, rows_ref, keys, value, inward, outward, *refs,
):
    pieces, refs = refs[:n_pieces], refs[n_pieces:]
    bias, params, out, low, pre, query, context, kept, whole, mixed, sems, out_sem = refs
    load_attention(place, (inward, outward), pieces, offset, layer, whole, sems)
    stream = rows_ref[...]
    hb = stream.astype(BF16)
    low[...] = hb
    finish_all(whole, sems)
    start(whole, kept, out_sem)
    query[...] = (dot_nt(hb, whole[0]) + bias[2 * layer : 2 * layer + 1]).astype(BF16).astype(F32)
    count = stream.shape[0] // seq
    size = keys.shape[0] // count
    units = attention_units(count, seq, size, hb.shape[1])
    attend_forward(units, real_patch(size, patches), query, keys, value, mixed)
    context[...] = mixed[...].astype(BF16)
    total = dot_nn(context[...], whole[3]) + params[3 * norm : 3 * norm + 1] + stream
    pre[...] = total
    out[...] = norm_rows(total, params[3 * norm + 1 : 3 * norm + 2], params[3 * norm + 2 : 3 * norm + 3])
    finish(whole, out_sem)


def cross_backward_kernel(
    norm, seq, patches, place, grad, low, pre, query, context, keys, value, kept, params,
    out, small, grad_keys, grad_value, branch_out, query_out, whole, grad_context, grad_query, sems,
):
    load_kept(kept, whole, sems, (3, 0))
    grad_pre = norm_back(pre[...], params[3 * norm + 1 : 3 * norm + 2], grad[...], small)
    branch = grad_pre.astype(BF16)
    branch_out[...] = branch
    finish(whole.at[3], sems.at[3])
    grad_context[...] = dot_nt(branch, whole[3]).astype(BF16).astype(F32)
    count = branch.shape[0] // seq
    size = keys.shape[0] // count
    units = attention_units(count, seq, size, branch.shape[1])
    attend_backward(
        units, real_patch(size, patches), query, keys, value, grad_context, grad_query, grad_keys, grad_value
    )
    query_low = grad_query[...].astype(BF16)
    query_out[...] = query_low
    small[3:4] = column_total(query_low)
    small[4:5] = column_total(grad_value[...])
    finish(whole.at[0], sems.at[0])
    out[...] = grad_pre + dot_nn(query_low, whole[0])


def cross_weights_kernel(
    spot, place, context, branch, grad_query, low, grad_keys, grad_value, source, keep_held, send_held,
    keep, send, grads, out_sem,
):
    grads[3] = dot_tn(context[...], branch[...]).astype(BF16)
    grads[0] = dot_tn(grad_query[...], low[...]).astype(BF16)
    grads[1] = dot_tn(grad_keys[...], source[...]).astype(BF16)
    grads[2] = dot_tn(grad_value[...], source[...]).astype(BF16)
    store_attention(place, grads, (keep, send), spot, out_sem)
    finish(grads, out_sem)


def image_backward_kernel(
    image_rows, spot, n_held, place, images, grad_keys, grad_value, kept, kept_image, *refs,
):
    out, small, keep, send, whole, whole_image, grads, low, sems, image_sem, out_sem = refs[n_held:]
    load_kept(kept, whole, sems, (1, 2))
    start(kept_image, whole_image, image_sem)
    finish(whole.at[1], sems.at[1])
    finish(whole.at[2], sems.at[2])
    finish(whole_image, image_sem)
    patches, count = out.shape[:2]
    size = images.shape[0] // count
    small[...] = jnp.zeros_like(small)
    for row in range(count):
        rows = slice(row * size, (row + 1) * size)
        source = dot_nn(grad_keys[rows], whole[1]) + dot_nn(grad_value[rows], whole[2])
        source = source.astype(BF16)
        low[rows] = source
        out[:, row, :] = dot_nn(source, whole_image[...])[:patches]
    grads[...] = dot_tn(low[...], images[...]).astype(BF16)
    store_image(place, grads, (keep, send), spot, image_rows, out_sem)
    small[0:1] = column_total(low[...])
    finish(grads, out_sem)


def combine_kernel(
    keep, core, one0, one1, two0, two1, own, down, across, up, kept, arrived, first, second, sems,
):
    for half, (one, two) in enumerate(((one0, two0), (one1, two1))):
        start(keep.at[half, 0], kept.at[half], sems.at[0])
        start(core.at[half, 0], arrived.at[half], sems.at[1])
        start(one.at[0], first.at[half], sems.at[2])
        start(two, second.at[half], sems.at[3])
    for number, target in enumerate((kept, arrived, first, second)):
        finish(target, sems.at[number])
    for step, target in enumerate((own, down, across, up)):
        for half in range(2):
            total = kept[half, step].astype(F32) + arrived[half, step].astype(F32)
            total = total + first[half, step].astype(F32) + second[half, step].astype(F32)
            target[half] = total.astype(target.dtype)


def pick_kernel(picks, *refs):
    *parts, out, held, sem = refs
    pick_copies(picks, parts, held, sem)
    finish(held, sem)
    out[...] = held[...].astype(out.dtype)


def finish_kernel(blocks, quarter, names, held, n_results, place, *refs):
    results, refs = refs[:n_results], refs[n_results:]
    width = results[0].shape[3]
    targets = dict(zip(names, refs[held:]))
    scratch = refs[held + len(names) :]
    sem, out_sem = scratch[-2:]
    for number, (kind, offset, _) in enumerate(blocks):
        buffer = scratch[2 * number]
        for core in range(2):
            for half in range(2):
                for entry in range(4):
                    if n_results == 1:
                        slot = core ^ DISTANCES[half][entry]
                        piece = results[0].at[slot, half]
                    else:
                        slot = place[0] ^ (core ^ DISTANCES[half][entry])
                        piece = piece_of(results, core, half, entry)
                    if kind == ATTENTION:
                        rows = quarter // 4
                        spot = attention_spot(buffer, quarter, half, slot, 0)
                        start(piece.at[pl.ds(offset, rows)], spot, sem.at[number])
                    elif kind == FEED:
                        rows = buffer.shape[1] // SLICES
                        spot = buffer.at[half, aligned(slot * rows, rows)]
                        start(piece.at[pl.ds(offset, rows)], spot, sem.at[number])
                    else:
                        rows = quarter * buffer.shape[1] // width // SLICES // 2
                        piece = piece.at[pl.ds(offset, rows)]
                        image_copies(buffer, piece, quarter, half, slot, 0, sem.at[number], True)
    for number, (kind, _, layer) in enumerate(blocks):
        buffer, wide = scratch[2 * number : 2 * number + 2]
        done = out_sem.at[number]
        finish(buffer, sem.at[number])
        wide[...] = buffer[...].astype(F32)
        if kind == ATTENTION:
            start(wide.at[pl.ds(0, 3)], targets[ATTENTION_IN].at[layer], done)
            start(wide.at[3], targets[ATTENTION_OUT].at[layer], done)
        elif kind == FEED:
            start(wide.at[0], targets[FEED_IN].at[layer], done)
            start(wide.at[1], targets[FEED_OUT].at[layer], done)
        else:
            start(wide, targets[IMAGE], done)
    for number in range(len(blocks)):
        finish(scratch[2 * number + 1], out_sem.at[number])


def shape(dims, kind=F32):
    return jax.ShapeDtypeStruct(tuple(dims), kind)


def call(kernel, ins, outs, scratch, aliases=None, megabytes=60):
    return pl.pallas_call(
        kernel,
        in_specs=[spec for _, spec in ins],
        out_specs=[spec for _, spec in outs],
        out_shape=[s for s, _ in outs],
        scratch_shapes=scratch,
        input_output_aliases=aliases or {},
        compiler_params=pltpu.CompilerParams(vmem_limit_bytes=megabytes << 20),
        cost_estimate=pl.CostEstimate(flops=0, bytes_accessed=0, transcendentals=0),
    )(*[v for v, _ in ins])


class Ring:
    def __init__(self, at, name, own):
        self.at, self.name = at, name
        at[name] = {0: own}

    def up(self):
        parts = self.at[self.name]
        parts[1] = pass_on(parts[0])

    def down(self):
        parts = self.at[self.name]
        parts[3] = pass_on(parts[0], -1)

    def far(self):
        parts = self.at[self.name]
        parts[2] = pass_on(parts[1])

    def direct(self):
        parts = self.at[self.name]
        for way in (1, 2, 3):
            parts[way] = pass_on(parts[0], way)

    def take(self):
        parts = self.at.pop(self.name)
        return [parts[i] for i in range(4)]


class Widen:
    def __init__(self, at, name, first, second):
        self.at, self.name = at, name
        at[name] = {"own": (first, second)}

    def one(self):
        held = self.at[self.name]
        first, second = held.pop("own")
        held["both"] = (first, swap(first, 2), second, swap(second, 4))

    def two(self):
        held = self.at[self.name]
        both = held.pop("both")
        near = jnp.stack(both[:2]), jnp.stack(both[2:])
        held["near"] = near
        held["far"] = swap(near[0], 4), swap(near[1], 2)

    def direct(self):
        held = self.at[self.name]
        own = held.pop("own")
        held["lines"] = [jnp.stack(own)] + [swap(jnp.stack(own), bit) for bit in (2, 4, 6)]

    def two_early(self):
        self.two()
        held = self.at[self.name]
        held["near all"] = jnp.stack(held.pop("near"))
        held["near core"] = swap(held["near all"], 1)

    def core_late(self):
        held = self.at[self.name]
        held["far all"] = jnp.stack(held.pop("far"))
        held["far core"] = swap(held["far all"], 1)

    def core_direct(self):
        held = self.at[self.name]
        lines = held.pop("lines")
        order = [[distance // 2 for distance in half] for half in DISTANCES]
        held["all"] = jnp.stack([jnp.stack([lines[i][half] for i in order[half]]) for half in range(2)])
        held["core"] = swap(held["all"], 1)

    def core(self):
        held = self.at[self.name]
        near, far = held.pop("near"), held.pop("far")
        held["all"] = jnp.stack([jnp.concatenate([near[half], far[half]]) for half in range(2)])
        held["core"] = swap(held["all"], 1)

    def take(self):
        held = self.at.pop(self.name)
        if "all" in held:
            return held["all"], held["core"]
        return held["near all"], held["far all"], held["near core"], held["far core"]


class Reduce:
    def __init__(self, at, name, keep, send):
        self.at, self.name = at, name
        at[name] = {"keep": keep, "send": send}

    def core(self):
        held = self.at[self.name]
        held["core"] = swap(held.pop("send"), 1)

    def one(self):
        held = self.at[self.name]
        keep, core = held["keep"], held["core"]
        held["one"] = swap(added(keep[0, 2:], core[0, 2:]), 4), swap(added(keep[1, 2:], core[1, 2:]), 2)

    def two(self):
        held = self.at[self.name]
        keep, core, one = held["keep"], held["core"], held["one"]
        held["two"] = (
            swap(added(keep[0, 1], core[0, 1], one[0][1]), 2),
            swap(added(keep[1, 1], core[1, 1], one[1][1]), 4),
        )

    def combine(self):
        held = self.at[self.name]
        arrays = [held[name] for name in ("keep", "core")] + list(held["one"]) + list(held["two"])
        rows, width = arrays[0].shape[3:]
        mp = arrays[0].shape[2]
        outs = [shape((2, rows, width), kind) for kind in (F32, BF16, BF16, F32)]
        parts = call(
            combine_kernel,
            [(v, ANY) for v in arrays],
            [(v, VMEM) for v in outs],
            [pltpu.VMEM((2, mp, rows, width), BF16)] * 4 + [pltpu.SemaphoreType.DMA((4,))],
            megabytes=12,
        )
        self.at[self.name] = {"own": parts[0], "parts": parts[1:]}

    def join(self, other):
        theirs = self.at.pop(other.name)
        held = self.at[self.name]
        held["own"] = jnp.concatenate([held["own"], theirs["own"]], axis=1)
        held["parts"] = [jnp.concatenate(pair, axis=1) for pair in zip(held["parts"], theirs["parts"])]

    def far(self):
        held = self.at[self.name]
        held["far"] = pass_on(held["parts"][1])

    def near(self):
        held = self.at[self.name]
        down, _, up = held.pop("parts")
        held["up"] = pass_on(added(up, held.pop("far")))
        held["down"] = pass_on(down, -1)

    def direct(self):
        held = self.at[self.name]
        down, across, up = held.pop("parts")
        held["up"], held["across"], held["down"] = pass_on(added(up)), pass_on(across, 2), pass_on(down, -1)

    def owned(self):
        held = self.at.pop(self.name)
        own = added(held["own"], *[held[name] for name in ("up", "across", "down") if name in held])
        bit = SLICES
        while bit < lax.axis_size("dp"):
            own = added(own, swap(own, bit))
            bit *= 2
        return own


def on_device(
    tokens, images, segment_of_token, image_of_row, attention_in, query_value_bias, attention_out, output_bias,
    feed_in, feed_bias, feed_out, image_weight, image_bias, norm_gain, norm_bias, cotangent,
):
    mp = lax.axis_size("mp")
    slot = lax.axis_index("dp") % SLICES
    owner = lax.axis_index("mp")
    place = jnp.stack([slot, owner]).astype(jnp.int32)
    own_rows, seq, width = tokens.shape
    group_rows = segment_of_token.shape[0]
    patches, image_width = images.shape[1:]
    quarter = attention_in.shape[3]
    units = feed_in.shape[2]
    n_tokens = own_rows * seq
    inward = attention_in.transpose(0, 1, 3, 2)
    image = image_weight.T

    attention_rows = quarter // 4
    feed_rows = units // SLICES
    image_rows = quarter * image_width // width // SLICES // 2

    token_shape = shape((n_tokens, width))
    token_low = shape((n_tokens, width), BF16)
    row_low = shape((own_rows, seq, width), BF16)
    inner_shape = shape((mp, n_tokens, units))
    inner_low = shape((mp, n_tokens, units), BF16)
    padded = -(-patches // 16) * 16
    n_patches = own_rows * padded
    patch_low = shape((n_patches, width), BF16)
    small_shape = shape((8, width))
    attention_grad = shape((2, 4, mp, attention_rows, width), BF16)
    feed_grad = shape((2, 4, mp, feed_rows, width), BF16)
    image_grad = shape((2, 4, mp, image_rows, width), BF16)
    kept_square = shape((4, width, width), BF16)
    kept_wide = shape((2, mp, units, width), BF16)
    kept_tall = shape((width, image_width), BF16)
    square = pltpu.VMEM((4, width, width), BF16)
    wide = pltpu.VMEM((2, mp, units, width), BF16)
    tall = pltpu.VMEM((width, image_width), BF16)
    token_f32 = pltpu.VMEM((n_tokens, width), F32)
    token_bf16 = pltpu.VMEM((n_tokens, width), BF16)
    row_bf16 = pltpu.VMEM((own_rows, seq, width), BF16)
    inner_f32 = pltpu.VMEM((mp, n_tokens, units), F32)
    inner_bf16 = pltpu.VMEM((mp, n_tokens, units), BF16)
    dma = pltpu.SemaphoreType.DMA
    matmul = 2 * n_tokens * width * width
    patch_matmul = 2 * n_patches * width * width

    local_order = image_of_row % group_rows
    here = owner * own_rows + jnp.arange(own_rows, dtype=jnp.int32)
    chosen = (local_order[None, :] == here[:, None]).astype(jnp.int32)
    source_row = jnp.sum(chosen * jnp.arange(group_rows, dtype=jnp.int32)[None, :], axis=1)
    picks_in = ((owner - source_row // own_rows) % mp) * own_rows + source_row % own_rows
    mine = (jnp.arange(group_rows, dtype=jnp.int32)[None, :] == here[:, None]).astype(jnp.int32)
    image_row = jnp.sum(mine * local_order[None, :], axis=1)
    picks_out = ((owner - image_row // own_rows) % mp) * own_rows + image_row % own_rows
    segments = jnp.sum(chosen[:, :, None] * segment_of_token[None], axis=1)
    code = jnp.arange(own_rows, dtype=jnp.int32)[:, None] * seq + segments
    code_col = code.reshape(n_tokens, 1)
    code_row = code.reshape(own_rows // 2, 2 * seq)

    first_rows = 2 * attention_rows + image_rows
    first, second, third = call(
        slice_kernel,
        [(place, SMEM)]
        + [(v, VMEM) for v in (query_value_bias.reshape(6, quarter), feed_bias, image_bias.reshape(1, quarter))]
        + [(v, ANY) for v in (inward, attention_out, feed_in, feed_out, image)],
        [
            (shape((2, rows, width), BF16), VMEM)
            for rows in (first_rows + 16, feed_rows + attention_rows, feed_rows)
        ],
        [dma((3,))],
    )

    at = {}

    def step():
        done = lax.optimization_barrier(at)
        at.clear()
        at.update(done)

    rings = {
        name: Ring(at, name, own)
        for name, own in (
            ("first", first), ("second", second), ("third", third), (TOKENS, tokens), (COTANGENT, cotangent),
        )
    }

    def gathered(name, rows=None):
        parts = rings[name].take()[1:]
        return Widen(at, name, *[jnp.stack([part[half, :rows] for part in parts]) for half in range(2)])

    rings["first"].direct()
    step()

    parts = [part[0, first_rows:] for part in at["first"].values()]
    ordered = jnp.stack(parts)[(owner - jnp.arange(mp)) % mp].astype(F32)
    bias = jnp.concatenate(
        [
            ordered[:, :6, :quarter].transpose(1, 0, 2).reshape(6, width),
            ordered[:, 6:8].transpose(1, 0, 2).reshape(2 * mp, width),
            ordered[:, 8, :quarter].reshape(1, width),
        ]
    )
    params = jnp.stack([output_bias, norm_gain, norm_bias], axis=1).astype(F32).reshape(-1, width)
    patch_rows = jnp.pad(images, ((0, 0), (0, padded - patches), (0, 0))).reshape(n_patches, image_width)
    at["tables"] = bias, params, code_col, code_row, picks_in, picks_out, image_row, patch_rows
    first_wide = gathered("first", first_rows)
    first_wide.one()
    rings["second"].up()
    rings["second"].down()
    step()
    bias, params, code_col, code_row, picks_in, picks_out, image_row, patch_rows = at.pop("tables")
    first_wide.two()
    rings["second"].far()
    rings[TOKENS].up()
    rings["third"].up()
    step()
    second_wide = gathered("second")
    first_wide.core()
    second_wide.one()
    rings[TOKENS].down()
    rings["third"].down()
    step()

    attention_pieces = [None, None, None]
    attention_at = [0, feed_rows, attention_rows]
    feed_pieces = [None, None]
    feed_at = [0, 0]

    def attention_ins(layer):
        return [(inward, ANY), (attention_out, ANY)] + [(piece, ANY) for piece in attention_pieces[layer]]

    def feed_ins(layer):
        return [(feed_in, ANY), (feed_out, ANY)] + [(piece, ANY) for piece in feed_pieces[layer]]

    def first_forward(layer, norm, parts):
        picked = len(parts) > 1
        return call(
            partial(self_forward_kernel, layer, norm, attention_at[layer], len(parts), len(attention_pieces[layer])),
            [(place, SMEM), (picks_in, SMEM)]
            + [(part, ANY if picked else VMEM) for part in parts]
            + attention_ins(layer)
            + [(bias, VMEM), (params, VMEM), (code_col, VMEM), (code_row, VMEM)],
            [(token_shape, VMEM), (token_low, VMEM), (token_shape, VMEM)] + [(token_low, VMEM)] * 4 + [(kept_square, ANY)],
            [square, dma((4,)), dma] + ([row_bf16, token_f32, dma] if picked else []),
        )

    def self_backward(norm, grad, kept, leave, spot, rows, held):
        _, low, pre, query, keys, value, context, weights = kept
        grads = shape((2, 4, mp, rows, width), BF16)
        ins = [(place, SMEM)] + [(v, VMEM) for v in (grad, low, pre, query, keys, value, context)]
        ins += [(weights, ANY), (params, VMEM), (code_col, VMEM), (code_row, VMEM)]
        return call(
            partial(self_backward_kernel, leave, norm, spot, len(held)),
            ins + [(v, ANY) for v in held],
            [(row_low if leave else token_shape, VMEM), (small_shape, VMEM)] + [(grads, ANY)] * 2,
            [square, square] + [token_bf16] * 4 + [dma((4,)), dma],
            {len(ins) + i: 2 + i for i in range(len(held))},
        )

    def feed_self_forward(layer, norm, next_layer, next_norm, rows):
        pieces, following = feed_pieces[layer], attention_pieces[next_layer]
        outs = call(
            partial(
                feed_self_forward_kernel, layer, norm, feed_at[layer], next_layer, next_norm, attention_at[next_layer],
                len(pieces), len(following),
            ),
            [(place, SMEM), (rows, VMEM)]
            + [(v, ANY) for v in (feed_in, feed_out, inward, attention_out, *pieces, *following)]
            + [(bias, VMEM), (params, VMEM), (code_col, VMEM), (code_row, VMEM)],
            [(token_shape, VMEM), (token_low, VMEM), (token_shape, VMEM)]
            + [(inner_shape, ANY), (inner_low, ANY), (kept_wide, ANY)]
            + [(token_shape, VMEM), (token_low, VMEM), (token_shape, VMEM)]
            + [(token_low, VMEM)] * 4
            + [(kept_square, ANY)],
            [wide, inner_f32, inner_bf16, dma((2, mp)), dma, square, dma((4,)), dma],
        )
        return outs[:6], outs[6:]

    def feed_backward(norm, grad, kept):
        _, low, pre, slope, active, weights = kept
        return call(
            partial(feed_backward_kernel, norm),
            [(place, SMEM)] + [(v, ANY) for v in (grad, low, pre, slope, active, weights)] + [(params, VMEM)],
            [(token_shape, VMEM), (small_shape, VMEM)] + [(feed_grad, ANY)] * 2,
            [wide, wide, token_f32, token_bf16, token_f32, inner_f32, inner_bf16]
            + [dma((3 + 2 * mp,)), dma((2, mp)), dma],
        )

    def feed_both(layer, norm, rows, parts):
        return call(
            partial(feed_both_kernel, layer, norm, feed_at[layer], len(parts), len(feed_pieces[layer])),
            [(place, SMEM), (picks_in, SMEM), (rows, VMEM), (feed_in, ANY), (feed_out, ANY)]
            + [(v, ANY) for v in parts + list(feed_pieces[layer])]
            + [(bias, VMEM), (params, VMEM)],
            [(row_low, VMEM), (token_shape, VMEM), (small_shape, VMEM)] + [(feed_grad, ANY)] * 2,
            [wide, wide, inner_f32, inner_bf16, token_bf16, token_f32, token_f32, row_bf16]
            + [dma((2, mp)), dma, dma],
        )

    def pick_rows(parts):
        return call(
            pick_kernel,
            [(picks_out, SMEM)] + [(part, ANY) for part in parts],
            [(shape((own_rows, seq, width)), VMEM)],
            [row_bf16, dma],
        )[0]

    attention_pieces[0] = attention_pieces[2] = first_wide.take()
    second_wide.two_early()
    rings[TOKENS].far()
    rings["third"].far()
    projected, image_keys, image_value, kept_image = call(
        partial(image_forward_kernel, 2, attention_rows, 2 * attention_rows, image_rows, len(attention_pieces[2])),
        [(place, SMEM), (patch_rows, VMEM), (image, ANY)] + attention_ins(2) + [(bias, VMEM)],
        [(patch_low, VMEM)] * 3 + [(kept_tall, ANY)],
        [square, tall, dma((4,)), dma, dma],
    )
    at["keys"] = image_keys
    step()

    text_attention = first_forward(0, 0, rings[TOKENS].take())
    at["stream"] = text_attention[0]
    second_wide.core_late()
    third_wide = gathered("third")
    third_wide.one()
    rings[COTANGENT].up()
    step()

    attention_pieces[1] = feed_pieces[0] = second_wide.take()
    third_wide.two()
    rings[COTANGENT].down()
    text_feed, joining_attention = feed_self_forward(0, 1, 1, 2, at.pop("stream"))
    at["stream"] = joining_attention[0]
    step()

    third_wide.core()
    rings[COTANGENT].far()
    image_keys = at.pop("keys")
    cross_attention = call(
        partial(cross_forward_kernel, 2, 3, attention_rows, seq, patches, len(attention_pieces[2])),
        [(place, SMEM), (at.pop("stream"), VMEM), (image_keys, VMEM), (image_value, VMEM)]
        + attention_ins(2)
        + [(bias, VMEM), (params, VMEM)],
        [(token_shape, VMEM), (token_low, VMEM), (token_shape, VMEM), (token_shape, VMEM), (token_low, VMEM)]
        + [(kept_square, ANY)],
        [square, token_f32, dma((4,)), dma],
    )
    at["stream"] = cross_attention[0]
    step()

    feed_pieces[1] = third_wide.take()

    mixed, grad, small_joining_feed, keep, send = feed_both(1, 4, at.pop("stream"), rings[COTANGENT].take())
    mixed_ring = Ring(at, "mixed", mixed)
    at["grad"] = grad
    last_grads = Reduce(at, "last", keep, send)
    step()

    last_grads.core()
    mixed_ring.up()
    grad, small_cross, grad_keys, grad_value, cross_branch, cross_query = call(
        partial(cross_backward_kernel, 3, seq, patches),
        [(place, SMEM), (at.pop("grad"), VMEM)]
        + [(cross_attention[i], VMEM) for i in (1, 2, 3, 4)]
        + [(image_keys, VMEM), (image_value, VMEM), (cross_attention[5], ANY), (params, VMEM)],
        [(token_shape, VMEM), (small_shape, VMEM)] + [(patch_low, VMEM)] * 2 + [(token_low, VMEM)] * 2,
        [square, token_f32, token_f32, dma((4,))],
    )
    at["grad"] = grad
    step()

    last_grads.one()
    mixed_ring.down()
    middle_rows = 2 * attention_rows
    grad, small_joining, keep, send = self_backward(
        2, at.pop("grad"), joining_attention, False, attention_rows, middle_rows, ()
    )
    at["grad"] = grad
    cross_grads = (cross_attention[4], cross_branch, cross_query, cross_attention[1], grad_keys, grad_value, projected)
    keep, send = call(
        partial(cross_weights_kernel, 0),
        [(place, SMEM)] + [(v, VMEM) for v in cross_grads] + [(keep, ANY), (send, ANY)],
        [(shape(keep.shape, BF16), ANY)] * 2,
        [square, dma],
        {8: 0, 9: 1},
    )
    middle_grads = Reduce(at, "middle", keep, send)
    at["patch grads"] = grad_keys, grad_value
    step()

    last_grads.two()
    middle_grads.core()
    mixed_ring.far()
    grad, small_text_feed, keep, send = feed_backward(1, at.pop("grad"), text_feed)
    at["grad"] = grad
    first_grads = Reduce(at, "first", keep, send)
    step()

    mixed_parts = mixed_ring.take()
    middle_grads.one()
    first_grads.core()
    last_grads.combine()
    held = at["last"]
    down, across, up = held.pop("parts")
    held["up"], held["down"] = pass_on(up.astype(BF16)), pass_on(down, -1)
    held["across part"] = across
    rows_back, small_text, keep, send = self_backward(
        0, at.pop("grad"), text_attention, True, 0, attention_rows + image_rows, ()
    )
    back_ring = Ring(at, "back", rows_back)
    at["text"] = keep, send
    step()

    middle_grads.two()
    first_grads.one()
    at["last"]["across"] = pass_on(at["last"].pop("across part"), 2)
    grad_keys, grad_value = at.pop("patch grads")
    keep, send = at.pop("text")
    grad_images, small_image, keep, send = call(
        partial(image_backward_kernel, image_rows, attention_rows, 2),
        [(place, SMEM), (patch_rows, VMEM), (grad_keys, VMEM), (grad_value, VMEM), (cross_attention[5], ANY)]
        + [(kept_image, ANY), (keep, ANY), (send, ANY)],
        [(shape((patches, own_rows, image_width)), VMEM), (small_shape, VMEM)] + [(shape(keep.shape, BF16), ANY)] * 2,
        [square, tall, tall, pltpu.VMEM((n_patches, width), BF16), dma((4,)), dma, dma],
        {6: 2, 7: 3},
    )
    text_grads = Reduce(at, "text", keep, send)
    at[SMALL] = jnp.concatenate(
        [small_text, small_text_feed, small_joining, small_cross, small_joining_feed, small_image]
    )
    step()

    first_grads.two()
    text_grads.core()
    middle_grads.combine()
    middle_grads.far()
    back_ring.up()
    step()

    text_grads.one()
    middle_grads.near()
    first_grads.combine()
    first_grads.far()
    at[SMALL] = at[SMALL] + swap(at[SMALL], 1)
    at["last own"] = last_grads.owned()
    step()

    early = Widen(at, "early", *jnp.concatenate([at.pop("last own"), middle_grads.owned()], axis=1))
    early.one()
    text_grads.two()
    first_grads.near()
    back_ring.down()
    at[SMALL] = at[SMALL] + swap(at[SMALL], 2)
    step()

    early.two()
    text_grads.combine()
    text_grads.direct()
    at["first own"] = first_grads.owned()
    at[SMALL] = at[SMALL] + swap(at[SMALL], 4)
    step()

    late = Widen(at, "late", *jnp.concatenate([at.pop("first own"), text_grads.owned()], axis=1))
    late.one()
    at["mixed"] = pick_rows(mixed_parts)
    early.core()
    back_ring.far()
    at[SMALL] = at[SMALL] + swap_owner(at[SMALL], 1)
    step()

    late.two()
    at[TOKENS] = pick_rows(back_ring.take())
    early_pieces = early.take()
    smalls = at.pop(SMALL)
    smalls = smalls + swap_owner(smalls, 2)
    bit = SLICES
    while bit < lax.axis_size("dp"):
        smalls = smalls + swap(smalls, bit)
        bit *= 2
    at[SMALL] = smalls

    whole_shapes = {
        ATTENTION_IN: shape(inward.shape),
        ATTENTION_OUT: shape(attention_out.shape),
        FEED_IN: shape(feed_in.shape),
        FEED_OUT: shape(feed_out.shape),
        IMAGE: shape(image.shape),
    }
    block_of = {ATTENTION: (4, quarter, width), FEED: (2, units, width), IMAGE: (quarter, image_width)}
    names_of = {ATTENTION: [ATTENTION_IN, ATTENTION_OUT], FEED: [FEED_IN, FEED_OUT], IMAGE: [IMAGE]}
    written = {}

    def write_out(result, *blocks):
        names = list(dict.fromkeys(name for kind, _, _ in blocks for name in names_of[kind]))
        names = [name for name in names if name in written] + [name for name in names if name not in written]
        held = [name for name in names if name in written]
        scratch = [pltpu.VMEM(block_of[kind], form) for kind, _, _ in blocks for form in (BF16, F32)]
        results = call(
            partial(finish_kernel, blocks, quarter, names, len(held), len(result)),
            [(place, SMEM)] + [(v, ANY) for v in result] + [(written[name], ANY) for name in held],
            [(whole_shapes[name], ANY) for name in names],
            scratch + [dma((len(blocks),)), dma((len(blocks),))],
            {1 + len(result) + i: i for i in range(len(held))},
        )
        written.update(zip(names, results))

    write_out(
        early_pieces, (FEED, 0, 1), (ATTENTION, feed_rows, 2), (ATTENTION, feed_rows + attention_rows, 1)
    )
    at["written"] = written
    step()
    written = at.pop("written")
    late.core()
    smalls = at.pop(SMALL).reshape(6, 8, width)

    def own_part(values):
        return lax.dynamic_slice_in_dim(values, owner * quarter, quarter, axis=values.ndim - 1)

    grad_query_value_bias = own_part(jnp.stack([smalls[i, 3:5] for i in (0, 2, 3)]))
    grad_feed_bias = jnp.stack([smalls[i, 3 : 3 + mp].reshape(-1) for i in (1, 4)])
    grad_feed_bias = lax.dynamic_slice_in_dim(grad_feed_bias, owner * units, units, axis=1)
    vectors = (
        grad_query_value_bias, smalls[:5, 2], grad_feed_bias, own_part(smalls[5, 0]), smalls[:5, 0], smalls[:5, 1]
    )
    at["vectors"] = vectors
    step()
    vectors = at.pop("vectors")
    write_out(
        late.take(), (FEED, 0, 0), (ATTENTION, feed_rows, 0), (IMAGE, feed_rows + attention_rows, 0)
    )
    return (
        at["mixed"],
        at[TOKENS],
        grad_images.transpose(1, 0, 2),
        written[ATTENTION_IN].transpose(0, 1, 3, 2),
        vectors[0],
        written[ATTENTION_OUT],
        vectors[1],
        written[FEED_IN],
        vectors[2],
        written[FEED_OUT],
        written[IMAGE].T,
        vectors[3],
        vectors[4],
        vectors[5],
    )


def solution(mesh):
    rows = P(("dp", "mp"), None, None)
    return jax.shard_map(
        on_device,
        mesh=mesh,
        in_specs=(
            rows,
            rows,
            P("dp", None),
            P("dp"),
            P(None, None, None, "mp"),
            P(None, None, "mp"),
            P(None, "mp", None),
            P(),
            P(None, None, "mp"),
            P(None, "mp"),
            P(None, "mp", None),
            P(None, "mp"),
            P("mp"),
            P(),
            P(),
            rows,
        ),
        out_specs=(
            rows,
            rows,
            rows,
            P(None, None, None, "mp"),
            P(None, None, "mp"),
            P(None, "mp", None),
            P(),
            P(None, None, "mp"),
            P(None, "mp"),
            P(None, "mp", None),
            P(None, "mp"),
            P("mp"),
            P(),
            P(),
        ),
        check_vma=False,
    )
```

```python
from functools import partial

import jax
import jax.numpy as jnp
from jax import lax
from jax.experimental import pallas as pl
from jax.experimental.pallas import tpu as pltpu
from jax.sharding import PartitionSpec as P

HEAD_DIM = 64
STACK = 4 * HEAD_DIM
TOGETHER = 6
SLICES = 8
EPSILON = 1e-06
BLOCKED = -1000000000.0
SCALE = HEAD_DIM ** (-0.5)
DISTANCES = ((0, 2, 4, 6), (0, 4, 2, 6))
ATTENTION, FEED, IMAGE, ATTENTION_IN, ATTENTION_OUT, FEED_IN, FEED_OUT = range(7)
SMALL, TOKENS, COTANGENT = "small", "tokens", "cotangent"
F32 = jnp.float32
BF16 = jnp.bfloat16

ANY = pl.BlockSpec(memory_space=pl.ANY)
VMEM = pl.BlockSpec(memory_space=pltpu.VMEM)
SMEM = pl.BlockSpec(memory_space=pltpu.SMEM)


def swap(values, bit):
    count = lax.axis_size("dp")
    return lax.ppermute(values, "dp", [(i, i ^ bit) for i in range(count)])


def pass_on(values, way=1):
    count = lax.axis_size("mp")
    return lax.ppermute(values, "mp", [(i, (i + way) % count) for i in range(count)])


def swap_owner(values, bit):
    count = lax.axis_size("mp")
    return lax.ppermute(values, "mp", [(i, i ^ bit) for i in range(count)])


def added(*terms):
    total = terms[0].astype(F32)
    for term in terms[1:]:
        total = total + term
    return total.astype(BF16)


def dot_nn(left, right):
    return lax.dot_general(left, right, (((1,), (0,)), ((), ())), preferred_element_type=F32)


def dot_nt(left, right):
    return lax.dot_general(left, right, (((1,), (1,)), ((), ())), preferred_element_type=F32)


def dot_tn(left, right):
    return lax.dot_general(left, right, (((0,), (0,)), ((), ())), preferred_element_type=F32)


def start(source, target, sem):
    pltpu.make_async_copy(source, target, sem).start()


def finish(whole, sem):
    pltpu.make_async_copy(whole, whole, sem).wait()


def aligned(first, count, step=16):
    return pl.ds(pl.multiple_of(first, step), count)


def each_slice(place, first_step, mp):
    for core in range(2):
        for half in range(2):
            for entry in range(4):
                slot = place[0] ^ (core ^ DISTANCES[half][entry])
                for step in range(first_step, mp):
                    yield core, half, entry, step, slot, (place[1] + mp - step) % mp


def piece_of(pieces, core, half, entry):
    if len(pieces) == 2:
        return pieces[core].at[half, entry]
    return pieces[2 * core + entry // 2].at[half, entry % 2]


def attention_spot(whole, quarter, half, slot, owner):
    span = 4 * quarter // SLICES
    count = quarter // span
    row = owner * quarter + (slot % count) * span + half * (span // 2)
    return whole.at[slot // count, aligned(row, span // 2)]


def load_attention(place, own, pieces, offset, layer, whole, sems):
    mp = pieces[0].shape[2] + 1
    quarter = whole.shape[1] // mp
    rows = quarter // 4
    for mat in range(4):
        source = own[0].at[layer, mat] if mat < 3 else own[1].at[layer]
        start(source, whole.at[mat, aligned(place[1] * quarter, quarter)], sems.at[mat])
    for core, half, entry, step, slot, owner in each_slice(place, 1, mp):
        start(
            piece_of(pieces, core, half, entry).at[step - 1, pl.ds(offset, rows)],
            attention_spot(whole, quarter, half, slot, owner),
            sems.at[slot // 2],
        )


def store_attention(place, whole, outs, offset, sem):
    mp = outs[0].shape[2]
    quarter = whole.shape[1] // mp
    for core, half, entry, step, slot, owner in each_slice(place, 0, mp):
        start(
            attention_spot(whole, quarter, half, slot, owner),
            outs[core].at[half, entry, step, pl.ds(offset, quarter // 4)],
            sem,
        )


def feed_spot(whole, half, slot, step):
    span = whole.shape[2] // SLICES
    return whole.at[half, step, aligned(slot * span, span)]


def load_feed(place, own, pieces, offset, layer, half, step, whole, sems):
    rows = whole.shape[2] // SLICES
    if step == 0:
        start(own[half].at[layer], whole.at[half, 0], sems.at[half, 0])
        return
    for core in range(2):
        for entry in range(4):
            slot = place[0] ^ (core ^ DISTANCES[half][entry])
            start(
                piece_of(pieces, core, half, entry).at[step - 1, pl.ds(offset, rows)],
                feed_spot(whole, half, slot, step),
                sems.at[half, step],
            )


def store_feed(place, whole, outs, half, step, sem):
    for core in range(2):
        for entry in range(4):
            slot = place[0] ^ (core ^ DISTANCES[half][entry])
            start(feed_spot(whole, half, slot, step), outs[core].at[half, entry, step], sem)


def image_copies(whole, piece, quarter, half, slot, owner, sem, inward):
    rows, width = piece.shape
    span = 2 * rows
    beyond = whole.shape[1] - width
    blocks = width // beyond
    plain = quarter // span
    base = owner * quarter + half * rows

    def move(inner, outer):
        start(inner, outer, sem) if inward else start(outer, inner, sem)

    @pl.when(slot < plain)
    def _():
        move(piece, whole.at[aligned(base + slot * span, rows), pl.ds(0, width)])

    @pl.when(slot >= plain)
    def _():
        for block in range(blocks):
            row = base + block * (quarter // blocks) + (slot - plain) * span
            move(
                piece.at[:, pl.ds(block * beyond, beyond)],
                whole.at[aligned(row, rows), pl.ds(width, beyond)],
            )


def load_image(place, own, pieces, offset, rows, whole, sem):
    mp = pieces[0].shape[2] + 1
    quarter = whole.shape[0] // mp
    start(own, whole.at[aligned(place[1] * quarter, quarter)], sem)
    for core, half, entry, step, slot, owner in each_slice(place, 1, mp):
        piece = piece_of(pieces, core, half, entry).at[step - 1, pl.ds(offset, rows)]
        image_copies(whole, piece, quarter, half, slot, owner, sem, True)


def store_image(place, whole, outs, offset, rows, sem):
    mp = outs[0].shape[2]
    quarter = whole.shape[0] // mp
    for core, half, entry, step, slot, owner in each_slice(place, 0, mp):
        piece = outs[core].at[half, entry, step, pl.ds(offset, rows)]
        image_copies(whole, piece, quarter, half, slot, owner, sem, False)


def norm_rows(values, gain_row, shift_row):
    center = values - jnp.mean(values, axis=-1, keepdims=True)
    moment = jnp.mean(center * center, axis=-1, keepdims=True)
    return center * lax.rsqrt(moment + EPSILON) * gain_row + shift_row


def norm_back(pre_norm, gain_row, grad_out, small):
    center = pre_norm - jnp.mean(pre_norm, axis=-1, keepdims=True)
    scale = lax.rsqrt(jnp.mean(center * center, axis=-1, keepdims=True) + EPSILON)
    normal = center * scale
    lifted = grad_out * gain_row
    grad_pre = scale * (
        lifted
        - jnp.mean(lifted, axis=-1, keepdims=True)
        - normal * jnp.mean(lifted * normal, axis=-1, keepdims=True)
    )
    small[...] = jnp.zeros_like(small)
    small[0:1] = jnp.sum(grad_out * normal, axis=0, keepdims=True)
    small[1:2] = jnp.sum(grad_out, axis=0, keepdims=True)
    small[2:3] = jnp.sum(grad_pre, axis=0, keepdims=True)
    return grad_pre


def column_total(values):
    return jnp.sum(values.astype(F32), axis=0, keepdims=True)


def spread_heads(values):
    lane = lax.broadcasted_iota(jnp.int32, (1, values.shape[1]), 1)
    parts = []
    for first in range(0, values.shape[1], HEAD_DIM):
        mask = ((lane >= first) & (lane < first + HEAD_DIM)).astype(F32).astype(values.dtype)
        parts.append(values * mask)
    return jnp.concatenate(parts, axis=0)


def pick_heads(values):
    lane = lax.broadcasted_iota(jnp.int32, (1, values.shape[1]), 1)
    rows = values.shape[0] * HEAD_DIM // values.shape[1]
    picked = values[:rows]
    for head in range(1, values.shape[1] // HEAD_DIM):
        picked = jnp.where(lane >= head * HEAD_DIM, values[head * rows : (head + 1) * rows], picked)
    return picked


def softmax(scores):
    raised = jnp.exp(scores - jnp.max(scores, axis=-1, keepdims=True))
    return raised * (1.0 / jnp.sum(raised, axis=-1, keepdims=True))


def score_back(weights, grad_weights):
    along = weights * grad_weights
    return (along - weights * jnp.sum(along, axis=-1, keepdims=True)).astype(BF16)


def attention_units(count, row_size, place_size, width):
    units = []
    for number in range(count):
        rows = slice(number * row_size, (number + 1) * row_size)
        places = slice(number * place_size, (number + 1) * place_size)
        units += [(number, rows, places, slice(first, first + STACK)) for first in range(0, width, STACK)]
    return [units[first : first + TOGETHER] for first in range(0, len(units), TOGETHER)]


def attend_forward(units, allowed, query, keys, value, context):
    for group in units:
        scores = [dot_nt(spread_heads(query[rows, lanes]).astype(BF16), keys[at, lanes]) for _, rows, at, lanes in group]
        weights = [
            softmax(jnp.where(allowed(unit[0]), score * SCALE, BLOCKED)).astype(BF16)
            for unit, score in zip(group, scores)
        ]
        for (_, rows, at, lanes), weight in zip(group, weights):
            context[rows, lanes] = pick_heads(dot_nn(weight, value[at, lanes])).astype(context.dtype)


def attend_backward(units, allowed, query, keys, value, grad_context, grad_query, grad_keys, grad_value):
    for group in units:
        queries = [spread_heads(query[rows, lanes]).astype(BF16) for _, rows, _, lanes in group]
        contexts = [spread_heads(grad_context[rows, lanes]).astype(BF16) for _, rows, _, lanes in group]
        scores = [dot_nt(one, keys[at, lanes]) for one, (_, _, at, lanes) in zip(queries, group)]
        grad_weights = [dot_nt(one, value[at, lanes]) for one, (_, _, at, lanes) in zip(contexts, group)]
        weights = [
            softmax(jnp.where(allowed(unit[0]), score * SCALE, BLOCKED)) for unit, score in zip(group, scores)
        ]
        grad_scores = [score_back(one, other) for one, other in zip(weights, grad_weights)]
        for weight, one, (_, _, at, lanes) in zip(weights, contexts, group):
            grad_value[at, lanes] = dot_tn(weight.astype(BF16), one).astype(BF16)
        for grad_score, one, (_, _, at, lanes) in zip(grad_scores, queries, group):
            grad_keys[at, lanes] = (dot_tn(grad_score, one) * SCALE).astype(BF16)
        for grad_score, (_, rows, at, lanes) in zip(grad_scores, group):
            mixed = pick_heads(dot_nn(grad_score, keys[at, lanes])) * SCALE
            grad_query[rows, lanes] = mixed.astype(grad_query.dtype)


def same_segment(code_col, code_row):
    size = code_row.shape[1]

    def allowed(group):
        column = code_col[group * size : (group + 1) * size]
        return jnp.concatenate([column] * (STACK // HEAD_DIM), axis=0) == code_row[group : group + 1]

    return allowed


def real_patch(size, patches):
    column = lax.broadcasted_iota(jnp.int32, (1, size), 1)
    return lambda row: column < patches


def pick_copies(picks, parts, target, sem):
    size = parts[0].shape[0]
    for row in range(target.shape[0]):
        for number, part in enumerate(parts):

            @pl.when(picks[row] // size == number)
            def _():
                start(part.at[picks[row] % size], target.at[row], sem)


def flat_rows(rows_ref, target):
    seq = rows_ref.shape[1]
    for row in range(rows_ref.shape[0]):
        target[row * seq : (row + 1) * seq] = rows_ref[row].astype(target.dtype)


def leave_rows(values, target):
    seq = target.shape[1]
    for row in range(target.shape[0]):
        target[row] = values[row * seq : (row + 1) * seq].astype(target.dtype)


def slice_kernel(
    place, head_bias, unit_bias, patch_bias, inward, outward, feed_in, feed_out, image, first, second, third, sems,
):
    slot = place[0]
    quarter, width = inward.shape[2:]
    span = 4 * quarter // SLICES
    count = quarter // span
    rows = span // 2
    feed_rows = feed_in.shape[1] // SLICES
    image_rows = first.shape[1] - 2 * rows - 16
    weights = first.at[:, pl.ds(0, 2 * rows + image_rows)]
    table = jnp.concatenate(
        [
            jnp.concatenate([head_bias[i].astype(F32) for i in range(head_bias.shape[0])], axis=0),
            jnp.zeros((6, width - quarter), F32),
        ],
        axis=1,
    )
    patch = jnp.concatenate([patch_bias[...].astype(F32), jnp.zeros((1, width - quarter), F32)], axis=1)
    table = jnp.concatenate([table, unit_bias[...].astype(F32), patch, jnp.zeros((7, width), F32)], axis=0)
    first[0, 2 * rows + image_rows :] = table.astype(BF16)
    first[1, 2 * rows + image_rows :] = jnp.zeros((16, width), BF16)

    def attention(layer, target, offset, sem):
        for half in range(2):
            row = (slot % count) * span + half * rows
            spot = target.at[half, pl.ds(offset, rows)]

            @pl.when(slot < 3 * count)
            def _():
                start(inward.at[layer, slot // count, aligned(row, rows)], spot, sem)

            @pl.when(slot >= 3 * count)
            def _():
                start(outward.at[layer, aligned(row, rows)], spot, sem)

    def feed(layer, target, offset, sem):
        for half, source in enumerate((feed_in, feed_out)):
            spot = target.at[half, pl.ds(offset, feed_rows)]
            start(source.at[layer, aligned(slot * feed_rows, feed_rows)], spot, sem)

    attention(0, first, 0, sems.at[0])
    attention(2, first, rows, sems.at[0])
    for half in range(2):
        spot = first.at[half, pl.ds(2 * rows, image_rows)]
        image_copies(image, spot, quarter, half, slot, 0, sems.at[0], False)
    feed(0, second, 0, sems.at[1])
    attention(1, second, feed_rows, sems.at[1])
    feed(1, third, 0, sems.at[2])
    for number, target in enumerate((weights, second, third)):
        finish(target, sems.at[number])


def self_forward(
    layer, norm, stream, bias, params, code_col, code_row, out, low, pre, query, keys, value, context, kept, whole, sems,
    out_sem,
):
    hb = stream.astype(BF16)
    low[...] = hb
    finish(whole.at[0], sems.at[0])
    query[...] = (dot_nt(hb, whole[0]) + bias[2 * layer : 2 * layer + 1]).astype(BF16)
    finish(whole.at[1], sems.at[1])
    keys[...] = dot_nt(hb, whole[1]).astype(BF16)
    finish(whole.at[2], sems.at[2])
    value[...] = (dot_nt(hb, whole[2]) + bias[2 * layer + 1 : 2 * layer + 2]).astype(BF16)
    groups, size = code_row.shape
    units = attention_units(groups, size, size, hb.shape[1])
    attend_forward(units, same_segment(code_col, code_row), query, keys, value, context)
    finish(whole.at[3], sems.at[3])
    start(whole, kept, out_sem)
    total = dot_nn(context[...], whole[3]) + params[3 * norm : 3 * norm + 1] + stream
    pre[...] = total
    out[...] = norm_rows(total, params[3 * norm + 1 : 3 * norm + 2], params[3 * norm + 2 : 3 * norm + 3])
    finish(whole, out_sem)


def self_forward_kernel(
    layer, norm, offset, n_parts, n_pieces, place, picks, *refs,
):
    parts, (inward, outward), refs = refs[:n_parts], refs[n_parts : n_parts + 2], refs[n_parts + 2 :]
    pieces, refs = refs[:n_pieces], refs[n_pieces:]
    held = refs[15:]
    if held:
        pick_copies(picks, parts, held[0], held[2])
    load_attention(place, (inward, outward), pieces, offset, layer, refs[12], refs[13])
    if held:
        finish(held[0], held[2])
        flat_rows(held[0], held[1])
        stream = held[1][...]
    else:
        stream = parts[0][...]
    self_forward(layer, norm, stream, *refs[:15])


def feed_self_forward_kernel(
    layer, norm, offset, next_layer, next_norm, next_offset, n_pieces, n_next, place, rows_ref, first_weight, second_weight,
    inward, outward, *refs,
):
    pieces, following, refs = refs[:n_pieces], refs[n_pieces : n_pieces + n_next], refs[n_pieces + n_next :]
    bias, params, code_col, code_row = refs[:4]
    feed_outs, self_outs, scratch = refs[4:10], refs[10:18], refs[18:]
    whole, slope, active, sems, out_sem, square, square_sems, square_out = scratch
    feed_refs = (bias, params, *feed_outs, whole, slope, active, sems, out_sem)
    for step in range(whole.shape[1]):
        for half in range(2):
            load_feed(place, (first_weight, second_weight), pieces, offset, layer, half, step, whole, sems)
    load_attention(place, (inward, outward), following, next_offset, next_layer, square, square_sems)
    feed_forward(layer, norm, place, rows_ref, *feed_refs)
    self_forward(
        next_layer, next_norm, feed_outs[0][...], bias, params, code_col, code_row, *self_outs, square, square_sems, square_out
    )


def load_kept(kept, whole, sems, order):
    for mat in order:
        start(kept.at[mat], whole.at[mat], sems.at[mat])


def self_backward_kernel(
    leave, norm, spot, n_held, place, grad, low, pre, query, keys, value, context, kept, params, code_col, code_row, *refs,
):
    out, small, keep, send, whole, grads, grad_context, grad_query, grad_keys, grad_value, sems, out_sem = refs[n_held:]
    load_kept(kept, whole, sems, (3, 0, 1, 2))
    grad_pre = norm_back(pre[...], params[3 * norm + 1 : 3 * norm + 2], grad[...], small)
    branch = grad_pre.astype(BF16)
    finish(whole.at[3], sems.at[3])
    grad_context[...] = dot_nt(branch, whole[3]).astype(BF16)
    grads[3] = dot_tn(context[...], branch).astype(BF16)
    groups, size = code_row.shape
    units = attention_units(groups, size, size, branch.shape[1])
    attend_backward(
        units, same_segment(code_col, code_row), query, keys, value, grad_context, grad_query, grad_keys, grad_value
    )
    hb = low[...]
    grads[0] = dot_tn(grad_query[...], hb).astype(BF16)
    grads[1] = dot_tn(grad_keys[...], hb).astype(BF16)
    grads[2] = dot_tn(grad_value[...], hb).astype(BF16)
    store_attention(place, grads, (keep, send), spot, out_sem)
    small[3:4] = column_total(grad_query[...])
    small[4:5] = column_total(grad_value[...])
    total = grad_pre
    for mat, part in enumerate((grad_query, grad_keys, grad_value)):
        finish(whole.at[mat], sems.at[mat])
        total = total + dot_nn(part[...], whole[mat])
    if leave:
        leave_rows(total, out)
    else:
        out[...] = total
    finish(grads, out_sem)


def feed_forward(
    layer, norm, place, rows_ref, bias, params, out, low, pre, slope_out, active_out, kept, whole, slope, active, sems, out_sem,
):
    parts = whole.shape[1]
    stream = rows_ref[...]
    hb = stream.astype(BF16)
    low[...] = hb
    total = params[3 * norm : 3 * norm + 1] + stream
    for step in range(parts):
        row = 6 + layer * parts + (place[1] + parts - step) % parts
        finish(whole.at[0, step], sems.at[0, step])
        units = dot_nn(hb, whole[0, step]) + bias[pl.ds(row, 1)]
        share = 0.5 * (1.0 + lax.erf(units * (2.0 ** -0.5)))
        slope[step] = share + units * jnp.exp(-0.5 * units * units) * 0.3989422804014327
        start(slope.at[step], slope_out.at[step], out_sem)
        gated = (units * share).astype(BF16)
        active[step] = gated
        start(active.at[step], active_out.at[step], out_sem)
        start(whole.at[0, step], kept.at[0, step], out_sem)
        finish(whole.at[1, step], sems.at[1, step])
        start(whole.at[1, step], kept.at[1, step], out_sem)
        total = total + dot_nn(gated, whole[1, step])
    pre[...] = total
    out[...] = norm_rows(total, params[3 * norm + 1 : 3 * norm + 2], params[3 * norm + 2 : 3 * norm + 3])
    finish(slope, out_sem)
    finish(active, out_sem)
    finish(whole, out_sem)


def feed_backward_kernel(
    norm, place, grad_in, low_in, pre_in, slope_in, active_in, kept, params,
    out, small, keep, send, whole, grads, grad, low, pre, slope, active, row_sems, sems, out_sem,
):
    parts = whole.shape[1]
    start(grad_in, grad, row_sems.at[0])
    start(pre_in, pre, row_sems.at[1])
    for step in range(parts):
        start(active_in.at[step], active.at[step], row_sems.at[3 + step])
        start(kept.at[1, step], whole.at[1, step], sems.at[1, step])
        start(slope_in.at[step], slope.at[step], row_sems.at[3 + parts + step])
        if step == 0:
            start(low_in, low, row_sems.at[2])
        start(kept.at[0, step], whole.at[0, step], sems.at[0, step])
    finish(grad, row_sems.at[0])
    finish(pre, row_sems.at[1])
    grad_pre = norm_back(pre[...], params[3 * norm + 1 : 3 * norm + 2], grad[...], small)
    branch = grad_pre.astype(BF16)
    total = grad_pre
    for step in range(parts):
        finish(active.at[step], row_sems.at[3 + step])
        grads[1, step] = dot_tn(active[step], branch).astype(BF16)
        store_feed(place, grads, (keep, send), 1, step, out_sem)
        finish(whole.at[1, step], sems.at[1, step])
        finish(slope.at[step], row_sems.at[3 + parts + step])
        grad_units = (dot_nt(branch, whole[1, step]) * slope[step]).astype(BF16)
        if step == 0:
            finish(low, row_sems.at[2])
        grads[0, step] = dot_tn(low[...], grad_units).astype(BF16)
        store_feed(place, grads, (keep, send), 0, step, out_sem)
        small[pl.ds(3 + (place[1] + parts - step) % parts, 1)] = column_total(grad_units)
        finish(whole.at[0, step], sems.at[0, step])
        total = total + dot_nt(grad_units, whole[0, step])
    out[...] = total
    finish(grads, out_sem)


def feed_both_kernel(
    layer, norm, offset, n_parts, n_pieces, place, picks, rows_ref, first_weight, second_weight, *refs,
):
    arrived, pieces, refs = refs[:n_parts], refs[n_parts : n_parts + n_pieces], refs[n_parts + n_pieces :]
    bias, params, mixed, out, small, keep, send, whole, grads, slope, active, low, pre, grad, held, sems, row_sem, out_sem = refs
    parts = whole.shape[1]
    for step in range(parts):
        for half in range(2):
            load_feed(place, (first_weight, second_weight), pieces, offset, layer, half, step, whole, sems)
    pick_copies(picks, arrived, held, row_sem)
    stream = rows_ref[...]
    low[...] = stream.astype(BF16)
    total = params[3 * norm : 3 * norm + 1] + stream
    for step in range(parts):
        row = 6 + layer * parts + (place[1] + parts - step) % parts
        finish(whole.at[0, step], sems.at[0, step])
        units = dot_nn(low[...], whole[0, step]) + bias[pl.ds(row, 1)]
        share = 0.5 * (1.0 + lax.erf(units * (2.0 ** -0.5)))
        slope[step] = share + units * jnp.exp(-0.5 * units * units) * 0.3989422804014327
        gated = (units * share).astype(BF16)
        active[step] = gated
        finish(whole.at[1, step], sems.at[1, step])
        total = total + dot_nn(gated, whole[1, step])
    pre[...] = total
    gain, shift = params[3 * norm + 1 : 3 * norm + 2], params[3 * norm + 2 : 3 * norm + 3]
    leave_rows(norm_rows(total, gain, shift), mixed)
    finish(held, row_sem)
    flat_rows(held, grad)
    grad_pre = norm_back(pre[...], gain, grad[...], small)
    branch = grad_pre.astype(BF16)
    total = grad_pre
    for step in range(parts):
        grads[1, step] = dot_tn(active[step], branch).astype(BF16)
        store_feed(place, grads, (keep, send), 1, step, out_sem)
        grad_units = (dot_nt(branch, whole[1, step]) * slope[step]).astype(BF16)
        grads[0, step] = dot_tn(low[...], grad_units).astype(BF16)
        store_feed(place, grads, (keep, send), 0, step, out_sem)
        small[pl.ds(3 + (place[1] + parts - step) % parts, 1)] = column_total(grad_units)
        total = total + dot_nt(grad_units, whole[0, step])
    out[...] = total
    finish(grads, out_sem)


def finish_all(whole, sems):
    for mat in range(whole.shape[0]):
        finish(whole.at[mat], sems.at[mat])


def image_forward_kernel(
    layer, offset, image_offset, image_rows, n_pieces, place, images, image, inward, outward, *refs,
):
    pieces, refs = refs[:n_pieces], refs[n_pieces:]
    bias, projected, keys, value, kept_image, whole, whole_image, sems, image_sem, out_sem = refs
    load_image(place, image, pieces, image_offset, image_rows, whole_image, image_sem)
    load_attention(place, (inward, outward), pieces, offset, layer, whole, sems)
    finish(whole_image, image_sem)
    start(whole_image, kept_image, out_sem)
    size = images.shape[0] // 4
    last = bias.shape[0] - 1
    for first in range(0, images.shape[0], size):
        rows = slice(first, first + size)
        source = (dot_nt(images[rows], whole_image[...]) + bias[last : last + 1]).astype(BF16)
        projected[rows] = source
        if first == 0:
            finish_all(whole, sems)
        keys[rows] = dot_nt(source, whole[1]).astype(BF16)
        value[rows] = (dot_nt(source, whole[2]) + bias[2 * layer + 1 : 2 * layer + 2]).astype(BF16)
    finish(whole_image, out_sem)


def cross_forward_kernel(
    layer, norm, offset, seq, patches, n_pieces, place, rows_ref, keys, value, inward, outward, *refs,
):
    pieces, refs = refs[:n_pieces], refs[n_pieces:]
    bias, params, out, low, pre, query, context, kept, whole, mixed, sems, out_sem = refs
    load_attention(place, (inward, outward), pieces, offset, layer, whole, sems)
    stream = rows_ref[...]
    hb = stream.astype(BF16)
    low[...] = hb
    finish_all(whole, sems)
    start(whole, kept, out_sem)
    query[...] = (dot_nt(hb, whole[0]) + bias[2 * layer : 2 * layer + 1]).astype(BF16).astype(F32)
    count = stream.shape[0] // seq
    size = keys.shape[0] // count
    units = attention_units(count, seq, size, hb.shape[1])
    attend_forward(units, real_patch(size, patches), query, keys, value, mixed)
    context[...] = mixed[...].astype(BF16)
    total = dot_nn(context[...], whole[3]) + params[3 * norm : 3 * norm + 1] + stream
    pre[...] = total
    out[...] = norm_rows(total, params[3 * norm + 1 : 3 * norm + 2], params[3 * norm + 2 : 3 * norm + 3])
    finish(whole, out_sem)


def cross_backward_kernel(
    norm, seq, patches, place, grad, low, pre, query, context, keys, value, kept, params,
    out, small, grad_keys, grad_value, branch_out, query_out, whole, grad_context, grad_query, sems,
):
    load_kept(kept, whole, sems, (3, 0))
    grad_pre = norm_back(pre[...], params[3 * norm + 1 : 3 * norm + 2], grad[...], small)
    branch = grad_pre.astype(BF16)
    branch_out[...] = branch
    finish(whole.at[3], sems.at[3])
    grad_context[...] = dot_nt(branch, whole[3]).astype(BF16).astype(F32)
    count = branch.shape[0] // seq
    size = keys.shape[0] // count
    units = attention_units(count, seq, size, branch.shape[1])
    attend_backward(
        units, real_patch(size, patches), query, keys, value, grad_context, grad_query, grad_keys, grad_value
    )
    query_low = grad_query[...].astype(BF16)
    query_out[...] = query_low
    small[3:4] = column_total(query_low)
    small[4:5] = column_total(grad_value[...])
    finish(whole.at[0], sems.at[0])
    out[...] = grad_pre + dot_nn(query_low, whole[0])


def cross_weights_kernel(
    spot, place, context, branch, grad_query, low, grad_keys, grad_value, source, keep_held, send_held,
    keep, send, grads, out_sem,
):
    grads[3] = dot_tn(context[...], branch[...]).astype(BF16)
    grads[0] = dot_tn(grad_query[...], low[...]).astype(BF16)
    grads[1] = dot_tn(grad_keys[...], source[...]).astype(BF16)
    grads[2] = dot_tn(grad_value[...], source[...]).astype(BF16)
    store_attention(place, grads, (keep, send), spot, out_sem)
    finish(grads, out_sem)


def image_backward_kernel(
    image_rows, spot, n_held, place, images, grad_keys, grad_value, kept, kept_image, *refs,
):
    out, small, keep, send, whole, whole_image, grads, low, sems, image_sem, out_sem = refs[n_held:]
    load_kept(kept, whole, sems, (1, 2))
    start(kept_image, whole_image, image_sem)
    finish(whole.at[1], sems.at[1])
    finish(whole.at[2], sems.at[2])
    finish(whole_image, image_sem)
    patches, count = out.shape[:2]
    size = images.shape[0] // count
    small[...] = jnp.zeros_like(small)
    for row in range(count):
        rows = slice(row * size, (row + 1) * size)
        source = dot_nn(grad_keys[rows], whole[1]) + dot_nn(grad_value[rows], whole[2])
        source = source.astype(BF16)
        low[rows] = source
        out[:, row, :] = dot_nn(source, whole_image[...])[:patches]
    grads[...] = dot_tn(low[...], images[...]).astype(BF16)
    store_image(place, grads, (keep, send), spot, image_rows, out_sem)
    small[0:1] = column_total(low[...])
    finish(grads, out_sem)


def combine_kernel(
    keep, core, one0, one1, two0, two1, own, down, across, up, kept, arrived, first, second, sems,
):
    for half, (one, two) in enumerate(((one0, two0), (one1, two1))):
        start(keep.at[half, 0], kept.at[half], sems.at[0])
        start(core.at[half, 0], arrived.at[half], sems.at[1])
        start(one.at[0], first.at[half], sems.at[2])
        start(two, second.at[half], sems.at[3])
    for number, target in enumerate((kept, arrived, first, second)):
        finish(target, sems.at[number])
    for step, target in enumerate((own, down, across, up)):
        for half in range(2):
            total = kept[half, step].astype(F32) + arrived[half, step].astype(F32)
            total = total + first[half, step].astype(F32) + second[half, step].astype(F32)
            target[half] = total.astype(target.dtype)


def pick_kernel(picks, *refs):
    *parts, out, held, sem = refs
    pick_copies(picks, parts, held, sem)
    finish(held, sem)
    out[...] = held[...].astype(out.dtype)


def finish_kernel(blocks, quarter, names, held, n_results, place, *refs):
    results, refs = refs[:n_results], refs[n_results:]
    width = results[0].shape[3]
    targets = dict(zip(names, refs[held:]))
    scratch = refs[held + len(names) :]
    sem, out_sem = scratch[-2:]
    for number, (kind, offset, _) in enumerate(blocks):
        buffer = scratch[2 * number]
        for core in range(2):
            for half in range(2):
                for entry in range(4):
                    if n_results == 1:
                        slot = core ^ DISTANCES[half][entry]
                        piece = results[0].at[slot, half]
                    else:
                        slot = place[0] ^ (core ^ DISTANCES[half][entry])
                        piece = piece_of(results, core, half, entry)
                    if kind == ATTENTION:
                        rows = quarter // 4
                        spot = attention_spot(buffer, quarter, half, slot, 0)
                        start(piece.at[pl.ds(offset, rows)], spot, sem.at[number])
                    elif kind == FEED:
                        rows = buffer.shape[1] // SLICES
                        spot = buffer.at[half, aligned(slot * rows, rows)]
                        start(piece.at[pl.ds(offset, rows)], spot, sem.at[number])
                    else:
                        rows = quarter * buffer.shape[1] // width // SLICES // 2
                        piece = piece.at[pl.ds(offset, rows)]
                        image_copies(buffer, piece, quarter, half, slot, 0, sem.at[number], True)
    for number, (kind, _, layer) in enumerate(blocks):
        buffer, wide = scratch[2 * number : 2 * number + 2]
        done = out_sem.at[number]
        finish(buffer, sem.at[number])
        wide[...] = buffer[...].astype(F32)
        if kind == ATTENTION:
            start(wide.at[pl.ds(0, 3)], targets[ATTENTION_IN].at[layer], done)
            start(wide.at[3], targets[ATTENTION_OUT].at[layer], done)
        elif kind == FEED:
            start(wide.at[0], targets[FEED_IN].at[layer], done)
            start(wide.at[1], targets[FEED_OUT].at[layer], done)
        else:
            start(wide, targets[IMAGE], done)
    for number in range(len(blocks)):
        finish(scratch[2 * number + 1], out_sem.at[number])


def shape(dims, kind=F32):
    return jax.ShapeDtypeStruct(tuple(dims), kind)


def call(kernel, ins, outs, scratch, aliases=None, megabytes=60):
    return pl.pallas_call(
        kernel,
        in_specs=[spec for _, spec in ins],
        out_specs=[spec for _, spec in outs],
        out_shape=[s for s, _ in outs],
        scratch_shapes=scratch,
        input_output_aliases=aliases or {},
        compiler_params=pltpu.CompilerParams(vmem_limit_bytes=megabytes << 20),
        cost_estimate=pl.CostEstimate(flops=0, bytes_accessed=0, transcendentals=0),
    )(*[v for v, _ in ins])


class Ring:
    def __init__(self, at, name, own):
        self.at, self.name = at, name
        at[name] = {0: own}

    def up(self):
        parts = self.at[self.name]
        parts[1] = pass_on(parts[0])

    def down(self):
        parts = self.at[self.name]
        parts[3] = pass_on(parts[0], -1)

    def far(self):
        parts = self.at[self.name]
        parts[2] = pass_on(parts[1])

    def direct(self):
        parts = self.at[self.name]
        for way in (1, 2, 3):
            parts[way] = pass_on(parts[0], way)

    def take(self):
        parts = self.at.pop(self.name)
        return [parts[i] for i in range(4)]


class Widen:
    def __init__(self, at, name, first, second):
        self.at, self.name = at, name
        at[name] = {"own": (first, second)}

    def one(self):
        held = self.at[self.name]
        first, second = held.pop("own")
        held["both"] = (first, swap(first, 2), second, swap(second, 4))

    def two(self):
        held = self.at[self.name]
        both = held.pop("both")
        near = jnp.stack(both[:2]), jnp.stack(both[2:])
        held["near"] = near
        held["far"] = swap(near[0], 4), swap(near[1], 2)

    def direct(self):
        held = self.at[self.name]
        own = held.pop("own")
        held["lines"] = [jnp.stack(own)] + [swap(jnp.stack(own), bit) for bit in (2, 4, 6)]

    def two_early(self):
        self.two()
        held = self.at[self.name]
        held["near all"] = jnp.stack(held.pop("near"))
        held["near core"] = swap(held["near all"], 1)

    def core_late(self):
        held = self.at[self.name]
        held["far all"] = jnp.stack(held.pop("far"))
        held["far core"] = swap(held["far all"], 1)

    def core_direct(self):
        held = self.at[self.name]
        lines = held.pop("lines")
        order = [[distance // 2 for distance in half] for half in DISTANCES]
        held["all"] = jnp.stack([jnp.stack([lines[i][half] for i in order[half]]) for half in range(2)])
        held["core"] = swap(held["all"], 1)

    def core(self):
        held = self.at[self.name]
        near, far = held.pop("near"), held.pop("far")
        held["all"] = jnp.stack([jnp.concatenate([near[half], far[half]]) for half in range(2)])
        held["core"] = swap(held["all"], 1)

    def take(self):
        held = self.at.pop(self.name)
        if "all" in held:
            return held["all"], held["core"]
        return held["near all"], held["far all"], held["near core"], held["far core"]


class Reduce:
    def __init__(self, at, name, keep, send):
        self.at, self.name = at, name
        at[name] = {"keep": keep, "send": send}

    def core(self):
        held = self.at[self.name]
        held["core"] = swap(held.pop("send"), 1)

    def one(self):
        held = self.at[self.name]
        keep, core = held["keep"], held["core"]
        held["one"] = swap(added(keep[0, 2:], core[0, 2:]), 4), swap(added(keep[1, 2:], core[1, 2:]), 2)

    def two(self):
        held = self.at[self.name]
        keep, core, one = held["keep"], held["core"], held["one"]
        held["two"] = (
            swap(added(keep[0, 1], core[0, 1], one[0][1]), 2),
            swap(added(keep[1, 1], core[1, 1], one[1][1]), 4),
        )

    def combine(self):
        held = self.at[self.name]
        arrays = [held[name] for name in ("keep", "core")] + list(held["one"]) + list(held["two"])
        rows, width = arrays[0].shape[3:]
        mp = arrays[0].shape[2]
        outs = [shape((2, rows, width), kind) for kind in (F32, BF16, BF16, F32)]
        parts = call(
            combine_kernel,
            [(v, ANY) for v in arrays],
            [(v, VMEM) for v in outs],
            [pltpu.VMEM((2, mp, rows, width), BF16)] * 4 + [pltpu.SemaphoreType.DMA((4,))],
            megabytes=12,
        )
        self.at[self.name] = {"own": parts[0], "parts": parts[1:]}

    def join(self, other):
        theirs = self.at.pop(other.name)
        held = self.at[self.name]
        held["own"] = jnp.concatenate([held["own"], theirs["own"]], axis=1)
        held["parts"] = [jnp.concatenate(pair, axis=1) for pair in zip(held["parts"], theirs["parts"])]

    def far(self):
        held = self.at[self.name]
        held["far"] = pass_on(held["parts"][1])

    def near(self):
        held = self.at[self.name]
        down, _, up = held.pop("parts")
        held["up"] = pass_on(added(up, held.pop("far")))
        held["down"] = pass_on(down, -1)

    def direct(self):
        held = self.at[self.name]
        down, across, up = held.pop("parts")
        held["up"], held["across"], held["down"] = pass_on(added(up)), pass_on(across, 2), pass_on(down, -1)

    def owned(self):
        held = self.at.pop(self.name)
        own = added(held["own"], *[held[name] for name in ("up", "across", "down") if name in held])
        bit = SLICES
        while bit < lax.axis_size("dp"):
            own = added(own, swap(own, bit))
            bit *= 2
        return own


def on_device(
    tokens, images, segment_of_token, image_of_row, attention_in, query_value_bias, attention_out, output_bias,
    feed_in, feed_bias, feed_out, image_weight, image_bias, norm_gain, norm_bias, cotangent,
):
    mp = lax.axis_size("mp")
    slot = lax.axis_index("dp") % SLICES
    owner = lax.axis_index("mp")
    place = jnp.stack([slot, owner]).astype(jnp.int32)
    own_rows, seq, width = tokens.shape
    group_rows = segment_of_token.shape[0]
    patches, image_width = images.shape[1:]
    quarter = attention_in.shape[3]
    units = feed_in.shape[2]
    n_tokens = own_rows * seq
    inward = attention_in.transpose(0, 1, 3, 2)
    image = image_weight.T

    attention_rows = quarter // 4
    feed_rows = units // SLICES
    image_rows = quarter * image_width // width // SLICES // 2

    token_shape = shape((n_tokens, width))
    token_low = shape((n_tokens, width), BF16)
    row_low = shape((own_rows, seq, width), BF16)
    inner_shape = shape((mp, n_tokens, units))
    inner_low = shape((mp, n_tokens, units), BF16)
    padded = -(-patches // 16) * 16
    n_patches = own_rows * padded
    patch_low = shape((n_patches, width), BF16)
    small_shape = shape((8, width))
    attention_grad = shape((2, 4, mp, attention_rows, width), BF16)
    feed_grad = shape((2, 4, mp, feed_rows, width), BF16)
    image_grad = shape((2, 4, mp, image_rows, width), BF16)
    kept_square = shape((4, width, width), BF16)
    kept_wide = shape((2, mp, units, width), BF16)
    kept_tall = shape((width, image_width), BF16)
    square = pltpu.VMEM((4, width, width), BF16)
    wide = pltpu.VMEM((2, mp, units, width), BF16)
    tall = pltpu.VMEM((width, image_width), BF16)
    token_f32 = pltpu.VMEM((n_tokens, width), F32)
    token_bf16 = pltpu.VMEM((n_tokens, width), BF16)
    row_bf16 = pltpu.VMEM((own_rows, seq, width), BF16)
    inner_f32 = pltpu.VMEM((mp, n_tokens, units), F32)
    inner_bf16 = pltpu.VMEM((mp, n_tokens, units), BF16)
    dma = pltpu.SemaphoreType.DMA
    matmul = 2 * n_tokens * width * width
    patch_matmul = 2 * n_patches * width * width

    local_order = image_of_row % group_rows
    here = owner * own_rows + jnp.arange(own_rows, dtype=jnp.int32)
    chosen = (local_order[None, :] == here[:, None]).astype(jnp.int32)
    source_row = jnp.sum(chosen * jnp.arange(group_rows, dtype=jnp.int32)[None, :], axis=1)
    picks_in = ((owner - source_row // own_rows) % mp) * own_rows + source_row % own_rows
    mine = (jnp.arange(group_rows, dtype=jnp.int32)[None, :] == here[:, None]).astype(jnp.int32)
    image_row = jnp.sum(mine * local_order[None, :], axis=1)
    picks_out = ((owner - image_row // own_rows) % mp) * own_rows + image_row % own_rows
    segments = jnp.sum(chosen[:, :, None] * segment_of_token[None], axis=1)
    code = jnp.arange(own_rows, dtype=jnp.int32)[:, None] * seq + segments
    code_col = code.reshape(n_tokens, 1)
    code_row = code.reshape(own_rows // 2, 2 * seq)

    first_rows = 2 * attention_rows + image_rows
    first, second, third = call(
        slice_kernel,
        [(place, SMEM)]
        + [(v, VMEM) for v in (query_value_bias, feed_bias, image_bias.reshape(1, quarter))]
        + [(v, ANY) for v in (inward, attention_out, feed_in, feed_out, image)],
        [
            (shape((2, rows, width), BF16), VMEM)
            for rows in (first_rows + 16, feed_rows + attention_rows, feed_rows)
        ],
        [dma((3,))],
    )

    at = {}

    def step():
        done = lax.optimization_barrier(at)
        at.clear()
        at.update(done)

    rings = {
        name: Ring(at, name, own)
        for name, own in (
            ("first", first), ("second", second), ("third", third), (TOKENS, tokens), (COTANGENT, cotangent),
        )
    }

    def gathered(name, rows=None):
        parts = rings[name].take()[1:]
        return Widen(at, name, *[jnp.stack([part[half, :rows] for part in parts]) for half in range(2)])

    rings["first"].direct()
    step()

    parts = [part[0, first_rows:] for part in at["first"].values()]
    ordered = jnp.stack(parts)[(owner - jnp.arange(mp)) % mp].astype(F32)
    bias = jnp.concatenate(
        [
            ordered[:, :6, :quarter].transpose(1, 0, 2).reshape(6, width),
            ordered[:, 6:8].transpose(1, 0, 2).reshape(2 * mp, width),
            ordered[:, 8, :quarter].reshape(1, width),
        ]
    )
    params = jnp.stack([output_bias, norm_gain, norm_bias], axis=1).astype(F32).reshape(-1, width)
    patch_rows = jnp.pad(images, ((0, 0), (0, padded - patches), (0, 0))).reshape(n_patches, image_width)
    at["tables"] = bias, params, code_col, code_row, picks_in, picks_out, image_row, patch_rows
    first_wide = gathered("first", first_rows)
    first_wide.one()
    rings["second"].up()
    rings["second"].down()
    step()
    bias, params, code_col, code_row, picks_in, picks_out, image_row, patch_rows = at.pop("tables")
    first_wide.two()
    rings["second"].far()
    rings[TOKENS].up()
    rings["third"].up()
    step()
    second_wide = gathered("second")
    first_wide.core()
    second_wide.one()
    rings[TOKENS].down()
    rings["third"].down()
    step()

    attention_pieces = [None, None, None]
    attention_at = [0, feed_rows, attention_rows]
    feed_pieces = [None, None]
    feed_at = [0, 0]

    def attention_ins(layer):
        return [(inward, ANY), (attention_out, ANY)] + [(piece, ANY) for piece in attention_pieces[layer]]

    def feed_ins(layer):
        return [(feed_in, ANY), (feed_out, ANY)] + [(piece, ANY) for piece in feed_pieces[layer]]

    def first_forward(layer, norm, parts):
        picked = len(parts) > 1
        return call(
            partial(self_forward_kernel, layer, norm, attention_at[layer], len(parts), len(attention_pieces[layer])),
            [(place, SMEM), (picks_in, SMEM)]
            + [(part, ANY if picked else VMEM) for part in parts]
            + attention_ins(layer)
            + [(bias, VMEM), (params, VMEM), (code_col, VMEM), (code_row, VMEM)],
            [(token_shape, VMEM), (token_low, VMEM), (token_shape, VMEM)] + [(token_low, VMEM)] * 4 + [(kept_square, ANY)],
            [square, dma((4,)), dma] + ([row_bf16, token_f32, dma] if picked else []),
        )

    def self_backward(norm, grad, kept, leave, spot, rows, held):
        _, low, pre, query, keys, value, context, weights = kept
        grads = shape((2, 4, mp, rows, width), BF16)
        ins = [(place, SMEM)] + [(v, VMEM) for v in (grad, low, pre, query, keys, value, context)]
        ins += [(weights, ANY), (params, VMEM), (code_col, VMEM), (code_row, VMEM)]
        return call(
            partial(self_backward_kernel, leave, norm, spot, len(held)),
            ins + [(v, ANY) for v in held],
            [(row_low if leave else token_shape, VMEM), (small_shape, VMEM)] + [(grads, ANY)] * 2,
            [square, square] + [token_bf16] * 4 + [dma((4,)), dma],
            {len(ins) + i: 2 + i for i in range(len(held))},
        )

    def feed_self_forward(layer, norm, next_layer, next_norm, rows):
        pieces, following = feed_pieces[layer], attention_pieces[next_layer]
        outs = call(
            partial(
                feed_self_forward_kernel, layer, norm, feed_at[layer], next_layer, next_norm, attention_at[next_layer],
                len(pieces), len(following),
            ),
            [(place, SMEM), (rows, VMEM)]
            + [(v, ANY) for v in (feed_in, feed_out, inward, attention_out, *pieces, *following)]
            + [(bias, VMEM), (params, VMEM), (code_col, VMEM), (code_row, VMEM)],
            [(token_shape, VMEM), (token_low, VMEM), (token_shape, VMEM)]
            + [(inner_shape, ANY), (inner_low, ANY), (kept_wide, ANY)]
            + [(token_shape, VMEM), (token_low, VMEM), (token_shape, VMEM)]
            + [(token_low, VMEM)] * 4
            + [(kept_square, ANY)],
            [wide, inner_f32, inner_bf16, dma((2, mp)), dma, square, dma((4,)), dma],
        )
        return outs[:6], outs[6:]

    def feed_backward(norm, grad, kept):
        _, low, pre, slope, active, weights = kept
        return call(
            partial(feed_backward_kernel, norm),
            [(place, SMEM)] + [(v, ANY) for v in (grad, low, pre, slope, active, weights)] + [(params, VMEM)],
            [(token_shape, VMEM), (small_shape, VMEM)] + [(feed_grad, ANY)] * 2,
            [wide, wide, token_f32, token_bf16, token_f32, inner_f32, inner_bf16]
            + [dma((3 + 2 * mp,)), dma((2, mp)), dma],
        )

    def feed_both(layer, norm, rows, parts):
        return call(
            partial(feed_both_kernel, layer, norm, feed_at[layer], len(parts), len(feed_pieces[layer])),
            [(place, SMEM), (picks_in, SMEM), (rows, VMEM), (feed_in, ANY), (feed_out, ANY)]
            + [(v, ANY) for v in parts + list(feed_pieces[layer])]
            + [(bias, VMEM), (params, VMEM)],
            [(row_low, VMEM), (token_shape, VMEM), (small_shape, VMEM)] + [(feed_grad, ANY)] * 2,
            [wide, wide, inner_f32, inner_bf16, token_bf16, token_f32, token_f32, row_bf16]
            + [dma((2, mp)), dma, dma],
        )

    def pick_rows(parts):
        return call(
            pick_kernel,
            [(picks_out, SMEM)] + [(part, ANY) for part in parts],
            [(shape((own_rows, seq, width)), VMEM)],
            [row_bf16, dma],
        )[0]

    attention_pieces[0] = attention_pieces[2] = first_wide.take()
    second_wide.two_early()
    rings[TOKENS].far()
    rings["third"].far()
    projected, image_keys, image_value, kept_image = call(
        partial(image_forward_kernel, 2, attention_rows, 2 * attention_rows, image_rows, len(attention_pieces[2])),
        [(place, SMEM), (patch_rows, VMEM), (image, ANY)] + attention_ins(2) + [(bias, VMEM)],
        [(patch_low, VMEM)] * 3 + [(kept_tall, ANY)],
        [square, tall, dma((4,)), dma, dma],
    )
    at["keys"] = image_keys
    step()

    text_attention = first_forward(0, 0, rings[TOKENS].take())
    at["stream"] = text_attention[0]
    second_wide.core_late()
    third_wide = gathered("third")
    third_wide.one()
    rings[COTANGENT].up()
    step()

    attention_pieces[1] = feed_pieces[0] = second_wide.take()
    third_wide.two()
    rings[COTANGENT].down()
    text_feed, joining_attention = feed_self_forward(0, 1, 1, 2, at.pop("stream"))
    at["stream"] = joining_attention[0]
    step()

    third_wide.core()
    rings[COTANGENT].far()
    image_keys = at.pop("keys")
    cross_attention = call(
        partial(cross_forward_kernel, 2, 3, attention_rows, seq, patches, len(attention_pieces[2])),
        [(place, SMEM), (at.pop("stream"), VMEM), (image_keys, VMEM), (image_value, VMEM)]
        + attention_ins(2)
        + [(bias, VMEM), (params, VMEM)],
        [(token_shape, VMEM), (token_low, VMEM), (token_shape, VMEM), (token_shape, VMEM), (token_low, VMEM)]
        + [(kept_square, ANY)],
        [square, token_f32, dma((4,)), dma],
    )
    at["stream"] = cross_attention[0]
    step()

    feed_pieces[1] = third_wide.take()

    mixed, grad, small_joining_feed, keep, send = feed_both(1, 4, at.pop("stream"), rings[COTANGENT].take())
    mixed_ring = Ring(at, "mixed", mixed)
    at["grad"] = grad
    last_grads = Reduce(at, "last", keep, send)
    step()

    last_grads.core()
    mixed_ring.up()
    grad, small_cross, grad_keys, grad_value, cross_branch, cross_query = call(
        partial(cross_backward_kernel, 3, seq, patches),
        [(place, SMEM), (at.pop("grad"), VMEM)]
        + [(cross_attention[i], VMEM) for i in (1, 2, 3, 4)]
        + [(image_keys, VMEM), (image_value, VMEM), (cross_attention[5], ANY), (params, VMEM)],
        [(token_shape, VMEM), (small_shape, VMEM)] + [(patch_low, VMEM)] * 2 + [(token_low, VMEM)] * 2,
        [square, token_f32, token_f32, dma((4,))],
    )
    at["grad"] = grad
    step()

    last_grads.one()
    mixed_ring.down()
    middle_rows = 2 * attention_rows
    grad, small_joining, keep, send = self_backward(
        2, at.pop("grad"), joining_attention, False, attention_rows, middle_rows, ()
    )
    at["grad"] = grad
    cross_grads = (cross_attention[4], cross_branch, cross_query, cross_attention[1], grad_keys, grad_value, projected)
    keep, send = call(
        partial(cross_weights_kernel, 0),
        [(place, SMEM)] + [(v, VMEM) for v in cross_grads] + [(keep, ANY), (send, ANY)],
        [(shape(keep.shape, BF16), ANY)] * 2,
        [square, dma],
        {8: 0, 9: 1},
    )
    middle_grads = Reduce(at, "middle", keep, send)
    at["patch grads"] = grad_keys, grad_value
    step()

    last_grads.two()
    middle_grads.core()
    mixed_ring.far()
    grad, small_text_feed, keep, send = feed_backward(1, at.pop("grad"), text_feed)
    at["grad"] = grad
    first_grads = Reduce(at, "first", keep, send)
    step()

    mixed_parts = mixed_ring.take()
    middle_grads.one()
    first_grads.core()
    last_grads.combine()
    held = at["last"]
    down, across, up = held.pop("parts")
    held["up"], held["down"] = pass_on(up.astype(BF16)), pass_on(down, -1)
    held["across part"] = across
    rows_back, small_text, keep, send = self_backward(
        0, at.pop("grad"), text_attention, True, 0, attention_rows + image_rows, ()
    )
    back_ring = Ring(at, "back", rows_back)
    at["text"] = keep, send
    step()

    middle_grads.two()
    first_grads.one()
    at["last"]["across"] = pass_on(at["last"].pop("across part"), 2)
    grad_keys, grad_value = at.pop("patch grads")
    keep, send = at.pop("text")
    grad_images, small_image, keep, send = call(
        partial(image_backward_kernel, image_rows, attention_rows, 2),
        [(place, SMEM), (patch_rows, VMEM), (grad_keys, VMEM), (grad_value, VMEM), (cross_attention[5], ANY)]
        + [(kept_image, ANY), (keep, ANY), (send, ANY)],
        [(shape((patches, own_rows, image_width)), VMEM), (small_shape, VMEM)] + [(shape(keep.shape, BF16), ANY)] * 2,
        [square, tall, tall, pltpu.VMEM((n_patches, width), BF16), dma((4,)), dma, dma],
        {6: 2, 7: 3},
    )
    text_grads = Reduce(at, "text", keep, send)
    at[SMALL] = jnp.concatenate(
        [small_text, small_text_feed, small_joining, small_cross, small_joining_feed, small_image]
    )
    step()

    first_grads.two()
    text_grads.core()
    middle_grads.combine()
    middle_grads.far()
    back_ring.up()
    step()

    text_grads.one()
    middle_grads.near()
    first_grads.combine()
    first_grads.far()
    at[SMALL] = at[SMALL] + swap(at[SMALL], 1)
    at["last own"] = last_grads.owned()
    step()

    early = Widen(at, "early", *jnp.concatenate([at.pop("last own"), middle_grads.owned()], axis=1))
    early.one()
    text_grads.two()
    first_grads.near()
    back_ring.down()
    at[SMALL] = at[SMALL] + swap(at[SMALL], 2)
    step()

    early.two()
    text_grads.combine()
    text_grads.direct()
    at["first own"] = first_grads.owned()
    at[SMALL] = at[SMALL] + swap(at[SMALL], 4)
    step()

    late = Widen(at, "late", *jnp.concatenate([at.pop("first own"), text_grads.owned()], axis=1))
    late.one()
    at["mixed"] = pick_rows(mixed_parts)
    early.core()
    back_ring.far()
    at[SMALL] = at[SMALL] + swap_owner(at[SMALL], 1)
    step()

    late.two()
    at[TOKENS] = pick_rows(back_ring.take())
    early_pieces = early.take()
    smalls = at.pop(SMALL)
    smalls = smalls + swap_owner(smalls, 2)
    bit = SLICES
    while bit < lax.axis_size("dp"):
        smalls = smalls + swap(smalls, bit)
        bit *= 2
    at[SMALL] = smalls

    whole_shapes = {
        ATTENTION_IN: shape(inward.shape),
        ATTENTION_OUT: shape(attention_out.shape),
        FEED_IN: shape(feed_in.shape),
        FEED_OUT: shape(feed_out.shape),
        IMAGE: shape(image.shape),
    }
    block_of = {ATTENTION: (4, quarter, width), FEED: (2, units, width), IMAGE: (quarter, image_width)}
    names_of = {ATTENTION: [ATTENTION_IN, ATTENTION_OUT], FEED: [FEED_IN, FEED_OUT], IMAGE: [IMAGE]}
    written = {}

    def write_out(result, *blocks):
        names = list(dict.fromkeys(name for kind, _, _ in blocks for name in names_of[kind]))
        names = [name for name in names if name in written] + [name for name in names if name not in written]
        held = [name for name in names if name in written]
        scratch = [pltpu.VMEM(block_of[kind], form) for kind, _, _ in blocks for form in (BF16, F32)]
        results = call(
            partial(finish_kernel, blocks, quarter, names, len(held), len(result)),
            [(place, SMEM)] + [(v, ANY) for v in result] + [(written[name], ANY) for name in held],
            [(whole_shapes[name], ANY) for name in names],
            scratch + [dma((len(blocks),)), dma((len(blocks),))],
            {1 + len(result) + i: i for i in range(len(held))},
        )
        written.update(zip(names, results))

    write_out(
        early_pieces, (FEED, 0, 1), (ATTENTION, feed_rows, 2), (ATTENTION, feed_rows + attention_rows, 1)
    )
    at["written"] = written
    step()
    written = at.pop("written")
    late.core()
    smalls = at.pop(SMALL).reshape(6, 8, width)

    def own_part(values):
        return lax.dynamic_slice_in_dim(values, owner * quarter, quarter, axis=values.ndim - 1)

    grad_query_value_bias = own_part(jnp.stack([smalls[i, 3:5] for i in (0, 2, 3)]))
    grad_feed_bias = jnp.stack([smalls[i, 3 : 3 + mp].reshape(-1) for i in (1, 4)])
    grad_feed_bias = lax.dynamic_slice_in_dim(grad_feed_bias, owner * units, units, axis=1)
    vectors = (
        grad_query_value_bias, smalls[:5, 2], grad_feed_bias, own_part(smalls[5, 0]), smalls[:5, 0], smalls[:5, 1]
    )
    at["vectors"] = vectors
    step()
    vectors = at.pop("vectors")
    write_out(
        late.take(), (FEED, 0, 0), (ATTENTION, feed_rows, 0), (IMAGE, feed_rows + attention_rows, 0)
    )
    return (
        at["mixed"],
        at[TOKENS],
        grad_images.transpose(1, 0, 2),
        written[ATTENTION_IN].transpose(0, 1, 3, 2),
        vectors[0],
        written[ATTENTION_OUT],
        vectors[1],
        written[FEED_IN],
        vectors[2],
        written[FEED_OUT],
        written[IMAGE].T,
        vectors[3],
        vectors[4],
        vectors[5],
    )


def solution(mesh):
    rows = P(("dp", "mp"), None, None)
    return jax.shard_map(
        on_device,
        mesh=mesh,
        in_specs=(
            rows,
            rows,
            P("dp", None),
            P("dp"),
            P(None, None, None, "mp"),
            P(None, None, "mp"),
            P(None, "mp", None),
            P(),
            P(None, None, "mp"),
            P(None, "mp"),
            P(None, "mp", None),
            P(None, "mp"),
            P("mp"),
            P(),
            P(),
            rows,
        ),
        out_specs=(
            rows,
            rows,
            rows,
            P(None, None, None, "mp"),
            P(None, None, "mp"),
            P(None, "mp", None),
            P(),
            P(None, None, "mp"),
            P(None, "mp"),
            P(None, "mp", None),
            P(None, "mp"),
            P("mp"),
            P(),
            P(),
        ),
        check_vma=False,
    )
```
